128 devices in a mesh: dp: 8 (over y, core), expert: 16 (over z, x).
Axes of the slice: x: 4, y: 4, z: 4, core: 2. Of those that a mesh axis runs over, the one named last changes fastest.
Arguments:
- hidden: bfloat16 [2, 2048, 2048], P(None, ('dp', 'expert')), may hold values from -6 to 6
- q_self: bfloat16 [2, 2048, 2048], P(None, ('dp', 'expert')), may hold values from -60 to 60
- k_new: bfloat16 [2, 2048, 2048], P(None, ('dp', 'expert')), may hold values from -6 to 6
- v_new: bfloat16 [2, 2048, 2048], P(None, ('dp', 'expert')), may hold values from -6 to 6
- q_cross: bfloat16 [2, 2048, 2048], P(None, ('dp', 'expert')), may hold values from -40 to 40
- cache_keys: bfloat16 [2048, 64, 2048], P(('dp', 'expert')), may hold values from -6 to 6
- cache_values: bfloat16 [2048, 64, 2048], P(('dp', 'expert')), may hold values from -6 to 6
- cross_keys: bfloat16 [512, 256, 2048], P(('dp', 'expert')), may hold values from -127 to 127, as said below
- cross_values: bfloat16 [512, 256, 2048], P(('dp', 'expert')), may hold values from -127 to 127, as said below
- key_scale: float32 [512, 16], P(('dp', 'expert')), may hold values from 0.01 to 0.02
- value_scale: float32 [512, 16], P(('dp', 'expert')), may hold values from 0.005 to 0.03
- parents: int32 [2, 2048], P(None, ('dp', 'expert')), may hold values from 0 to 2047, as said below
- expert_ids: int32 [2, 2048, 2], P(None, ('dp', 'expert')), may hold values from 0 to 15, all different within a row; in each aligned block of 16 rows (0 to 15, 16 to 31, ..., all dimensions but the last counted through in order) at most 4 rows name the same one
- norm_gain: float32 [2048], replicated, may hold values from 0.1 to 1.9
- router: bfloat16 [2048, 16], replicated, may hold values from -0.125 to 0.125
- w_in: bfloat16 [16, 2048, 8192], P('expert', None, 'dp'), may hold values from -0.125 to 0.125
- w_out: bfloat16 [16, 8192, 2048], P('expert', 'dp'), may hold values from -0.0625 to 0.0625
Outputs:
- mixed: bfloat16 [2, 2048, 2048], P(None, ('dp', 'expert'))
The draws below stay inside these ranges and needn't reach their ends.
Inputs may be any that keep to these rules, and one draw needn't show every extreme that they name: `parents`: in each step, on the rows of each device exactly 4 beams take a parent among the rows of the previous device along dp+expert (the last device for the first); every other beam takes a beam of its own sentence. `expert_ids`: in each step, no expert is named by more than 4 of the rows of one device. `cross_keys`: whole numbers. `cross_values`: whole numbers.
All inputs are finite; a program needn't handle non-finite values.
Results may differ from the reference program's by a relative error of at most 0.012.
Values may be sent and summed in bfloat16 or wider, within the bound.
A program may use at most 192 MiB of HBM per device.

```python
import math
import jax
import jax.numpy as jnp
import numpy as np
from jax import lax

D = 2048
HEADS = 16
HEAD_DIM = 128
FF = 8192
EXPERTS = 16
TOP = 2
BEAMS = 4
SENT_DEV = 4
ROWS_DEV = 16
SENTS = 512
TOKENS = 2048
SRC = 256
CACHE = 64
STEPS = 2
CAP = 4
N_DP = 8


def draw_q_self(key, part):
    key = jax.random.fold_in(key, 11)
    values = jax.random.truncated_normal(key, -6.0, 6.0, (STEPS, TOKENS, D), jnp.float32)
    return values.astype(jnp.bfloat16)


def draw_cache_keys(key, part):
    key = jax.random.fold_in(key, 12)
    values = jax.random.truncated_normal(key, -6.0, 6.0, (TOKENS, CACHE, D), jnp.float32)
    return values.astype(jnp.bfloat16)


def draw_q_cross(key, part):
    key = jax.random.fold_in(key, 13)
    values = jax.random.truncated_normal(key, -6.0, 6.0, (STEPS, TOKENS, D), jnp.float32)
    return values.astype(jnp.bfloat16)


def draw_cross_keys(key, part):
    key = jax.random.fold_in(key, 14)
    values = jax.random.randint(key, (SENTS, SRC, D), -127, 128).astype(jnp.float32)
    return values.astype(jnp.bfloat16)


def draw_cross_values(key, part):
    key = jax.random.fold_in(key, 15)
    return jax.random.randint(key, (SENTS, SRC, D), -127, 128).astype(jnp.float32).astype(jnp.bfloat16)


def draw_parents(key, part):
    key = jax.random.fold_in(key, 16)
    key_order, key_own, key_far = jax.random.split(key, 3)
    blocks = TOKENS // ROWS_DEV
    spare = max(1, ROWS_DEV // 4)
    local_rows = jnp.arange(ROWS_DEV, dtype=jnp.int32)[None, None, :]
    block_ids = jnp.arange(blocks, dtype=jnp.int32)[None, :, None]
    scores = jax.random.randint(key_order, (STEPS, blocks, ROWS_DEV), 0, 1 << 20) * ROWS_DEV + local_rows
    ranks = jnp.argsort(jnp.argsort(scores, axis=2), axis=2)
    remote = ranks < spare
    own_parent = block_ids * ROWS_DEV + local_rows // BEAMS * BEAMS + jax.random.randint(key_own, (STEPS, blocks, ROWS_DEV), 0, BEAMS)
    far_parent = (block_ids + blocks - 1) % blocks * ROWS_DEV + jax.random.randint(key_far, (STEPS, blocks, ROWS_DEV), 0, ROWS_DEV)
    return jnp.where(remote, far_parent, own_parent).reshape(STEPS, TOKENS).astype(jnp.int32)


def level_of(own_key, shape, cuts, low, top_value):
    def one(axis_at, blocks):
        heights = jax.random.uniform(jax.random.fold_in(jax.random.fold_in(own_key, 6), axis_at), (blocks,), jnp.float32, low / len(cuts), top_value / len(cuts))
        return jnp.repeat(jnp.exp(heights), shape[axis_at] // blocks).reshape((-1,) + (1,) * (len(shape) - axis_at - 1))

    level = one(*cuts[0])
    for cut in cuts[1:]:
        level = level * one(*cut)
    return level


def routed_block(rng, own, number, rows, amount, top, limit, skew):
    order = jax.random.permutation(rng, amount)
    heavy_load, ordinary = portions_of(amount, rows * top, limit, skew, True), portions_of(amount, rows * top, limit, skew, False)
    places = jnp.arange(amount)

    def named(lengths, turn):
        used = int((lengths > 0).sum())
        fixed = max(1, used // 4)
        moved = fixed + (places - fixed + turn * (used - fixed)) % max(1, amount - fixed)
        return jnp.zeros((amount,), jnp.int32).at[order[jnp.where(places < fixed, places, moved)]].set(jnp.asarray(lengths, jnp.int32))

    lengths = jnp.where(number % 4 == 0, named(heavy_load, number // 4), named(ordinary, number - number // 4 - 1))
    mixed = jax.random.permutation(jax.random.fold_in(own, 3), amount)
    source_of, receiver = mixed[0:amount // 2 * 2:2], mixed[1:amount // 2 * 2:2]
    room = jnp.minimum(lengths[source_of] - 1, limit - lengths[receiver]) // 2
    room = jnp.where((source_of == order[0]) | (receiver == order[0]) | (lengths[receiver] == 0), 0, jnp.maximum(room, 0))
    moved = jax.random.randint(jax.random.fold_in(own, 4), (amount // 2,), 0, 1 << 20) % (room + 1)
    lengths = lengths.at[source_of].add(-moved).at[receiver].add(moved)
    items = jnp.searchsorted(jnp.cumsum(lengths), jnp.arange(rows * top), side="right").astype(jnp.int32)
    table = items.reshape(top, rows).T
    table = table[jax.random.permutation(jax.random.fold_in(own, 1), rows)]
    turn = jax.random.randint(jax.random.fold_in(own, 2), (rows, 1), 0, top)
    return jnp.take_along_axis(table, (jnp.arange(top)[None, :] + turn) % top, axis=1)


def portions_of(count, total, limit, lean, full):
    loads = [(1 << 20) // math.isqrt(standing ** lean) + 1 for standing in range(1, count + 1)]
    largest = limit if full else min(limit, max(-(-total // count), total * loads[0] // sum(loads)))
    least = 1 if total - largest >= count - 1 else 0
    counts, spare = [largest] + [least] * (count - 1), total - largest - least * (count - 1)
    while spare > 0:
        candidates = [i for i in range(1, count) if counts[i] < largest] or [i for i in range(1, count) if counts[i] < limit]
        pool, left = sum([loads[i] for i in candidates]), spare
        for i in candidates:
            addition = min(limit - counts[i], max(1, left * loads[i] // pool), spare)
            counts[i] = counts[i] + addition
            spare = spare - addition
    return np.array(counts)


def bell_draw(key, extent, deviation, limit, cuts=(), kind=jnp.bfloat16):
    loudness = level_of(key, extent, cuts, -0.22, 0.18) if cuts else 1.0
    drawn = jax.random.normal(key, extent, jnp.float32) * deviation * loudness
    return jnp.minimum(jnp.maximum(drawn, -limit), limit).astype(kind)


def setup_inputs(seed: int = 0) -> dict:
    streams_of = jax.random.split(jax.random.key(seed), 18)
    hidden = bell_draw(streams_of[0], (STEPS, TOKENS, D), 1.0, 6.0, ((1, 128),))
    q_self = draw_q_self(jax.random.fold_in(streams_of[17], 71), 0)
    k_new = bell_draw(streams_of[2], (STEPS, TOKENS, D), 1.0, 6.0, ((1, 128),))
    v_new = bell_draw(streams_of[3], (STEPS, TOKENS, D), 1.0, 6.0, ((1, 128),))
    q_cross = draw_q_cross(jax.random.fold_in(streams_of[17], 71), 0)
    cache_keys = draw_cache_keys(jax.random.fold_in(streams_of[17], 71), 0)
    cache_values = bell_draw(streams_of[6], (TOKENS, CACHE, D), 1.0, 6.0, ((0, 128),))
    cross_keys = draw_cross_keys(jax.random.fold_in(streams_of[17], 71), 0)
    cross_values = draw_cross_values(jax.random.fold_in(streams_of[17], 71), 0)
    key_scale = jnp.clip(jnp.exp(math.log(0.02) - 0.6931472 * jax.random.uniform(streams_of[9], (SENTS, HEADS), jnp.float32) ** level_of(streams_of[9], (SENTS, HEADS), ((0, 128),), -0.2, 0.2)), 0.01, 0.02)
    value_scale = jnp.clip(jnp.exp(math.log(0.03) - 1.7917595 * jax.random.uniform(streams_of[10], (SENTS, HEADS), jnp.float32) ** level_of(streams_of[10], (SENTS, HEADS), ((0, 128),), -0.2, 0.2)), 0.005, 0.03)
    parents = draw_parents(jax.random.fold_in(streams_of[17], 71), 0)
    expert_ids_keys = jax.random.split(jax.random.fold_in(streams_of[12], 1), STEPS * TOKENS // ROWS_DEV)
    expert_ids_turns = jax.random.permutation(jax.random.fold_in(streams_of[12], 3), STEPS * TOKENS // ROWS_DEV)
    expert_ids = jax.vmap(lambda own, number: routed_block(jax.random.fold_in(streams_of[12], 2), own, number, ROWS_DEV, EXPERTS, TOP, CAP, 2))(expert_ids_keys, expert_ids_turns).reshape((STEPS, TOKENS, TOP))
    norm_gain = jnp.clip(1.0 + 0.18 * jax.random.normal(streams_of[13], (D,), jnp.float32), 0.1, 1.9)
    router = bell_draw(streams_of[14], (D, EXPERTS), D ** -0.5, 0.125)
    w_in = bell_draw(streams_of[15], (EXPERTS, D, FF), D ** -0.5, 0.125, ((0, 16), (2, 8)))
    w_out = bell_draw(streams_of[16], (EXPERTS, FF, D), FF ** -0.5, 0.0625, ((0, 16), (1, 8)))
    return {"hidden": hidden, "q_self": q_self, "k_new": k_new, "v_new": v_new, "q_cross": q_cross, "cache_keys": cache_keys, "cache_values": cache_values, "cross_keys": cross_keys, "cross_values": cross_values, "key_scale": key_scale, "value_scale": value_scale, "parents": parents, "expert_ids": expert_ids, "norm_gain": norm_gain, "router": router, "w_in": w_in, "w_out": w_out}


epsilon = 1e-05

def soft_weights(scores):
    top_score = lax.optimization_barrier(jnp.max(scores, axis=-1, keepdims=True))
    weights = jnp.exp(scores - top_score)
    prob_bf = (weights / lax.optimization_barrier(jnp.sum(weights, axis=-1, keepdims=True))).astype(jnp.bfloat16)
    return lax.optimization_barrier(prob_bf).astype(jnp.float32)

def self_block(entry):
    query, key_rows, value_rows = entry
    length = key_rows.shape[1]
    query = query.reshape(ROWS_DEV, HEADS, HEAD_DIM).astype(jnp.float32)
    key_rows = key_rows.reshape(ROWS_DEV, length, HEADS, HEAD_DIM).astype(jnp.float32)
    value_rows = value_rows.reshape(ROWS_DEV, length, HEADS, HEAD_DIM).astype(jnp.float32)
    scores = jnp.einsum('rhe,rlhe->rhl', query, key_rows) / math.sqrt(HEAD_DIM)
    prob_f = soft_weights(scores)
    return jnp.einsum('rhl,rlhe->rhe', prob_f, value_rows).reshape(ROWS_DEV, D)

def cross_block(entry):
    query, key_int, value_int, key_sc, value_sc = entry
    key_deq = (key_int.astype(jnp.float32).reshape(SENT_DEV, SRC, HEADS, HEAD_DIM) * key_sc[:, None, :, None]).astype(jnp.bfloat16)
    value_deq = (value_int.astype(jnp.float32).reshape(SENT_DEV, SRC, HEADS, HEAD_DIM) * value_sc[:, None, :, None]).astype(jnp.bfloat16)
    key_deq = lax.optimization_barrier(key_deq).astype(jnp.float32)
    value_deq = lax.optimization_barrier(value_deq).astype(jnp.float32)
    query = query.reshape(SENT_DEV, BEAMS, HEADS, HEAD_DIM).astype(jnp.float32)
    scores = jnp.einsum('sbhe,slhe->sbhl', query, key_deq) / math.sqrt(HEAD_DIM)
    prob_f = soft_weights(scores)
    return jnp.einsum('sbhl,slhe->sbhe', prob_f, value_deq).reshape(ROWS_DEV, D)

def mixture(normed, chosen_ids, w_in, w_out):
    blocks = TOKENS // ROWS_DEV
    per_block = ROWS_DEV * TOP
    picked_ids = chosen_ids.reshape(blocks, per_block)
    one_hot = (picked_ids[:, :, None] == jnp.arange(EXPERTS, dtype=jnp.int32)[None, None, :]).astype(jnp.int32)
    before = jnp.cumsum(one_hot, axis=1) - one_hot
    slot_pos = lax.optimization_barrier(jnp.sum(before * one_hot, axis=2))
    block_ids = jnp.arange(blocks, dtype=jnp.int32)[:, None]
    column = (picked_ids * (blocks * CAP) + block_ids * CAP + slot_pos).reshape(-1).astype(jnp.int32)
    token_ids = (block_ids * ROWS_DEV + jnp.arange(per_block, dtype=jnp.int32)[None, :] // TOP).reshape(-1).astype(jnp.int32)
    buffer_rows = EXPERTS * blocks * CAP
    filled = jnp.zeros((buffer_rows,), jnp.int32).at[column].set(1)
    token_of = jnp.zeros((buffer_rows,), jnp.int32).at[column].set(token_ids)
    inputs = jnp.where(filled[:, None] > 0, jnp.take(normed, token_of, axis=0), jnp.zeros((), jnp.bfloat16))
    inputs = inputs.reshape(EXPERTS, blocks * CAP, D)
    slice_width = FF // N_DP

    def one_expert(entry):
        rows_in, first_w, second_w = entry
        units = jax.nn.relu(jnp.dot(rows_in, first_w, preferred_element_type=jnp.float32)).astype(jnp.bfloat16)
        units = lax.optimization_barrier(units).astype(jnp.float32)
        partial_sums = jnp.einsum('mjf,jfd->jmd', units.reshape(-1, N_DP, slice_width), second_w.reshape(N_DP, slice_width, D).astype(jnp.float32))
        rounded = lax.optimization_barrier(partial_sums.astype(jnp.bfloat16)).astype(jnp.float32)
        return lax.optimization_barrier(jnp.sum(rounded, axis=0)).astype(jnp.bfloat16)
    results = lax.map(one_expert, (inputs, w_in, w_out)).reshape(buffer_rows, D)
    return jnp.take(results, column, axis=0).reshape(TOKENS, TOP, D)

def reference(hidden, q_self, k_new, v_new, q_cross, cache_keys, cache_values, cross_keys, cross_values, key_scale, value_scale, parents, expert_ids, norm_gain, router, w_in, w_out):
    blocks = TOKENS // ROWS_DEV
    key_cache, value_cache = (cache_keys, cache_values)
    outputs = []
    for step_index in range(STEPS):
        key_cache = jnp.take(key_cache, parents[step_index], axis=0)
        value_cache = jnp.take(value_cache, parents[step_index], axis=0)
        key_cache = jnp.concatenate([key_cache, k_new[step_index][:, None, :]], axis=1)
        value_cache = jnp.concatenate([value_cache, v_new[step_index][:, None, :]], axis=1)
        length = key_cache.shape[1]
        self_out = lax.map(self_block, (q_self[step_index].reshape(blocks, ROWS_DEV, D), key_cache.reshape(blocks, ROWS_DEV, length, D), value_cache.reshape(blocks, ROWS_DEV, length, D))).reshape(TOKENS, D)
        cross_out = lax.map(cross_block, (q_cross[step_index].reshape(blocks, ROWS_DEV, D), cross_keys.reshape(blocks, SENT_DEV, SRC, D), cross_values.reshape(blocks, SENT_DEV, SRC, D), key_scale.reshape(blocks, SENT_DEV, HEADS), value_scale.reshape(blocks, SENT_DEV, HEADS))).reshape(TOKENS, D)
        residual = hidden[step_index].astype(jnp.float32) + self_out + cross_out
        average = lax.optimization_barrier(jnp.mean(residual, axis=1, keepdims=True))
        centered = residual - average
        variance = lax.optimization_barrier(jnp.mean(centered * centered, axis=1, keepdims=True))
        normed = (centered * lax.rsqrt(variance + epsilon) * norm_gain[None, :]).astype(jnp.bfloat16)
        logits = jnp.dot(normed, router, preferred_element_type=jnp.float32)
        chosen = jnp.take_along_axis(logits, expert_ids[step_index], axis=1)
        first_gate = jax.nn.sigmoid(chosen[:, 0] - chosen[:, 1])
        gate_mix = jnp.stack([first_gate, 1.0 - first_gate], axis=1)
        expert_out = mixture(normed, expert_ids[step_index], w_in, w_out).astype(jnp.float32)
        outputs.append((residual + lax.optimization_barrier(jnp.sum(gate_mix[:, :, None] * expert_out, axis=1))).astype(jnp.bfloat16))
    return jnp.stack(outputs, axis=0)
```

```python
import functools
import math

import jax
import jax.numpy as jnp
from jax import lax
from jax.experimental import pallas as pl
from jax.experimental.pallas import tpu as pltpu
from jax.sharding import PartitionSpec as P

epsilon = 1e-05
MESH = pl.DeviceIdType.MESH
BF = jnp.bfloat16
F32 = jnp.float32
LOW = -1e30
FLOOR = -1e20


def iota(shape, dim):
    return lax.broadcasted_iota(jnp.int32, shape, dim)


def as_column(row, n):
    return jnp.sum(jnp.where(iota((n, n), 0) == iota((n, n), 1), row, 0.0), axis=1, keepdims=True)


def pick(row, index_col, n):
    lanes = iota((n, n), 1).astype(F32)
    return jnp.sum(jnp.where(lanes == index_col, row, 0.0), axis=1, keepdims=True)


def inside(value, start, n):
    return (value >= start) & (value < start + n)


def remote_rank(row, start, n):
    far = jnp.where(inside(row, start, n), 0.0, 1.0)
    far_col = as_column(far, n)
    rank = jnp.sum(jnp.where(iota((n, n), 0) < iota((n, n), 1), far_col, 0.0), axis=0, keepdims=True)
    return far, rank


def bdot(a, b):
    return lax.dot_general(a, b, (((1,), (0,)), ((), ())), preferred_element_type=F32)


def tdot(a, b):
    return lax.dot_general(a, b, (((1,), (1,)), ((), ())), preferred_element_type=F32)


def attention_kernel(
    n_dp, n_ex, rows, cache, src, beams, chunks,
    hidden, q_self, k_new, v_new, q_cross, parents, key_scale, value_scale, gain,
    ck_hbm, cv_hbm, xk_hbm, xv_hbm,
    residual_ref, normed_ref,
    kbuf, vbuf, xkbuf, xvbuf, q_all, o_all, o_send, x_out, bias, bias_e, bias_x, scales,
    stat, par_own, par_in, q_d, q_e, in_c, in_d, in_e, o_d, o_e, back_c, back_d, back_e, stat_in, stat_in2,
    load_sem, send_sem, recv_sem,
):
    width = hidden.shape[2]
    heads = key_scale.shape[1]
    size = width // heads
    per_chunk = heads // chunks
    quarter = width // 4
    n_dev = n_dp * n_ex
    me = lax.axis_index("dp") * n_ex + lax.axis_index("expert")

    def at(offset):
        other = lax.rem(me + offset + n_dev, n_dev)
        return (other // n_ex, lax.rem(other, n_ex))

    barrier = pltpu.get_barrier_semaphore()
    for offset in (-1, -2, 1, 2):
        pl.semaphore_signal(barrier, inc=1, device_id=at(offset), device_id_type=MESH)

    loads = []
    for k, (source, buffer) in enumerate(
        ((ck_hbm, kbuf), (cv_hbm, vbuf), (xk_hbm, xkbuf), (xv_hbm, xvbuf))
    ):
        for c in range(chunks):
            loads.append((k, c, source, buffer))

    def load(k, c, source, buffer):
        part = width // chunks
        return pltpu.make_async_copy(
            source.at[:, pl.ds(pl.multiple_of(c * part, part), part)], buffer.at[c], load_sem.at[k, c]
        )

    for c in range(chunks):
        load(0, c, ck_hbm, kbuf).start()
        load(1, c, cv_hbm, vbuf).start()
    for c in range(chunks):
        load(2, c, xk_hbm, xkbuf).start()
        load(3, c, xv_hbm, xvbuf).start()

    par_own[...] = jnp.zeros_like(par_own)
    par_own[0:2, 0:rows] = parents[...]
    own = (me * rows).astype(F32)
    after = (lax.rem(me + 1, n_dev) * rows).astype(F32)
    after2 = (lax.rem(me + 2, n_dev) * rows).astype(F32)
    p0 = parents[0:1, :].astype(F32)
    p1 = parents[1:2, :].astype(F32)
    far0, rank0 = remote_rank(p0, own, rows)
    far1, rank1 = remote_rank(p1, own, rows)
    far0_col, rank0_col = as_column(far0, rows), as_column(rank0, rows)
    far1_col, rank1_col = as_column(far1, rows), as_column(rank1, rows)
    sub = iota((16, rows), 0)
    lane = iota((rows, 16), 1)

    def compact(value, far, rank):
        total = jnp.zeros((16, quarter), F32)
        for k in range(4):
            hot = ((sub >> 2) == k) & ((sub & 3).astype(F32) == rank) & (far > 0.5)
            total += bdot(jnp.where(hot, 1.0, 0.0).astype(BF), value[:, k * quarter:(k + 1) * quarter])
        return total.astype(BF)

    q_d[...] = compact(q_self[0], far0, rank0)
    q_e[...] = compact(q_self[1], far1, rank1)

    def remote(source, target, number, offset):
        return pltpu.make_async_remote_copy(
            src_ref=source, dst_ref=target, send_sem=send_sem.at[number], recv_sem=recv_sem.at[number],
            device_id=at(offset), device_id_type=MESH,
        )

    out_copies = [
        remote(par_own, par_in.at[0], 0, -1),
        remote(par_own, par_in.at[1], 1, -2),
        remote(q_d, in_d, 2, -1),
        remote(q_e, in_e, 3, -2),
        remote(q_self.at[1], in_c, 4, -1),
    ]
    pl.semaphore_wait(barrier, 4)
    for copy in out_copies:
        copy.start()

    sentence = (iota((2 * rows, 1), 0) & (rows - 1)) // beams
    ks = jnp.zeros((2 * rows, heads), F32)
    vs = jnp.zeros((2 * rows, heads), F32)
    for s in range(rows // beams):
        ks = jnp.where(sentence == s, key_scale[s:s + 1, :], ks)
        vs = jnp.where(sentence == s, value_scale[s:s + 1, :], vs)
    root = 1.0 / math.sqrt(size)
    scales[0, :, 0:heads] = ks * root
    scales[1, :, 0:heads] = vs
    n_cross = (rows // beams) * src
    bias_x[...] = jnp.where(
        iota((2 * rows, n_cross), 1) // src == (iota((2 * rows, n_cross), 0) & (rows - 1)) // beams, 0.0, LOW
    )
    q_all[0:rows, :] = q_self[0]
    q_all[rows:2 * rows, :] = q_self[1]

    for copy in out_copies:
        copy.wait()
    q_all[2 * rows:3 * rows, :] = in_c[...]
    a16, b16 = iota((16, 16), 0), iota((16, 16), 1)
    for k in range(4):
        take_d = jnp.where((b16 == a16 + 4 * k) & (a16 < 4), 1.0, 0.0).astype(BF)
        take_e = jnp.where((b16 == a16 - 4 + 4 * k) & (a16 >= 4) & (a16 < 8), 1.0, 0.0).astype(BF)
        q_all[3 * rows:4 * rows, k * quarter:(k + 1) * quarter] = (
            bdot(take_d, in_d[...]) + bdot(take_e, in_e[...])
        ).astype(BF)

    n0 = par_in[0, 0:1, 0:rows].astype(F32)
    n1 = par_in[0, 1:2, 0:rows].astype(F32)
    m1 = par_in[1, 1:2, 0:rows].astype(F32)
    p0_col, p1_col = as_column(p0, rows), as_column(p1, rows)
    n1_col = as_column(n1, rows)
    index = iota((rows, 1), 0).astype(F32)
    none = jnp.full((rows, 1), -1000.0, F32)

    def local(value):
        return jnp.where(inside(value, own, rows), value - own, -1.0)

    own_b = p1_col - own
    in_own = inside(p1_col, own, rows)
    row_b = jnp.where(in_own, local(pick(p0, own_b, rows)), -1.0)
    first_b = jnp.where(in_own, own_b, -1.0)
    in_next = inside(n1_col, after, rows)
    in_here = inside(n1_col, own, rows)
    row_c = jnp.where(
        in_next,
        local(pick(n0, n1_col - after, rows)),
        jnp.where(in_here, local(pick(p0, n1_col - own, rows)), -1.0),
    )
    first_c = jnp.where(in_here & jnp.logical_not(in_next), n1_col - own, -1.0)
    far_n, rank_n = remote_rank(n0, after, rows)
    far_m, rank_m = remote_rank(m1, after2, rows)
    i_col = iota((rows, rows), 0).astype(F32)
    val_d = jnp.sum(jnp.where((rank_n == i_col) & (far_n > 0.5), n0, 0.0), axis=1, keepdims=True)
    val_e = jnp.sum(jnp.where((rank_m == i_col - 4.0) & (far_m > 0.5), m1, 0.0), axis=1, keepdims=True)
    row_de = jnp.where(
        index < 4.0,
        local(val_d),
        jnp.where(
            (index < 8.0) & inside(val_e, after, rows), local(pick(n0, val_e - after, rows)), -1.0
        ),
    )
    row_sel = jnp.concatenate([local(p0_col), row_b, row_c, row_de], axis=0)
    first_sel = jnp.concatenate([index, first_b, first_c, none], axis=0)
    second_sel = jnp.concatenate([none, index, none, none], axis=0)
    slots = 4 * rows
    bias[...] = jnp.where((iota((slots, rows * cache), 1) // cache).astype(F32) == row_sel, 0.0, LOW)
    lane_e = iota((slots, 2 * rows), 1).astype(F32)
    bias_e[...] = jnp.where((lane_e == first_sel) | (lane_e - rows == second_sel), 0.0, LOW)

    stat[...] = jnp.zeros_like(stat)
    lanes = iota((slots, 128), 1)

    def self_chunk(c, carry):
        load(0, c, ck_hbm, kbuf).wait()
        load(1, c, cv_hbm, vbuf).wait()
        for j in range(per_chunk):
            h = c * per_chunk + j
            at_h = pl.ds(pl.multiple_of(h * size, size), size)
            q = q_all[:, at_h]
            k_extra = jnp.concatenate([k_new[0, :, at_h], k_new[1, :, at_h]], axis=0)
            v_extra = jnp.concatenate([v_new[0, :, at_h], v_new[1, :, at_h]], axis=0)
            s = tdot(q, kbuf[c, :, j * size:(j + 1) * size]) * root + bias[...]
            s_e = tdot(q, k_extra) * root + bias_e[...]
            top = jnp.maximum(
                jnp.maximum(jnp.max(s, axis=1, keepdims=True), jnp.max(s_e, axis=1, keepdims=True)), FLOOR
            )
            w = jnp.exp(s - top)
            w_e = jnp.exp(s_e - top)
            total = jnp.sum(w, axis=1, keepdims=True) + jnp.sum(w_e, axis=1, keepdims=True)
            o = bdot(w.astype(BF), vbuf[c, :, j * size:(j + 1) * size]) + bdot(w_e.astype(BF), v_extra)
            o_all[:, at_h] = o
            stat[0] = jnp.where(lanes == h, top, stat[0])
            stat[1] = jnp.where(lanes == h, total, stat[1])
        return carry

    lax.fori_loop(0, chunks, self_chunk, 0)

    o_send[...] = o_all[2 * rows:4 * rows, :].astype(BF)
    total_d = jnp.zeros((16, quarter), F32)
    total_e = jnp.zeros((16, quarter), F32)
    for k in range(4):
        piece = o_send[rows:2 * rows, k * quarter:(k + 1) * quarter]
        put_d = jnp.where(((a16 >> 2) == k) & (b16 == (a16 & 3)), 1.0, 0.0).astype(BF)
        put_e = jnp.where(((a16 >> 2) == k) & (b16 == (a16 & 3) + 4), 1.0, 0.0).astype(BF)
        total_d += bdot(put_d, piece)
        total_e += bdot(put_e, piece)
    o_d[...] = total_d.astype(BF)
    o_e[...] = total_e.astype(BF)
    back_copies = [
        remote(o_send.at[pl.ds(0, rows)], back_c, 5, 1),
        remote(o_d, back_d, 6, 1),
        remote(o_e, back_e, 7, 2),
        remote(stat.at[:, pl.ds(2 * rows, rows + 8)], stat_in, 8, 1),
        remote(stat.at[:, pl.ds(3 * rows, 8)], stat_in2, 9, 2),
    ]
    for copy in back_copies:
        copy.start()

    def cross_chunk(c, carry):
        load(2, c, xk_hbm, xkbuf).wait()
        load(3, c, xv_hbm, xvbuf).wait()
        for j in range(per_chunk):
            h = c * per_chunk + j
            at_h = pl.ds(pl.multiple_of(h * size, size), size)
            lanes_x = iota((2 * rows, 128), 1)
            ks_h = jnp.sum(jnp.where(lanes_x == h, scales[0], 0.0), axis=1, keepdims=True)
            vs_h = jnp.sum(jnp.where(lanes_x == h, scales[1], 0.0), axis=1, keepdims=True)
            q = jnp.concatenate([q_cross[0, :, at_h], q_cross[1, :, at_h]], axis=0)
            s = tdot(q, xkbuf[c, :, j * size:(j + 1) * size]) * ks_h + bias_x[...]
            top = jnp.max(s, axis=1, keepdims=True)
            w = jnp.exp(s - top)
            total = jnp.sum(w, axis=1, keepdims=True)
            o = bdot(w.astype(BF), xvbuf[c, :, j * size:(j + 1) * size])
            x_out[:, at_h] = o * (vs_h / total)
        return carry

    lax.fori_loop(0, chunks, cross_chunk, 0)

    for copy in back_copies:
        copy.wait()

    def spread(compact_ref, far_col, rank_col):
        pieces = []
        for k in range(4):
            hot = ((lane >> 2) == k) & ((lane & 3).astype(F32) == rank_col) & (far_col > 0.5)
            pieces.append(bdot(jnp.where(hot, 1.0, 0.0).astype(BF), compact_ref[...]))
        return pieces

    def spread_stat(ref, start, far_col, rank_col):
        top = jnp.where(far_col > 0.5, 0.0, FLOOR) + jnp.zeros((rows, 128), F32)
        total = jnp.zeros((rows, 128), F32)
        for j in range(4):
            hot = (rank_col == float(j)) & (far_col > 0.5)
            top += jnp.where(hot, ref[0, start + j:start + j + 1, :], 0.0)
            total += jnp.where(hot, ref[1, start + j:start + j + 1, :], 0.0)
        return top, total

    o_far0 = spread(back_d, far0_col, rank0_col)
    o_far1 = spread(back_e, far1_col, rank1_col)
    stats0 = [
        (stat[0, 0:rows, :], stat[1, 0:rows, :]),
        spread_stat(stat_in, rows, far0_col, rank0_col),
    ]
    stats1 = [
        (stat[0, rows:2 * rows, :], stat[1, rows:2 * rows, :]),
        (stat_in[0, 0:rows, :], stat_in[1, 0:rows, :]),
        spread_stat(stat_in2, 4, far1_col, rank1_col),
    ]

    def weights(stats):
        top = stats[0][0]
        for t, _ in stats[1:]:
            top = jnp.maximum(top, t)
        parts = [jnp.exp(t - top) for t, _ in stats]
        total = sum(w * l for w, (_, l) in zip(parts, stats))
        return [w / total for w in parts]

    w0 = weights(stats0)
    w1 = weights(stats1)
    per_quarter = heads // 4
    for t in range(2):
        for h in range(heads):
            at_h = slice(h * size, (h + 1) * size)
            k, j = h // per_quarter, h % per_quarter
            inner = slice(j * size, (j + 1) * size)
            if t == 0:
                mixed = o_all[0:rows, at_h] * w0[0][:, h:h + 1] + o_far0[k][:, inner] * w0[1][:, h:h + 1]
            else:
                mixed = (
                    o_all[rows:2 * rows, at_h] * w1[0][:, h:h + 1]
                    + back_c[:, at_h].astype(F32) * w1[1][:, h:h + 1]
                    + o_far1[k][:, inner] * w1[2][:, h:h + 1]
                )
            residual_ref[t, :, at_h] = (
                hidden[t, :, at_h].astype(F32) + mixed + x_out[t * rows:(t + 1) * rows, at_h]
            )
    for t in range(2):
        value = residual_ref[t]
        average = jnp.mean(value, axis=1, keepdims=True)
        centered = value - average
        variance = jnp.mean(centered * centered, axis=1, keepdims=True)
        normed_ref[t] = (centered * lax.rsqrt(variance + epsilon) * gain[...]).astype(BF)


def attention(hidden, q_self, k_new, v_new, q_cross, cache_keys, cache_values, cross_keys, cross_values,
              key_scale, value_scale, parents, norm_gain):
    steps, rows, width = hidden.shape
    heads = key_scale.shape[1]
    cache = cache_keys.shape[1]
    sentences, src = cross_keys.shape[:2]
    chunks = 4
    n_dp, n_ex = lax.axis_size("dp"), lax.axis_size("expert")
    part = width // chunks
    n_self, n_cross, slots = rows * cache, sentences * src, 4 * rows
    vmem = pl.BlockSpec(memory_space=pltpu.VMEM)
    hbm = pl.BlockSpec(memory_space=pl.ANY)
    quarter = width // 4
    return pl.pallas_call(
        functools.partial(attention_kernel, n_dp, n_ex, rows, cache, src, rows // sentences, chunks),
        out_shape=(
            jax.ShapeDtypeStruct((steps, rows, width), F32),
            jax.ShapeDtypeStruct((steps, rows, width), BF),
        ),
        in_specs=[vmem] * 9 + [hbm] * 4,
        out_specs=(vmem, vmem),
        scratch_shapes=[
            pltpu.VMEM((chunks, n_self, part), BF),
            pltpu.VMEM((chunks, n_self, part), BF),
            pltpu.VMEM((chunks, n_cross, part), BF),
            pltpu.VMEM((chunks, n_cross, part), BF),
            pltpu.VMEM((slots, width), BF),
            pltpu.VMEM((slots, width), F32),
            pltpu.VMEM((2 * rows, width), BF),
            pltpu.VMEM((2 * rows, width), F32),
            pltpu.VMEM((slots, n_self), F32),
            pltpu.VMEM((slots, 2 * rows), F32),
            pltpu.VMEM((2 * rows, n_cross), F32),
            pltpu.VMEM((2, 2 * rows, 128), F32),
            pltpu.VMEM((2, slots, 128), F32),
            pltpu.VMEM((8, 128), jnp.int32),
            pltpu.VMEM((2, 8, 128), jnp.int32),
            pltpu.VMEM((16, quarter), BF),
            pltpu.VMEM((16, quarter), BF),
            pltpu.VMEM((rows, width), BF),
            pltpu.VMEM((16, quarter), BF),
            pltpu.VMEM((16, quarter), BF),
            pltpu.VMEM((16, quarter), BF),
            pltpu.VMEM((16, quarter), BF),
            pltpu.VMEM((rows, width), BF),
            pltpu.VMEM((16, quarter), BF),
            pltpu.VMEM((16, quarter), BF),
            pltpu.VMEM((2, rows + 8, 128), F32),
            pltpu.VMEM((2, 8, 128), F32),
            pltpu.SemaphoreType.DMA((4, chunks)),
            pltpu.SemaphoreType.DMA((10,)),
            pltpu.SemaphoreType.DMA((10,)),
        ],
        compiler_params=pltpu.CompilerParams(
            collective_id=0, has_side_effects=True, vmem_limit_bytes=48 * 2**20
        ),
    )(
        hidden, q_self, k_new, v_new, q_cross, parents, key_scale, value_scale, norm_gain.reshape(1, width),
        cache_keys.reshape(n_self, width), cache_values.reshape(n_self, width),
        cross_keys.reshape(n_cross, width), cross_values.reshape(n_cross, width),
    )


def experts_apply(normed, chosen_ids, w_in, w_out):
    stack_size, row_count, top_count = chosen_ids.shape
    width = normed.shape[2]
    expert_count = lax.axis_size("expert") * w_in.shape[0]
    capacity = max(2, 2 * row_count * top_count // expert_count)
    picked_ids = chosen_ids.reshape(stack_size, row_count * top_count)
    one_hot = (
        picked_ids[:, :, None] == jnp.arange(expert_count, dtype=jnp.int32)[None, None, :]
    ).astype(jnp.int32)
    before = jnp.cumsum(one_hot, axis=1) - one_hot
    slot_pos = jnp.sum(before * one_hot, axis=2)
    column = (
        picked_ids * (stack_size * capacity)
        + jnp.arange(stack_size, dtype=jnp.int32)[:, None] * capacity
        + slot_pos
    )
    columns = expert_count * stack_size * capacity
    dispatch = (
        column.reshape(-1)[:, None] == jnp.arange(columns, dtype=jnp.int32)[None, :]
    ).astype(jnp.bfloat16)
    sources = jnp.repeat(normed.reshape(stack_size * row_count, width), top_count, axis=0)
    outgoing = jnp.einsum(
        "pc,pd->cd", dispatch, sources, preferred_element_type=jnp.float32
    ).astype(jnp.bfloat16)
    outgoing = outgoing.reshape(expert_count, stack_size * capacity, width)
    arrived = lax.all_to_all(outgoing, "expert", split_axis=0, concat_axis=0, tiled=True)
    arrived = arrived.reshape(lax.axis_size("expert"), w_in.shape[0], stack_size * capacity, width)
    units = jax.nn.relu(
        jnp.einsum(
            "secd,edf->secf",
            lax.all_gather(arrived, "dp", axis=0, tiled=True),
            w_in,
            preferred_element_type=jnp.float32,
        )
    ).astype(jnp.bfloat16)
    partial_out = jnp.einsum(
        "secf,efd->secd", units, w_out, preferred_element_type=jnp.float32
    ).astype(jnp.bfloat16)
    summed = (
        lax.psum_scatter(partial_out, "dp", scatter_dimension=0, tiled=True)
        .astype(jnp.float32)
        .astype(jnp.bfloat16)
    )
    returned = lax.all_to_all(
        summed.reshape(expert_count, stack_size * capacity, width),
        "expert",
        split_axis=0,
        concat_axis=0,
        tiled=True,
    )
    gathered = jnp.dot(
        dispatch, returned.reshape(columns, width), preferred_element_type=jnp.float32
    )
    return gathered.reshape(stack_size, row_count, top_count, width)


def finish(residual, normed, chosen_ids, router, w_in, w_out):
    expert_count = router.shape[1]
    logits = jnp.einsum("srd,de->sre", normed, router, preferred_element_type=jnp.float32)
    match_table = (
        chosen_ids[:, :, :, None] == jnp.arange(expert_count, dtype=jnp.int32)[None, None, None, :]
    )
    chosen = jnp.sum(jnp.where(match_table, logits[:, :, None, :], 0.0), axis=3)
    first_gate = jax.nn.sigmoid(chosen[:, :, 0] - chosen[:, :, 1])
    gate_mix = jnp.stack([first_gate, 1.0 - first_gate], axis=2)
    expert_out = experts_apply(normed, chosen_ids, w_in, w_out)
    return (residual + jnp.sum(gate_mix[:, :, :, None] * expert_out, axis=2)).astype(jnp.bfloat16)


def shards(
    hidden, q_self, k_new, v_new, q_cross, cache_keys, cache_values, cross_keys, cross_values,
    key_scale, value_scale, parents, expert_ids, norm_gain, router, w_in, w_out,
):
    residual, normed = attention(
        hidden, q_self, k_new, v_new, q_cross, cache_keys, cache_values, cross_keys, cross_values,
        key_scale, value_scale, parents, norm_gain,
    )
    return finish(residual, normed, expert_ids, router, w_in, w_out)


def solution(mesh):
    in_specs = (
        P(None, ("dp", "expert"), None),
        P(None, ("dp", "expert"), None),
        P(None, ("dp", "expert"), None),
        P(None, ("dp", "expert"), None),
        P(None, ("dp", "expert"), None),
        P(("dp", "expert"), None, None),
        P(("dp", "expert"), None, None),
        P(("dp", "expert"), None, None),
        P(("dp", "expert"), None, None),
        P(("dp", "expert"), None),
        P(("dp", "expert"), None),
        P(None, ("dp", "expert")),
        P(None, ("dp", "expert"), None),
        P(),
        P(),
        P("expert", None, "dp"),
        P("expert", "dp", None),
    )
    out_specs = P(None, ("dp", "expert"), None)
    return jax.shard_map(shards, mesh=mesh, in_specs=in_specs, out_specs=out_specs, check_vma=False)
```

```python
import functools
import math

import jax
import jax.numpy as jnp
from jax import lax
from jax.experimental import pallas as pl
from jax.experimental.pallas import tpu as pltpu
from jax.sharding import PartitionSpec as P

epsilon = 1e-05
MESH = pl.DeviceIdType.MESH
BF = jnp.bfloat16
F32 = jnp.float32
LOW = -1e30
FLOOR = -1e20


def iota(shape, dim):
    return lax.broadcasted_iota(jnp.int32, shape, dim)


def as_column(row, n):
    return jnp.sum(jnp.where(iota((n, n), 0) == iota((n, n), 1), row, 0.0), axis=1, keepdims=True)


def pick(row, index_col, n):
    lanes = iota((n, n), 1).astype(F32)
    return jnp.sum(jnp.where(lanes == index_col, row, 0.0), axis=1, keepdims=True)


def inside(value, start, n):
    return (value >= start) & (value < start + n)


def remote_rank(row, start, n):
    far = jnp.where(inside(row, start, n), 0.0, 1.0)
    far_col = as_column(far, n)
    rank = jnp.sum(jnp.where(iota((n, n), 0) < iota((n, n), 1), far_col, 0.0), axis=0, keepdims=True)
    return far, rank


def bdot(a, b):
    return lax.dot_general(a, b, (((1,), (0,)), ((), ())), preferred_element_type=F32)


def tdot(a, b):
    return lax.dot_general(a, b, (((1,), (1,)), ((), ())), preferred_element_type=F32)


def attention_kernel(
    n_dp, n_ex, rows, cache, src, beams, chunks,
    hidden_hbm, q_self_hbm, k_new_hbm, v_new_hbm, q_cross_hbm, parents_hbm, ks_hbm, vs_hbm, gain_hbm,
    ck_hbm, cv_hbm, xk_hbm, xv_hbm,
    residual_ref, normed_ref,
    hidden, q_self, k_new, v_new, q_cross, parents, key_scale, value_scale, gain,
    kbuf, vbuf, xkbuf, xvbuf, q_all, o_all, o_send, x_out, bias, bias_e, bias_x, scales,
    stat, par_own, par_in, q_d, q_e, in_c, in_d, in_e, o_d, o_e, back_c, back_d, back_e, stat_in, stat_in2,
    load_sem, small_sem, send_sem, recv_sem,
):
    width = hidden.shape[2]
    heads = key_scale.shape[1]
    size = width // heads
    per_chunk = heads // chunks
    quarter = width // 4
    n_dev = n_dp * n_ex
    me = lax.axis_index("dp") * n_ex + lax.axis_index("expert")

    def at(offset):
        other = lax.rem(me + offset + n_dev, n_dev)
        return (other // n_ex, lax.rem(other, n_ex))

    barrier = pltpu.get_barrier_semaphore()
    for offset in (-1, -2, 1, 2):
        pl.semaphore_signal(barrier, inc=1, device_id=at(offset), device_id_type=MESH)

    def load(k, c, source, buffer):
        part = width // chunks
        return pltpu.make_async_copy(
            source.at[:, pl.ds(pl.multiple_of(c * part, part), part)], buffer.at[c], load_sem.at[k, c]
        )

    small = [
        pltpu.make_async_copy(source, target, small_sem.at[i])
        for i, (source, target) in enumerate((
            (parents_hbm, parents), (q_self_hbm, q_self), (k_new_hbm, k_new), (v_new_hbm, v_new),
            (ks_hbm, key_scale), (vs_hbm, value_scale), (q_cross_hbm, q_cross), (hidden_hbm, hidden),
            (gain_hbm, gain),
        ))
    ]
    for copy in small:
        copy.start()
    for c in range(chunks):
        load(0, c, ck_hbm, kbuf).start()
        load(1, c, cv_hbm, vbuf).start()
    for c in range(chunks):
        load(2, c, xk_hbm, xkbuf).start()
        load(3, c, xv_hbm, xvbuf).start()

    par_own[...] = jnp.zeros_like(par_own)
    small[0].wait()
    small[1].wait()
    par_own[0:2, 0:rows] = parents[...]
    own = (me * rows).astype(F32)
    after = (lax.rem(me + 1, n_dev) * rows).astype(F32)
    after2 = (lax.rem(me + 2, n_dev) * rows).astype(F32)
    p0 = parents[0:1, :].astype(F32)
    p1 = parents[1:2, :].astype(F32)
    far0, rank0 = remote_rank(p0, own, rows)
    far1, rank1 = remote_rank(p1, own, rows)
    far0_col, rank0_col = as_column(far0, rows), as_column(rank0, rows)
    far1_col, rank1_col = as_column(far1, rows), as_column(rank1, rows)
    sub = iota((16, rows), 0)
    lane = iota((rows, 16), 1)

    def compact(value, far, rank):
        total = jnp.zeros((16, quarter), F32)
        for k in range(4):
            hot = ((sub >> 2) == k) & ((sub & 3).astype(F32) == rank) & (far > 0.5)
            total += bdot(jnp.where(hot, 1.0, 0.0).astype(BF), value[:, k * quarter:(k + 1) * quarter])
        return total.astype(BF)

    q_d[...] = compact(q_self[0], far0, rank0)
    q_e[...] = compact(q_self[1], far1, rank1)

    def remote(source, target, number, offset):
        return pltpu.make_async_remote_copy(
            src_ref=source, dst_ref=target, send_sem=send_sem.at[number], recv_sem=recv_sem.at[number],
            device_id=at(offset), device_id_type=MESH,
        )

    out_copies = [
        remote(par_own, par_in.at[0], 0, -1),
        remote(par_own, par_in.at[1], 1, -2),
        remote(q_d, in_d, 2, -1),
        remote(q_e, in_e, 3, -2),
        remote(q_self.at[1], in_c, 4, -1),
    ]
    pl.semaphore_wait(barrier, 4)
    for copy in out_copies:
        copy.start()

    small[4].wait()
    small[5].wait()
    sentence = (iota((2 * rows, 1), 0) & (rows - 1)) // beams
    ks = jnp.zeros((2 * rows, heads), F32)
    vs = jnp.zeros((2 * rows, heads), F32)
    for s in range(rows // beams):
        ks = jnp.where(sentence == s, key_scale[s:s + 1, :], ks)
        vs = jnp.where(sentence == s, value_scale[s:s + 1, :], vs)
    root = 1.0 / math.sqrt(size)
    scales[0, :, 0:heads] = ks * root
    scales[1, :, 0:heads] = vs
    n_cross = (rows // beams) * src
    bias_x[...] = jnp.where(
        iota((2 * rows, n_cross), 1) // src == (iota((2 * rows, n_cross), 0) & (rows - 1)) // beams, 0.0, LOW
    )
    q_all[0:rows, :] = q_self[0]
    q_all[rows:2 * rows, :] = q_self[1]

    for i in (2, 3, 6, 7, 8):
        small[i].wait()
    for copy in out_copies:
        copy.wait()
    q_all[2 * rows:3 * rows, :] = in_c[...]
    a16, b16 = iota((16, 16), 0), iota((16, 16), 1)
    for k in range(4):
        take_d = jnp.where((b16 == a16 + 4 * k) & (a16 < 4), 1.0, 0.0).astype(BF)
        take_e = jnp.where((b16 == a16 - 4 + 4 * k) & (a16 >= 4) & (a16 < 8), 1.0, 0.0).astype(BF)
        q_all[3 * rows:4 * rows, k * quarter:(k + 1) * quarter] = (
            bdot(take_d, in_d[...]) + bdot(take_e, in_e[...])
        ).astype(BF)

    n0 = par_in[0, 0:1, 0:rows].astype(F32)
    n1 = par_in[0, 1:2, 0:rows].astype(F32)
    m1 = par_in[1, 1:2, 0:rows].astype(F32)
    p0_col, p1_col = as_column(p0, rows), as_column(p1, rows)
    n1_col = as_column(n1, rows)
    index = iota((rows, 1), 0).astype(F32)
    none = jnp.full((rows, 1), -1000.0, F32)

    def local(value):
        return jnp.where(inside(value, own, rows), value - own, -1.0)

    own_b = p1_col - own
    in_own = inside(p1_col, own, rows)
    row_b = jnp.where(in_own, local(pick(p0, own_b, rows)), -1.0)
    first_b = jnp.where(in_own, own_b, -1.0)
    in_next = inside(n1_col, after, rows)
    in_here = inside(n1_col, own, rows)
    row_c = jnp.where(
        in_next,
        local(pick(n0, n1_col - after, rows)),
        jnp.where(in_here, local(pick(p0, n1_col - own, rows)), -1.0),
    )
    first_c = jnp.where(in_here & jnp.logical_not(in_next), n1_col - own, -1.0)
    far_n, rank_n = remote_rank(n0, after, rows)
    far_m, rank_m = remote_rank(m1, after2, rows)
    i_col = iota((rows, rows), 0).astype(F32)
    val_d = jnp.sum(jnp.where((rank_n == i_col) & (far_n > 0.5), n0, 0.0), axis=1, keepdims=True)
    val_e = jnp.sum(jnp.where((rank_m == i_col - 4.0) & (far_m > 0.5), m1, 0.0), axis=1, keepdims=True)
    row_de = jnp.where(
        index < 4.0,
        local(val_d),
        jnp.where(
            (index < 8.0) & inside(val_e, after, rows), local(pick(n0, val_e - after, rows)), -1.0
        ),
    )
    row_sel = jnp.concatenate([local(p0_col), row_b, row_c, row_de], axis=0)
    first_sel = jnp.concatenate([index, first_b, first_c, none], axis=0)
    second_sel = jnp.concatenate([none, index, none, none], axis=0)
    slots = 4 * rows
    bias[...] = jnp.where((iota((slots, rows * cache), 1) // cache).astype(F32) == row_sel, 0.0, LOW)
    lane_e = iota((slots, 2 * rows), 1).astype(F32)
    bias_e[...] = jnp.where((lane_e == first_sel) | (lane_e - rows == second_sel), 0.0, LOW)

    stat[...] = jnp.zeros_like(stat)
    lanes = iota((slots, 128), 1)

    def self_chunk(c, carry):
        load(0, c, ck_hbm, kbuf).wait()
        load(1, c, cv_hbm, vbuf).wait()
        for j in range(per_chunk):
            h = c * per_chunk + j
            at_h = pl.ds(pl.multiple_of(h * size, size), size)
            q = q_all[:, at_h]
            k_extra = jnp.concatenate([k_new[0, :, at_h], k_new[1, :, at_h]], axis=0)
            v_extra = jnp.concatenate([v_new[0, :, at_h], v_new[1, :, at_h]], axis=0)
            s = tdot(q, kbuf[c, :, j * size:(j + 1) * size]) * root + bias[...]
            s_e = tdot(q, k_extra) * root + bias_e[...]
            top = jnp.maximum(
                jnp.maximum(jnp.max(s, axis=1, keepdims=True), jnp.max(s_e, axis=1, keepdims=True)), FLOOR
            )
            w = jnp.exp(s - top)
            w_e = jnp.exp(s_e - top)
            total = jnp.sum(w, axis=1, keepdims=True) + jnp.sum(w_e, axis=1, keepdims=True)
            o = bdot(w.astype(BF), vbuf[c, :, j * size:(j + 1) * size]) + bdot(w_e.astype(BF), v_extra)
            o_all[:, at_h] = o
            stat[0] = jnp.where(lanes == h, top, stat[0])
            stat[1] = jnp.where(lanes == h, total, stat[1])
        return carry

    lax.fori_loop(0, chunks, self_chunk, 0)

    o_send[...] = o_all[2 * rows:4 * rows, :].astype(BF)
    total_d = jnp.zeros((16, quarter), F32)
    total_e = jnp.zeros((16, quarter), F32)
    for k in range(4):
        piece = o_send[rows:2 * rows, k * quarter:(k + 1) * quarter]
        put_d = jnp.where(((a16 >> 2) == k) & (b16 == (a16 & 3)), 1.0, 0.0).astype(BF)
        put_e = jnp.where(((a16 >> 2) == k) & (b16 == (a16 & 3) + 4), 1.0, 0.0).astype(BF)
        total_d += bdot(put_d, piece)
        total_e += bdot(put_e, piece)
    o_d[...] = total_d.astype(BF)
    o_e[...] = total_e.astype(BF)
    back_copies = [
        remote(o_send.at[pl.ds(0, rows)], back_c, 5, 1),
        remote(o_d, back_d, 6, 1),
        remote(o_e, back_e, 7, 2),
        remote(stat.at[:, pl.ds(2 * rows, rows + 8)], stat_in, 8, 1),
        remote(stat.at[:, pl.ds(3 * rows, 8)], stat_in2, 9, 2),
    ]
    for copy in back_copies:
        copy.start()

    def cross_chunk(c, carry):
        load(2, c, xk_hbm, xkbuf).wait()
        load(3, c, xv_hbm, xvbuf).wait()
        for j in range(per_chunk):
            h = c * per_chunk + j
            at_h = pl.ds(pl.multiple_of(h * size, size), size)
            lanes_x = iota((2 * rows, 128), 1)
            ks_h = jnp.sum(jnp.where(lanes_x == h, scales[0], 0.0), axis=1, keepdims=True)
            vs_h = jnp.sum(jnp.where(lanes_x == h, scales[1], 0.0), axis=1, keepdims=True)
            q = jnp.concatenate([q_cross[0, :, at_h], q_cross[1, :, at_h]], axis=0)
            s = tdot(q, xkbuf[c, :, j * size:(j + 1) * size]) * ks_h + bias_x[...]
            top = jnp.max(s, axis=1, keepdims=True)
            w = jnp.exp(s - top)
            total = jnp.sum(w, axis=1, keepdims=True)
            o = bdot(w.astype(BF), xvbuf[c, :, j * size:(j + 1) * size])
            x_out[:, at_h] = o * (vs_h / total)
        return carry

    lax.fori_loop(0, chunks, cross_chunk, 0)

    for copy in back_copies:
        copy.wait()

    def spread(compact_ref, far_col, rank_col):
        pieces = []
        for k in range(4):
            hot = ((lane >> 2) == k) & ((lane & 3).astype(F32) == rank_col) & (far_col > 0.5)
            pieces.append(bdot(jnp.where(hot, 1.0, 0.0).astype(BF), compact_ref[...]))
        return pieces

    def spread_stat(ref, start, far_col, rank_col):
        top = jnp.where(far_col > 0.5, 0.0, FLOOR) + jnp.zeros((rows, 128), F32)
        total = jnp.zeros((rows, 128), F32)
        for j in range(4):
            hot = (rank_col == float(j)) & (far_col > 0.5)
            top += jnp.where(hot, ref[0, start + j:start + j + 1, :], 0.0)
            total += jnp.where(hot, ref[1, start + j:start + j + 1, :], 0.0)
        return top, total

    o_far0 = spread(back_d, far0_col, rank0_col)
    o_far1 = spread(back_e, far1_col, rank1_col)
    stats0 = [
        (stat[0, 0:rows, :], stat[1, 0:rows, :]),
        spread_stat(stat_in, rows, far0_col, rank0_col),
    ]
    stats1 = [
        (stat[0, rows:2 * rows, :], stat[1, rows:2 * rows, :]),
        (stat_in[0, 0:rows, :], stat_in[1, 0:rows, :]),
        spread_stat(stat_in2, 4, far1_col, rank1_col),
    ]

    def weights(stats):
        top = stats[0][0]
        for t, _ in stats[1:]:
            top = jnp.maximum(top, t)
        parts = [jnp.exp(t - top) for t, _ in stats]
        total = sum(w * l for w, (_, l) in zip(parts, stats))
        return [w / total for w in parts]

    w0 = weights(stats0)
    w1 = weights(stats1)
    per_quarter = heads // 4
    for t in range(2):
        for h in range(heads):
            at_h = slice(h * size, (h + 1) * size)
            k, j = h // per_quarter, h % per_quarter
            inner = slice(j * size, (j + 1) * size)
            if t == 0:
                mixed = o_all[0:rows, at_h] * w0[0][:, h:h + 1] + o_far0[k][:, inner] * w0[1][:, h:h + 1]
            else:
                mixed = (
                    o_all[rows:2 * rows, at_h] * w1[0][:, h:h + 1]
                    + back_c[:, at_h].astype(F32) * w1[1][:, h:h + 1]
                    + o_far1[k][:, inner] * w1[2][:, h:h + 1]
                )
            residual_ref[t, :, at_h] = (
                hidden[t, :, at_h].astype(F32) + mixed + x_out[t * rows:(t + 1) * rows, at_h]
            )
    for t in range(2):
        value = residual_ref[t]
        average = jnp.mean(value, axis=1, keepdims=True)
        centered = value - average
        variance = jnp.mean(centered * centered, axis=1, keepdims=True)
        normed_ref[t] = (centered * lax.rsqrt(variance + epsilon) * gain[...]).astype(BF)


def attention(hidden, q_self, k_new, v_new, q_cross, cache_keys, cache_values, cross_keys, cross_values,
              key_scale, value_scale, parents, norm_gain):
    steps, rows, width = hidden.shape
    heads = key_scale.shape[1]
    cache = cache_keys.shape[1]
    sentences, src = cross_keys.shape[:2]
    chunks = 4
    n_dp, n_ex = lax.axis_size("dp"), lax.axis_size("expert")
    part = width // chunks
    n_self, n_cross, slots = rows * cache, sentences * src, 4 * rows
    vmem = pl.BlockSpec(memory_space=pltpu.VMEM)
    hbm = pl.BlockSpec(memory_space=pl.ANY)
    quarter = width // 4
    return pl.pallas_call(
        functools.partial(attention_kernel, n_dp, n_ex, rows, cache, src, rows // sentences, chunks),
        out_shape=(
            jax.ShapeDtypeStruct((steps, rows, width), F32),
            jax.ShapeDtypeStruct((steps, rows, width), BF),
        ),
        in_specs=[hbm] * 13,
        out_specs=(vmem, vmem),
        scratch_shapes=[pltpu.VMEM((steps, rows, width), BF)] * 5 + [
            pltpu.VMEM((steps, rows), jnp.int32),
            pltpu.VMEM((sentences, heads), F32),
            pltpu.VMEM((sentences, heads), F32),
            pltpu.VMEM((1, width), F32),
            pltpu.VMEM((chunks, n_self, part), BF),
            pltpu.VMEM((chunks, n_self, part), BF),
            pltpu.VMEM((chunks, n_cross, part), BF),
            pltpu.VMEM((chunks, n_cross, part), BF),
            pltpu.VMEM((slots, width), BF),
            pltpu.VMEM((slots, width), F32),
            pltpu.VMEM((2 * rows, width), BF),
            pltpu.VMEM((2 * rows, width), F32),
            pltpu.VMEM((slots, n_self), F32),
            pltpu.VMEM((slots, 2 * rows), F32),
            pltpu.VMEM((2 * rows, n_cross), F32),
            pltpu.VMEM((2, 2 * rows, 128), F32),
            pltpu.VMEM((2, slots, 128), F32),
            pltpu.VMEM((8, 128), jnp.int32),
            pltpu.VMEM((2, 8, 128), jnp.int32),
            pltpu.VMEM((16, quarter), BF),
            pltpu.VMEM((16, quarter), BF),
            pltpu.VMEM((rows, width), BF),
            pltpu.VMEM((16, quarter), BF),
            pltpu.VMEM((16, quarter), BF),
            pltpu.VMEM((16, quarter), BF),
            pltpu.VMEM((16, quarter), BF),
            pltpu.VMEM((rows, width), BF),
            pltpu.VMEM((16, quarter), BF),
            pltpu.VMEM((16, quarter), BF),
            pltpu.VMEM((2, rows + 8, 128), F32),
            pltpu.VMEM((2, 8, 128), F32),
            pltpu.SemaphoreType.DMA((4, chunks)),
            pltpu.SemaphoreType.DMA((9,)),
            pltpu.SemaphoreType.DMA((10,)),
            pltpu.SemaphoreType.DMA((10,)),
        ],
        compiler_params=pltpu.CompilerParams(
            collective_id=0, has_side_effects=True, vmem_limit_bytes=60 * 2**20
        ),
    )(
        hidden, q_self, k_new, v_new, q_cross, parents, key_scale, value_scale, norm_gain.reshape(1, width),
        cache_keys.reshape(n_self, width), cache_values.reshape(n_self, width),
        cross_keys.reshape(n_cross, width), cross_values.reshape(n_cross, width),
    )


def experts_kernel(
    n_dp, n_ex, cap,
    residual_hbm, normed_hbm, ids_hbm, router_hbm, w_in_hbm, w_out_hbm,
    out_ref,
    residual, normed, ids, ids_all, router, w_in, w_out, outgoing, xbuf, units, p_mine, p_send, p_back,
    rs_a, rs_b, fin_a, fin_b, home, returned, y_send, y_back,
    load_sem, pair_s, pair_r, a2a_s, a2a_r, near_s, near_r, fwd_s, fwd_r, sib_s, sib_r, part_s, part_r,
    rs_s, rs_r, fin_s, fin_r, ret_s, ret_r,
):
    steps, rows = ids.shape[0], ids.shape[2]
    tokens = steps * rows
    width = residual.shape[1]
    half = width // 2
    hidden_units = w_in.shape[1]
    slots = 2 * steps * cap
    chunk = n_ex * slots
    group = chunk // 4
    dp = lax.axis_index("dp")
    me = lax.axis_index("expert")
    core = lax.rem(dp, 2)
    n_y = n_dp // 2
    place = dp // 2
    sibling = (dp + 1 - 2 * core, me)
    up_y = (lax.rem(place + 1, n_y) * 2 + core, me)
    down_y = (lax.rem(place + n_y - 1, n_y) * 2 + core, me)

    def peer(o):
        return (dp, lax.rem(me + o, n_ex))

    def peer_back(o):
        return (dp, lax.rem(me - o + n_ex, n_ex))

    barrier = pltpu.get_barrier_semaphore()
    others = [sibling, up_y, down_y] + [peer(o) for o in range(1, n_ex)]
    for other in others:
        pl.semaphore_signal(barrier, inc=1, device_id=other, device_id_type=MESH)

    mine = pl.ds(pl.multiple_of(core * tokens, tokens), tokens)
    theirs = pl.ds(pl.multiple_of((1 - core) * tokens, tokens), tokens)
    loads = [
        pltpu.make_async_copy(normed_hbm, normed.at[mine], load_sem.at[0]),
        pltpu.make_async_copy(ids_hbm, ids, load_sem.at[1]),
        pltpu.make_async_copy(router_hbm, router, load_sem.at[2]),
        pltpu.make_async_copy(w_in_hbm, w_in, load_sem.at[3]),
        pltpu.make_async_copy(w_out_hbm, w_out, load_sem.at[4]),
        pltpu.make_async_copy(residual_hbm, residual, load_sem.at[5]),
    ]
    for copy in loads:
        copy.start()

    started = []

    def send(source, target, s_sem, r_sem, device):
        copy = pltpu.make_async_remote_copy(
            src_ref=source, dst_ref=target, send_sem=s_sem, recv_sem=r_sem,
            device_id=device, device_id_type=MESH,
        )
        copy.start()
        started.append(copy)
        return copy

    loads[0].wait()
    loads[1].wait()
    for t in range(steps):
        named = [as_column(ids[t, k:k + 1, :].astype(F32), rows).astype(jnp.int32) for k in range(2)]
        ids_all[core, t * rows:(t + 1) * rows, :] = jnp.where(iota((rows, 128), 1) == 0, named[0], named[1])
    pl.semaphore_wait(barrier, len(others))
    pair = [
        send(normed.at[mine], normed.at[mine], pair_s.at[0], pair_r.at[0], sibling),
        send(ids_all.at[core], ids_all.at[core], pair_s.at[1], pair_r.at[1], sibling),
    ]
    for copy in pair:
        copy.wait_recv()

    lane_x = iota((tokens, 128), 1)
    lower = (iota((tokens, tokens), 1) < iota((tokens, tokens), 0)) & (
        iota((tokens, tokens), 0) // rows == iota((tokens, tokens), 1) // rows
    )
    lower = jnp.where(lower, 1.0, 0.0).astype(BF)
    step_of = (iota((tokens, 1), 0) // rows)
    hots = []
    for c in range(2):
        named = [ids_all[c, :, k:k + 1] for k in range(2)]
        one_hot = [lane_x == n for n in named]
        count = jnp.where(one_hot[0] | one_hot[1], 1.0, 0.0).astype(BF)
        before = bdot(lower, count)
        pair_hot = []
        for k in range(2):
            spot = jnp.sum(jnp.where(one_hot[k], before, 0.0), axis=1, keepdims=True).astype(jnp.int32)
            distance = named[k] - me
            distance = jnp.where(distance < 0, distance + n_ex, distance)
            column = distance * slots + (c * steps * cap + spot) + step_of * cap
            pair_hot.append(iota((tokens, chunk), 1) == column)
        hots.append(pair_hot)
    dispatch = jnp.concatenate([jnp.where(h[0] | h[1], 1.0, 0.0).astype(BF) for h in hots], axis=0)
    at_half = pl.ds(pl.multiple_of(core * half, half), half)
    outgoing[...] = lax.dot_general(
        dispatch, normed[:, at_half], (((0,), (0,)), ((), ())), preferred_element_type=F32
    ).astype(BF)

    def block(o):
        return pl.ds(o * slots, slots)

    arrivals = [None]
    for o in range(1, n_ex):
        arrivals.append(
            send(outgoing.at[block(o)], xbuf.at[core, 0, block(o)], a2a_s.at[o], a2a_r.at[o], peer(o))
        )
    xbuf[core, 0, block(0), :] = outgoing[block(0), :]

    loads[2].wait()
    logits = tdot(normed[...], router[...])
    lane_e = iota((tokens, n_ex), 1)
    gates = []
    for c in range(2):
        part = logits[c * tokens:(c + 1) * tokens]
        picked = [
            jnp.sum(jnp.where(lane_e == ids_all[c, :, k:k + 1], part, 0.0), axis=1, keepdims=True)
            for k in range(2)
        ]
        first = 1.0 / (1.0 + jnp.exp(picked[1] - picked[0]))
        gates.append(
            jnp.where(hots[c][0], first, 0.0) + jnp.where(hots[c][1], 1.0 - first, 0.0)
        )

    def piece(g):
        return pl.ds(g * group, group)

    per_group = n_ex // 4

    def to_sibling(k, g):
        return send(
            xbuf.at[core, k, piece(g)], xbuf.at[core, k, piece(g)], sib_s.at[k, g], sib_r.at[k, g], sibling
        )

    tile = min(256, half, hidden_units)

    def compute(k):
        def first(j, carry):
            cols = pl.ds(pl.multiple_of(j * tile, tile), tile)
            a = bdot(xbuf[0, k], w_in[0:half, cols]) + bdot(xbuf[1, k], w_in[half:width, cols])
            units[:, cols] = jnp.maximum(a, 0.0).astype(BF)
            return carry

        lax.fori_loop(0, hidden_units // tile, first, 0)

        def second(base, target):
            def step(j, carry):
                cols = pl.ds(pl.multiple_of(base + j * tile, tile), tile)
                target[k, :, pl.ds(pl.multiple_of(j * tile, tile), tile)] = bdot(
                    units[...], w_out[:, cols]
                ).astype(BF)
                return carry

            lax.fori_loop(0, half // tile, step, 0)

        second((1 - core) * half, p_send)
        copy = send(p_send.at[k], p_back.at[k], part_s.at[k], part_r.at[k], sibling)
        second(core * half, p_mine)
        return copy

    def reduce_part(k, g):
        return p_mine[k, piece(g), :].astype(F32) + p_back[k, piece(g), :].astype(F32)

    sib = {}
    near = {}
    for g in range(4):
        for o in range(g * per_group, (g + 1) * per_group):
            if o:
                arrivals[o].wait_recv()
        near[1, g] = send(xbuf.at[core, 0, piece(g)], xbuf.at[core, 1, piece(g)], near_s.at[0, g], near_r.at[0, g], up_y)
        near[2, g] = send(xbuf.at[core, 0, piece(g)], xbuf.at[core, 2, piece(g)], near_s.at[1, g], near_r.at[1, g], down_y)
        sib[0, g] = to_sibling(0, g)
    loads[3].wait()
    loads[4].wait()
    for g in range(4):
        sib[0, g].wait_recv()
    parts = [compute(0)]
    far = []
    for g in range(4):
        for k in (1, 2):
            near[k, g].wait_recv()
            if (k == 1) == (g < 2):
                far.append(send(
                    xbuf.at[core, k, piece(g)], xbuf.at[core, 3, piece(g)], fwd_s.at[g], fwd_r.at[g],
                    up_y if k == 1 else down_y,
                ))
            sib[k, g] = to_sibling(k, g)
    for k in (1, 2):
        for g in range(4):
            sib[k, g].wait_recv()
        parts.append(compute(k))
    for g in range(4):
        far[g].wait_recv()
        sib[3, g] = to_sibling(3, g)

    final = {}

    def finish_near(k, g, extra=None):
        value = reduce_part(k, g)
        if extra is not None:
            value += extra.astype(F32)
        p_send[k, piece(g), :] = value.astype(BF)
        final[k, g] = send(
            p_send.at[k, piece(g)], (fin_b if k == 1 else fin_a).at[piece(g)],
            fin_s.at[k - 1, g], fin_r.at[k - 1, g], down_y if k == 1 else up_y,
        )

    parts[0].wait()
    parts[1].wait()
    parts[2].wait()
    for g in range(4):
        finish_near(1 if g < 2 else 2, g)
    home[...] = p_mine[0].astype(F32) + p_back[0].astype(F32)
    for g in range(4):
        sib[3, g].wait_recv()
    parts.append(compute(3))
    parts[3].wait()
    relay = []
    for g in range(4):
        p_send[3, piece(g), :] = reduce_part(3, g).astype(BF)
        relay.append(send(
            p_send.at[3, piece(g)], (rs_a if g < 2 else rs_b).at[pl.ds((g % 2) * group, group)],
            rs_s.at[g], rs_r.at[g], up_y if g < 2 else down_y,
        ))
    for g in (0, 2, 1, 3):
        relay[g].wait_recv()
        source = rs_a if g < 2 else rs_b
        finish_near(2 if g < 2 else 1, g, source[pl.ds((g % 2) * group, group), :])
    replies = [None] * n_ex
    for g in (2, 3, 0, 1):
        final[1, g].wait_recv()
        final[2, g].wait_recv()
        total = home[piece(g), :] + fin_a[piece(g), :].astype(F32) + fin_b[piece(g), :].astype(F32)
        outgoing_rows = total.astype(BF)
        p_mine[0, piece(g), :] = outgoing_rows
        for o in range(g * per_group, (g + 1) * per_group):
            if o:
                replies[o] = send(
                    p_mine.at[0, block(o)], returned.at[block(o)], ret_s.at[o], ret_r.at[o], peer_back(o)
                )
    returned[block(0), :] = p_mine[0, block(0), :]
    for o in range(1, n_ex):
        replies[o].wait_recv()
    mix = []
    for c in range(2):
        high = gates[c].astype(BF)
        low = (gates[c] - high.astype(F32)).astype(BF)
        mix.append((high, low))

    back = returned[...]
    ys = [bdot(high, back) + bdot(low, back) for high, low in mix]
    is_first = core == 0
    y_send[...] = jnp.where(is_first, ys[1], ys[0])
    swap = send(y_send, y_back, pair_s.at[2], pair_r.at[2], sibling)
    own_y = jnp.where(is_first, ys[0], ys[1])
    loads[5].wait()
    residual[:, at_half] = residual[:, at_half] + own_y
    swap.wait_recv()
    at_other = pl.ds(pl.multiple_of((1 - core) * half, half), half)
    residual[:, at_other] = residual[:, at_other] + y_back[...]
    for t in range(steps):
        out_ref[t] = residual[t * rows:(t + 1) * rows, :].astype(BF)
    parts_done = {id(p) for p in parts}
    for copy in started:
        if id(copy) not in parts_done:
            copy.wait_send()


def experts(residual, normed, expert_ids, router, w_in, w_out):
    steps, rows, width = residual.shape
    n_dp, n_ex = lax.axis_size("dp"), lax.axis_size("expert")
    tokens = steps * rows
    hidden_units = w_in.shape[2]
    half = width // 2
    cap = 4 * rows // n_ex
    slots = 2 * steps * cap
    chunk = n_ex * slots
    vmem = pl.BlockSpec(memory_space=pltpu.VMEM)
    hbm = pl.BlockSpec(memory_space=pl.ANY)
    dma = pltpu.SemaphoreType.DMA
    return pl.pallas_call(
        functools.partial(experts_kernel, n_dp, n_ex, cap),
        out_shape=jax.ShapeDtypeStruct((steps, rows, width), BF),
        in_specs=[hbm] * 6,
        out_specs=vmem,
        scratch_shapes=[
            pltpu.VMEM((tokens, width), F32),
            pltpu.VMEM((2 * tokens, width), BF),
            pltpu.VMEM((steps, 2, rows), jnp.int32),
            pltpu.VMEM((2, tokens, 128), jnp.int32),
            pltpu.VMEM((n_ex, width), BF),
            pltpu.VMEM((width, hidden_units), BF),
            pltpu.VMEM((hidden_units, width), BF),
            pltpu.VMEM((chunk, half), BF),
            pltpu.VMEM((2, 4, chunk, half), BF),
            pltpu.VMEM((chunk, hidden_units), BF),
            pltpu.VMEM((4, chunk, half), BF),
            pltpu.VMEM((4, chunk, half), BF),
            pltpu.VMEM((4, chunk, half), BF),
            pltpu.VMEM((chunk // 2, half), BF),
            pltpu.VMEM((chunk // 2, half), BF),
            pltpu.VMEM((chunk, half), BF),
            pltpu.VMEM((chunk, half), BF),
            pltpu.VMEM((chunk, half), F32),
            pltpu.VMEM((chunk, half), BF),
            pltpu.VMEM((tokens, half), F32),
            pltpu.VMEM((tokens, half), F32),
            dma((6,)), dma((3,)), dma((3,)), dma((n_ex,)), dma((n_ex,)), dma((2, 4)), dma((2, 4)),
            dma((4,)), dma((4,)), dma((4, 4)), dma((4, 4)), dma((4,)), dma((4,)),
            dma((4,)), dma((4,)), dma((2, 4)), dma((2, 4)), dma((n_ex,)), dma((n_ex,)),
        ],
        compiler_params=pltpu.CompilerParams(
            collective_id=1, has_side_effects=True, vmem_limit_bytes=60 * 2**20
        ),
    )(
        residual.reshape(tokens, width), normed.reshape(tokens, width), jnp.swapaxes(expert_ids, 1, 2), router.T,
        w_in.reshape(width, hidden_units), w_out.reshape(hidden_units, width),
    )


def shards(
    hidden, q_self, k_new, v_new, q_cross, cache_keys, cache_values, cross_keys, cross_values,
    key_scale, value_scale, parents, expert_ids, norm_gain, router, w_in, w_out,
):
    residual, normed = attention(
        hidden, q_self, k_new, v_new, q_cross, cache_keys, cache_values, cross_keys, cross_values,
        key_scale, value_scale, parents, norm_gain,
    )
    return experts(residual, normed, expert_ids, router, w_in, w_out)


def solution(mesh):
    in_specs = (
        P(None, ("dp", "expert"), None),
        P(None, ("dp", "expert"), None),
        P(None, ("dp", "expert"), None),
        P(None, ("dp", "expert"), None),
        P(None, ("dp", "expert"), None),
        P(("dp", "expert"), None, None),
        P(("dp", "expert"), None, None),
        P(("dp", "expert"), None, None),
        P(("dp", "expert"), None, None),
        P(("dp", "expert"), None),
        P(("dp", "expert"), None),
        P(None, ("dp", "expert")),
        P(None, ("dp", "expert"), None),
        P(),
        P(),
        P("expert", None, "dp"),
        P("expert", "dp", None),
    )
    out_specs = P(None, ("dp", "expert"), None)
    return jax.shard_map(shards, mesh=mesh, in_specs=in_specs, out_specs=out_specs, check_vma=False)
```

```python
import functools
import math

import jax
import jax.numpy as jnp
from jax import lax
from jax.experimental import pallas as pl
from jax.experimental.pallas import tpu as pltpu
from jax.sharding import PartitionSpec as P

epsilon = 1e-05
MESH = pl.DeviceIdType.MESH
BF = jnp.bfloat16
F32 = jnp.float32
LOW = -1e30
FLOOR = -1e20


def iota(shape, dim):
    return lax.broadcasted_iota(jnp.int32, shape, dim)


def as_column(row, n):
    return jnp.sum(jnp.where(iota((n, n), 0) == iota((n, n), 1), row, 0.0), axis=1, keepdims=True)


def pick(row, index_col, n):
    lanes = iota((n, n), 1).astype(F32)
    return jnp.sum(jnp.where(lanes == index_col, row, 0.0), axis=1, keepdims=True)


def inside(value, start, n):
    return (value >= start) & (value < start + n)


def remote_rank(row, start, n):
    far = jnp.where(inside(row, start, n), 0.0, 1.0)
    far_col = as_column(far, n)
    rank = jnp.sum(jnp.where(iota((n, n), 0) < iota((n, n), 1), far_col, 0.0), axis=0, keepdims=True)
    return far, rank


def bdot(a, b):
    return lax.dot_general(a, b, (((1,), (0,)), ((), ())), preferred_element_type=F32)


def tdot(a, b):
    return lax.dot_general(a, b, (((1,), (1,)), ((), ())), preferred_element_type=F32)


def attention_part(n_dp, n_ex, rows, cache, src, beams, chunks, inputs, scratch, residual, normed, first_row, enter):
    (
        hidden_hbm, q_self_hbm, k_new_hbm, v_new_hbm, q_cross_hbm, parents_hbm, ks_hbm, vs_hbm, gain_hbm,
        ck_hbm, cv_hbm, xk_hbm, xv_hbm,
    ) = inputs
    (
    hidden, q_self, k_new, v_new, q_cross, parents, key_scale, value_scale, gain,
    kbuf, vbuf, xkbuf, xvbuf, q_all, o_all, o_send, x_out, bias, bias_e, bias_x, scales,
    stat, par_own, par_in, q_d, q_e, in_c, in_d, in_e, o_d, o_e, back_c, back_d, back_e, stat_in, stat_in2,
    s_self, w_self, s_cross, w_cross, load_sem, small_sem, send_sem, recv_sem,
    ) = scratch
    width = hidden.shape[2]
    heads = key_scale.shape[1]
    size = width // heads
    per_chunk = heads // chunks
    quarter = width // 4
    n_dev = n_dp * n_ex
    me = lax.axis_index("dp") * n_ex + lax.axis_index("expert")

    def at(offset):
        other = lax.rem(me + offset + n_dev, n_dev)
        return (other // n_ex, lax.rem(other, n_ex))

    def load(k, c, source, buffer):
        part = width // chunks
        return pltpu.make_async_copy(
            source.at[:, pl.ds(pl.multiple_of(c * part, part), part)], buffer.at[c], load_sem.at[k, c]
        )

    small = [
        pltpu.make_async_copy(source, target, small_sem.at[i])
        for i, (source, target) in enumerate((
            (parents_hbm, parents), (q_self_hbm, q_self), (k_new_hbm, k_new), (v_new_hbm, v_new),
            (ks_hbm, key_scale), (vs_hbm, value_scale), (q_cross_hbm, q_cross), (hidden_hbm, hidden),
            (gain_hbm, gain),
        ))
    ]
    for copy in small:
        copy.start()
    early = chunks // 2
    for c in range(early):
        load(2, c, xk_hbm, xkbuf).start()
        load(3, c, xv_hbm, xvbuf).start()
    for c in range(chunks):
        load(0, c, ck_hbm, kbuf).start()
        load(1, c, cv_hbm, vbuf).start()
    for c in range(early, chunks):
        load(2, c, xk_hbm, xkbuf).start()
        load(3, c, xv_hbm, xvbuf).start()

    par_own[...] = jnp.zeros_like(par_own)
    small[0].wait()
    small[1].wait()
    par_own[0:2, 0:rows] = parents[...]
    own = (me * rows).astype(F32)
    after = (lax.rem(me + 1, n_dev) * rows).astype(F32)
    after2 = (lax.rem(me + 2, n_dev) * rows).astype(F32)
    p0 = parents[0:1, :].astype(F32)
    p1 = parents[1:2, :].astype(F32)
    far0, rank0 = remote_rank(p0, own, rows)
    far1, rank1 = remote_rank(p1, own, rows)
    far0_col, rank0_col = as_column(far0, rows), as_column(rank0, rows)
    far1_col, rank1_col = as_column(far1, rows), as_column(rank1, rows)
    sub = iota((16, rows), 0)
    lane = iota((rows, 16), 1)

    def compact(value, far, rank):
        total = jnp.zeros((16, quarter), F32)
        for k in range(4):
            hot = ((sub >> 2) == k) & ((sub & 3).astype(F32) == rank) & (far > 0.5)
            total += bdot(jnp.where(hot, 1.0, 0.0).astype(BF), value[:, k * quarter:(k + 1) * quarter])
        return total.astype(BF)

    q_d[...] = compact(q_self[0], far0, rank0)
    q_e[...] = compact(q_self[1], far1, rank1)

    def remote(source, target, number, offset):
        return pltpu.make_async_remote_copy(
            src_ref=source, dst_ref=target, send_sem=send_sem.at[number], recv_sem=recv_sem.at[number],
            device_id=at(offset), device_id_type=MESH,
        )

    out_copies = [
        remote(par_own, par_in.at[0], 0, -1),
        remote(par_own, par_in.at[1], 1, -2),
        remote(q_d, in_d, 2, -1),
        remote(q_e, in_e, 3, -2),
        remote(q_self.at[1], in_c, 4, -1),
    ]
    enter()
    for copy in out_copies:
        copy.start()

    small[4].wait()
    small[5].wait()
    sentence = (iota((2 * rows, 1), 0) & (rows - 1)) // beams
    ks = jnp.zeros((2 * rows, heads), F32)
    vs = jnp.zeros((2 * rows, heads), F32)
    for s in range(rows // beams):
        ks = jnp.where(sentence == s, key_scale[s:s + 1, :], ks)
        vs = jnp.where(sentence == s, value_scale[s:s + 1, :], vs)
    root = 1.0 / math.sqrt(size)
    scales[0, :, 0:heads] = ks * root
    scales[1, :, 0:heads] = vs
    n_cross = (rows // beams) * src
    bias_x[...] = jnp.where(
        iota((2 * rows, n_cross), 1) // src == (iota((2 * rows, n_cross), 0) & (rows - 1)) // beams, 0.0, LOW
    )
    def cross_chunk(c, carry):
        load(2, c, xk_hbm, xkbuf).wait()
        load(3, c, xv_hbm, xvbuf).wait()
        lanes_x = iota((2 * rows, 128), 1)
        heads_at = [pl.ds(pl.multiple_of((c * per_chunk + j) * size, size), size) for j in range(per_chunk)]
        for j in range(per_chunk):
            ks_h = jnp.sum(jnp.where(lanes_x == c * per_chunk + j, scales[0], 0.0), axis=1, keepdims=True)
            q = jnp.concatenate([q_cross[0, :, heads_at[j]], q_cross[1, :, heads_at[j]]], axis=0)
            s_cross[j] = tdot(q, xkbuf[c, :, j * size:(j + 1) * size]) * ks_h + bias_x[...]
        totals = []
        for j in range(per_chunk):
            s = s_cross[j]
            w = jnp.exp(s - jnp.max(s, axis=1, keepdims=True))
            totals.append(jnp.sum(w, axis=1, keepdims=True))
            w_cross[j] = w.astype(BF)
        for j in range(per_chunk):
            vs_h = jnp.sum(jnp.where(lanes_x == c * per_chunk + j, scales[1], 0.0), axis=1, keepdims=True)
            o = bdot(w_cross[j], xvbuf[c, :, j * size:(j + 1) * size])
            x_out[:, heads_at[j]] = o * (vs_h / totals[j])
        return carry

    small[6].wait()
    lax.fori_loop(0, early, cross_chunk, 0)
    q_all[0:rows, :] = q_self[0]
    q_all[rows:2 * rows, :] = q_self[1]

    for i in (2, 3, 7, 8):
        small[i].wait()
    for copy in out_copies:
        copy.wait()
    q_all[2 * rows:3 * rows, :] = in_c[...]
    a16, b16 = iota((16, 16), 0), iota((16, 16), 1)
    for k in range(4):
        take_d = jnp.where((b16 == a16 + 4 * k) & (a16 < 4), 1.0, 0.0).astype(BF)
        take_e = jnp.where((b16 == a16 - 4 + 4 * k) & (a16 >= 4) & (a16 < 8), 1.0, 0.0).astype(BF)
        q_all[3 * rows:4 * rows, k * quarter:(k + 1) * quarter] = (
            bdot(take_d, in_d[...]) + bdot(take_e, in_e[...])
        ).astype(BF)

    n0 = par_in[0, 0:1, 0:rows].astype(F32)
    n1 = par_in[0, 1:2, 0:rows].astype(F32)
    m1 = par_in[1, 1:2, 0:rows].astype(F32)
    p0_col, p1_col = as_column(p0, rows), as_column(p1, rows)
    n1_col = as_column(n1, rows)
    index = iota((rows, 1), 0).astype(F32)
    none = jnp.full((rows, 1), -1000.0, F32)

    def local(value):
        return jnp.where(inside(value, own, rows), value - own, -1.0)

    own_b = p1_col - own
    in_own = inside(p1_col, own, rows)
    row_b = jnp.where(in_own, local(pick(p0, own_b, rows)), -1.0)
    first_b = jnp.where(in_own, own_b, -1.0)
    in_next = inside(n1_col, after, rows)
    in_here = inside(n1_col, own, rows)
    row_c = jnp.where(
        in_next,
        local(pick(n0, n1_col - after, rows)),
        jnp.where(in_here, local(pick(p0, n1_col - own, rows)), -1.0),
    )
    first_c = jnp.where(in_here & jnp.logical_not(in_next), n1_col - own, -1.0)
    far_n, rank_n = remote_rank(n0, after, rows)
    far_m, rank_m = remote_rank(m1, after2, rows)
    i_col = iota((rows, rows), 0).astype(F32)
    val_d = jnp.sum(jnp.where((rank_n == i_col) & (far_n > 0.5), n0, 0.0), axis=1, keepdims=True)
    val_e = jnp.sum(jnp.where((rank_m == i_col - 4.0) & (far_m > 0.5), m1, 0.0), axis=1, keepdims=True)
    row_de = jnp.where(
        index < 4.0,
        local(val_d),
        jnp.where(
            (index < 8.0) & inside(val_e, after, rows), local(pick(n0, val_e - after, rows)), -1.0
        ),
    )
    row_sel = jnp.concatenate([local(p0_col), row_b, row_c, row_de], axis=0)
    first_sel = jnp.concatenate([index, first_b, first_c, none], axis=0)
    second_sel = jnp.concatenate([none, index, none, none], axis=0)
    slots = 4 * rows
    bias[...] = jnp.where((iota((slots, rows * cache), 1) // cache).astype(F32) == row_sel, 0.0, LOW)
    lane_e = iota((slots, 2 * rows), 1).astype(F32)
    bias_e[...] = jnp.where((lane_e == first_sel) | (lane_e - rows == second_sel), 0.0, LOW)

    stat[...] = jnp.zeros_like(stat)
    lanes = iota((slots, 128), 1)

    def self_chunk(c, carry):
        load(0, c, ck_hbm, kbuf).wait()
        load(1, c, cv_hbm, vbuf).wait()
        heads_at = [pl.ds(pl.multiple_of((c * per_chunk + j) * size, size), size) for j in range(per_chunk)]
        extras = []
        for j in range(per_chunk):
            q = q_all[:, heads_at[j]]
            k_extra = jnp.concatenate([k_new[0, :, heads_at[j]], k_new[1, :, heads_at[j]]], axis=0)
            s_self[j] = tdot(q, kbuf[c, :, j * size:(j + 1) * size]) * root + bias[...]
            extras.append(tdot(q, k_extra) * root + bias_e[...])
        for j in range(per_chunk):
            s, s_e = s_self[j], extras[j]
            top = jnp.maximum(
                jnp.maximum(jnp.max(s, axis=1, keepdims=True), jnp.max(s_e, axis=1, keepdims=True)), FLOOR
            )
            w = jnp.exp(s - top)
            w_e = jnp.exp(s_e - top)
            total = jnp.sum(w, axis=1, keepdims=True) + jnp.sum(w_e, axis=1, keepdims=True)
            w_self[j] = w.astype(BF)
            extras[j] = w_e.astype(BF)
            here = lanes == c * per_chunk + j
            stat[0] = jnp.where(here, top, stat[0])
            stat[1] = jnp.where(here, total, stat[1])
        for j in range(per_chunk):
            v_extra = jnp.concatenate([v_new[0, :, heads_at[j]], v_new[1, :, heads_at[j]]], axis=0)
            o_all[:, heads_at[j]] = bdot(w_self[j], vbuf[c, :, j * size:(j + 1) * size]) + bdot(
                extras[j], v_extra
            )
        return carry

    lax.fori_loop(0, chunks, self_chunk, 0)

    o_send[...] = o_all[2 * rows:4 * rows, :].astype(BF)
    total_d = jnp.zeros((16, quarter), F32)
    total_e = jnp.zeros((16, quarter), F32)
    for k in range(4):
        piece = o_send[rows:2 * rows, k * quarter:(k + 1) * quarter]
        put_d = jnp.where(((a16 >> 2) == k) & (b16 == (a16 & 3)), 1.0, 0.0).astype(BF)
        put_e = jnp.where(((a16 >> 2) == k) & (b16 == (a16 & 3) + 4), 1.0, 0.0).astype(BF)
        total_d += bdot(put_d, piece)
        total_e += bdot(put_e, piece)
    o_d[...] = total_d.astype(BF)
    o_e[...] = total_e.astype(BF)
    back_copies = [
        remote(o_send.at[pl.ds(0, rows)], back_c, 5, 1),
        remote(o_d, back_d, 6, 1),
        remote(o_e, back_e, 7, 2),
        remote(stat.at[:, pl.ds(2 * rows, rows + 8)], stat_in, 8, 1),
        remote(stat.at[:, pl.ds(3 * rows, 8)], stat_in2, 9, 2),
    ]
    for copy in back_copies:
        copy.start()

    lax.fori_loop(early, chunks, cross_chunk, 0)

    for copy in back_copies:
        copy.wait()

    def spread(compact_ref, far_col, rank_col):
        pieces = []
        for k in range(4):
            hot = ((lane >> 2) == k) & ((lane & 3).astype(F32) == rank_col) & (far_col > 0.5)
            pieces.append(bdot(jnp.where(hot, 1.0, 0.0).astype(BF), compact_ref[...]))
        return pieces

    def spread_stat(ref, start, far_col, rank_col):
        top = jnp.where(far_col > 0.5, 0.0, FLOOR) + jnp.zeros((rows, 128), F32)
        total = jnp.zeros((rows, 128), F32)
        for j in range(4):
            hot = (rank_col == float(j)) & (far_col > 0.5)
            top += jnp.where(hot, ref[0, start + j:start + j + 1, :], 0.0)
            total += jnp.where(hot, ref[1, start + j:start + j + 1, :], 0.0)
        return top, total

    o_far0 = spread(back_d, far0_col, rank0_col)
    o_far1 = spread(back_e, far1_col, rank1_col)
    stats0 = [
        (stat[0, 0:rows, :], stat[1, 0:rows, :]),
        spread_stat(stat_in, rows, far0_col, rank0_col),
    ]
    stats1 = [
        (stat[0, rows:2 * rows, :], stat[1, rows:2 * rows, :]),
        (stat_in[0, 0:rows, :], stat_in[1, 0:rows, :]),
        spread_stat(stat_in2, 4, far1_col, rank1_col),
    ]

    def weights(stats):
        top = stats[0][0]
        for t, _ in stats[1:]:
            top = jnp.maximum(top, t)
        parts = [jnp.exp(t - top) for t, _ in stats]
        total = sum(w * l for w, (_, l) in zip(parts, stats))
        return [w / total for w in parts]

    w0 = weights(stats0)
    w1 = weights(stats1)
    per_quarter = heads // 4
    for t in range(2):
        for h in range(heads):
            at_h = slice(h * size, (h + 1) * size)
            k, j = h // per_quarter, h % per_quarter
            inner = slice(j * size, (j + 1) * size)
            if t == 0:
                mixed = o_all[0:rows, at_h] * w0[0][:, h:h + 1] + o_far0[k][:, inner] * w0[1][:, h:h + 1]
            else:
                mixed = (
                    o_all[rows:2 * rows, at_h] * w1[0][:, h:h + 1]
                    + back_c[:, at_h].astype(F32) * w1[1][:, h:h + 1]
                    + o_far1[k][:, inner] * w1[2][:, h:h + 1]
                )
            residual[t * rows:(t + 1) * rows, at_h] = (
                hidden[t, :, at_h].astype(F32) + mixed + x_out[t * rows:(t + 1) * rows, at_h]
            )
    value = residual[...]
    average = jnp.mean(value, axis=1, keepdims=True)
    centered = value - average
    variance = jnp.mean(centered * centered, axis=1, keepdims=True)
    normed[first_row, :] = (centered * lax.rsqrt(variance + epsilon) * gain[...]).astype(BF)


def layer_kernel(
    n_dp, n_ex, cap,
    inputs, attention_args, scratch, out_ref,
):
    ids_hbm, router_hbm, w_in_hbm, w_out_hbm = inputs
    (
    residual, normed, ids, ids_all, router, w_in, w_out, outgoing, xbuf, units, p_mine, p_send, p_back,
    rs_a, rs_b, fin_a, fin_b, home, returned, y_send, y_back,
    load_sem, pair_s, pair_r, a2a_s, a2a_r, near_s, near_r, fwd_s, fwd_r, sib_s, sib_r, part_s, part_r,
    rs_s, rs_r, fin_s, fin_r, ret_s, ret_r,
    ) = scratch
    steps, rows = ids.shape[0], ids.shape[2]
    tokens = steps * rows
    width = residual.shape[1]
    half = width // 2
    hidden_units = w_in.shape[1]
    slots = 2 * steps * cap
    chunk = n_ex * slots
    group = chunk // 4
    dp = lax.axis_index("dp")
    me = lax.axis_index("expert")
    core = lax.rem(dp, 2)
    n_y = n_dp // 2
    place = dp // 2
    sibling = (dp + 1 - 2 * core, me)
    up_y = (lax.rem(place + 1, n_y) * 2 + core, me)
    down_y = (lax.rem(place + n_y - 1, n_y) * 2 + core, me)

    def peer(o):
        return (dp, lax.rem(me + o, n_ex))

    def peer_back(o):
        return (dp, lax.rem(me - o + n_ex, n_ex))

    barrier = pltpu.get_barrier_semaphore()
    position = dp * n_ex + me

    def along(offset):
        other = lax.rem(position + offset + n_dp * n_ex, n_dp * n_ex)
        return (other // n_ex, lax.rem(other, n_ex))

    others = [sibling, up_y, down_y] + [peer(o) for o in range(1, n_ex)] + [along(o) for o in (-1, -2, 1, 2)]
    for other in others:
        pl.semaphore_signal(barrier, inc=1, device_id=other, device_id_type=MESH)

    mine = pl.ds(pl.multiple_of(core * tokens, tokens), tokens)
    theirs = pl.ds(pl.multiple_of((1 - core) * tokens, tokens), tokens)
    loads = [
        pltpu.make_async_copy(ids_hbm, ids, load_sem.at[0]),
        pltpu.make_async_copy(router_hbm, router, load_sem.at[1]),
        pltpu.make_async_copy(w_in_hbm, w_in, load_sem.at[2]),
        pltpu.make_async_copy(w_out_hbm, w_out, load_sem.at[3]),
    ]

    def enter():
        for copy in loads:
            copy.start()
        pl.semaphore_wait(barrier, len(others))

    attention_part(n_dp, n_ex, *attention_args, residual, normed, mine, enter)

    started = []

    def send(source, target, s_sem, r_sem, device):
        copy = pltpu.make_async_remote_copy(
            src_ref=source, dst_ref=target, send_sem=s_sem, recv_sem=r_sem,
            device_id=device, device_id_type=MESH,
        )
        copy.start()
        started.append(copy)
        return copy

    loads[0].wait()
    for t in range(steps):
        named = [as_column(ids[t, k:k + 1, :].astype(F32), rows).astype(jnp.int32) for k in range(2)]
        ids_all[core, t * rows:(t + 1) * rows, :] = jnp.where(iota((rows, 128), 1) == 0, named[0], named[1])
    pair = [
        send(normed.at[mine], normed.at[mine], pair_s.at[0], pair_r.at[0], sibling),
        send(ids_all.at[core], ids_all.at[core], pair_s.at[1], pair_r.at[1], sibling),
    ]
    for copy in pair:
        copy.wait_recv()

    lane_x = iota((tokens, 128), 1)
    lower = (iota((tokens, tokens), 1) < iota((tokens, tokens), 0)) & (
        iota((tokens, tokens), 0) // rows == iota((tokens, tokens), 1) // rows
    )
    lower = jnp.where(lower, 1.0, 0.0).astype(BF)
    step_of = (iota((tokens, 1), 0) // rows)
    hots = []
    for c in range(2):
        named = [ids_all[c, :, k:k + 1] for k in range(2)]
        one_hot = [lane_x == n for n in named]
        count = jnp.where(one_hot[0] | one_hot[1], 1.0, 0.0).astype(BF)
        before = bdot(lower, count)
        pair_hot = []
        for k in range(2):
            spot = jnp.sum(jnp.where(one_hot[k], before, 0.0), axis=1, keepdims=True).astype(jnp.int32)
            distance = named[k] - me
            distance = jnp.where(distance < 0, distance + n_ex, distance)
            column = distance * slots + (c * steps * cap + spot) + step_of * cap
            pair_hot.append(iota((tokens, chunk), 1) == column)
        hots.append(pair_hot)
    dispatch = jnp.concatenate([jnp.where(h[0] | h[1], 1.0, 0.0).astype(BF) for h in hots], axis=0)
    at_half = pl.ds(pl.multiple_of(core * half, half), half)
    outgoing[...] = lax.dot_general(
        dispatch, normed[:, at_half], (((0,), (0,)), ((), ())), preferred_element_type=F32
    ).astype(BF)

    def block(o):
        return pl.ds(o * slots, slots)

    arrivals = [None]
    for o in range(1, n_ex):
        arrivals.append(
            send(outgoing.at[block(o)], xbuf.at[core, 0, block(o)], a2a_s.at[o], a2a_r.at[o], peer(o))
        )
    xbuf[core, 0, block(0), :] = outgoing[block(0), :]

    loads[1].wait()
    logits = tdot(normed[...], router[...])
    lane_e = iota((tokens, n_ex), 1)
    gates = []
    for c in range(2):
        part = logits[c * tokens:(c + 1) * tokens]
        picked = [
            jnp.sum(jnp.where(lane_e == ids_all[c, :, k:k + 1], part, 0.0), axis=1, keepdims=True)
            for k in range(2)
        ]
        first = 1.0 / (1.0 + jnp.exp(picked[1] - picked[0]))
        gates.append(
            jnp.where(hots[c][0], first, 0.0) + jnp.where(hots[c][1], 1.0 - first, 0.0)
        )

    def piece(g):
        return pl.ds(g * group, group)

    per_group = n_ex // 4

    def to_sibling(k, g):
        return send(
            xbuf.at[core, k, piece(g)], xbuf.at[core, k, piece(g)], sib_s.at[k, g], sib_r.at[k, g], sibling
        )

    tile = min(256, half, hidden_units)

    def compute(k):
        def first(j, carry):
            cols = pl.ds(pl.multiple_of(j * tile, tile), tile)
            a = bdot(xbuf[0, k], w_in[0:half, cols]) + bdot(xbuf[1, k], w_in[half:width, cols])
            units[:, cols] = jnp.maximum(a, 0.0).astype(BF)
            return carry

        lax.fori_loop(0, hidden_units // tile, first, 0)

        def second(base, target):
            def step(j, carry):
                cols = pl.ds(pl.multiple_of(base + j * tile, tile), tile)
                target[k, :, pl.ds(pl.multiple_of(j * tile, tile), tile)] = bdot(
                    units[...], w_out[:, cols]
                ).astype(BF)
                return carry

            lax.fori_loop(0, half // tile, step, 0)

        second((1 - core) * half, p_send)
        copy = send(p_send.at[k], p_back.at[k], part_s.at[k], part_r.at[k], sibling)
        second(core * half, p_mine)
        return copy

    def reduce_part(k, g):
        return p_mine[k, piece(g), :].astype(F32) + p_back[k, piece(g), :].astype(F32)

    sib = {}
    near = {}
    for g in range(4):
        for o in range(g * per_group, (g + 1) * per_group):
            if o:
                arrivals[o].wait_recv()
        near[1, g] = send(xbuf.at[core, 0, piece(g)], xbuf.at[core, 1, piece(g)], near_s.at[0, g], near_r.at[0, g], up_y)
        near[2, g] = send(xbuf.at[core, 0, piece(g)], xbuf.at[core, 2, piece(g)], near_s.at[1, g], near_r.at[1, g], down_y)
        sib[0, g] = to_sibling(0, g)
    loads[2].wait()
    loads[3].wait()
    for g in range(4):
        sib[0, g].wait_recv()
    parts = [compute(0)]
    far = []
    for g in range(4):
        for k in (1, 2):
            near[k, g].wait_recv()
            if (k == 1) == (g < 2):
                far.append(send(
                    xbuf.at[core, k, piece(g)], xbuf.at[core, 3, piece(g)], fwd_s.at[g], fwd_r.at[g],
                    up_y if k == 1 else down_y,
                ))
            sib[k, g] = to_sibling(k, g)
    for k in (1, 2):
        for g in range(4):
            sib[k, g].wait_recv()
        parts.append(compute(k))
    for g in range(4):
        far[g].wait_recv()
        sib[3, g] = to_sibling(3, g)

    final = {}

    def finish_near(k, g, extra=None):
        value = reduce_part(k, g)
        if extra is not None:
            value += extra.astype(F32)
        p_send[k, piece(g), :] = value.astype(BF)
        final[k, g] = send(
            p_send.at[k, piece(g)], (fin_b if k == 1 else fin_a).at[piece(g)],
            fin_s.at[k - 1, g], fin_r.at[k - 1, g], down_y if k == 1 else up_y,
        )

    parts[0].wait()
    parts[1].wait()
    parts[2].wait()
    for g in range(4):
        finish_near(1 if g < 2 else 2, g)
    home[...] = p_mine[0].astype(F32) + p_back[0].astype(F32)
    for g in range(4):
        sib[3, g].wait_recv()
    parts.append(compute(3))
    parts[3].wait()
    relay = []
    for g in range(4):
        p_send[3, piece(g), :] = reduce_part(3, g).astype(BF)
        relay.append(send(
            p_send.at[3, piece(g)], (rs_a if g < 2 else rs_b).at[pl.ds((g % 2) * group, group)],
            rs_s.at[g], rs_r.at[g], up_y if g < 2 else down_y,
        ))
    for g in (0, 2, 1, 3):
        relay[g].wait_recv()
        source = rs_a if g < 2 else rs_b
        finish_near(2 if g < 2 else 1, g, source[pl.ds((g % 2) * group, group), :])
    replies = [None] * n_ex
    for g in (2, 3, 0, 1):
        final[1, g].wait_recv()
        final[2, g].wait_recv()
        total = home[piece(g), :] + fin_a[piece(g), :].astype(F32) + fin_b[piece(g), :].astype(F32)
        outgoing_rows = total.astype(BF)
        p_mine[0, piece(g), :] = outgoing_rows
        for o in range(g * per_group, (g + 1) * per_group):
            if o:
                replies[o] = send(
                    p_mine.at[0, block(o)], returned.at[block(o)], ret_s.at[o], ret_r.at[o], peer_back(o)
                )
    returned[block(0), :] = p_mine[0, block(0), :]
    for o in range(1, n_ex):
        replies[o].wait_recv()
    mix = []
    for c in range(2):
        high = gates[c].astype(BF)
        low = (gates[c] - high.astype(F32)).astype(BF)
        mix.append((high, low))

    back = returned[...]
    ys = [bdot(high, back) + bdot(low, back) for high, low in mix]
    is_first = core == 0
    y_send[...] = jnp.where(is_first, ys[1], ys[0])
    swap = send(y_send, y_back, pair_s.at[2], pair_r.at[2], sibling)
    own_y = jnp.where(is_first, ys[0], ys[1])
    residual[:, at_half] = residual[:, at_half] + own_y
    swap.wait_recv()
    at_other = pl.ds(pl.multiple_of((1 - core) * half, half), half)
    residual[:, at_other] = residual[:, at_other] + y_back[...]
    for t in range(steps):
        out_ref[t] = residual[t * rows:(t + 1) * rows, :].astype(BF)
    parts_done = {id(p) for p in parts}
    for copy in started:
        if id(copy) not in parts_done:
            copy.wait_send()


def layer(hidden, q_self, k_new, v_new, q_cross, cache_keys, cache_values, cross_keys, cross_values,
          key_scale, value_scale, parents, expert_ids, norm_gain, router, w_in, w_out):
    steps, rows, width = hidden.shape
    heads = key_scale.shape[1]
    cache = cache_keys.shape[1]
    sentences, src = cross_keys.shape[:2]
    chunks = 4
    n_dp, n_ex = lax.axis_size("dp"), lax.axis_size("expert")
    part = width // chunks
    n_self, n_cross, slots = rows * cache, sentences * src, 4 * rows
    quarter = width // 4
    tokens = steps * rows
    hidden_units = w_in.shape[2]
    half = width // 2
    cap = 4 * rows // n_ex
    chunk_slots = n_ex * 2 * steps * cap
    dma = pltpu.SemaphoreType.DMA
    attention_scratch = [pltpu.VMEM((steps, rows, width), BF)] * 5 + [
            pltpu.VMEM((steps, rows), jnp.int32),
            pltpu.VMEM((sentences, heads), F32),
            pltpu.VMEM((sentences, heads), F32),
            pltpu.VMEM((1, width), F32),
            pltpu.VMEM((chunks, n_self, part), BF),
            pltpu.VMEM((chunks, n_self, part), BF),
            pltpu.VMEM((chunks, n_cross, part), BF),
            pltpu.VMEM((chunks, n_cross, part), BF),
            pltpu.VMEM((slots, width), BF),
            pltpu.VMEM((slots, width), F32),
            pltpu.VMEM((2 * rows, width), BF),
            pltpu.VMEM((2 * rows, width), F32),
            pltpu.VMEM((slots, n_self), F32),
            pltpu.VMEM((slots, 2 * rows), F32),
            pltpu.VMEM((2 * rows, n_cross), F32),
            pltpu.VMEM((2, 2 * rows, 128), F32),
            pltpu.VMEM((2, slots, 128), F32),
            pltpu.VMEM((8, 128), jnp.int32),
            pltpu.VMEM((2, 8, 128), jnp.int32),
            pltpu.VMEM((16, quarter), BF),
            pltpu.VMEM((16, quarter), BF),
            pltpu.VMEM((rows, width), BF),
            pltpu.VMEM((16, quarter), BF),
            pltpu.VMEM((16, quarter), BF),
            pltpu.VMEM((16, quarter), BF),
            pltpu.VMEM((16, quarter), BF),
            pltpu.VMEM((rows, width), BF),
            pltpu.VMEM((16, quarter), BF),
            pltpu.VMEM((16, quarter), BF),
            pltpu.VMEM((2, rows + 8, 128), F32),
            pltpu.VMEM((2, 8, 128), F32),
            pltpu.VMEM((heads // chunks, slots, n_self), F32),
            pltpu.VMEM((heads // chunks, slots, n_self), BF),
            pltpu.VMEM((heads // chunks, 2 * rows, n_cross), F32),
            pltpu.VMEM((heads // chunks, 2 * rows, n_cross), BF),
            pltpu.SemaphoreType.DMA((4, chunks)),
            pltpu.SemaphoreType.DMA((9,)),
            pltpu.SemaphoreType.DMA((10,)),
            pltpu.SemaphoreType.DMA((10,)),
        ]
    expert_scratch = [
            pltpu.VMEM((tokens, width), F32),
            pltpu.VMEM((2 * tokens, width), BF),
            pltpu.VMEM((steps, 2, rows), jnp.int32),
            pltpu.VMEM((2, tokens, 128), jnp.int32),
            pltpu.VMEM((n_ex, width), BF),
            pltpu.VMEM((width, hidden_units), BF),
            pltpu.VMEM((hidden_units, width), BF),
            pltpu.VMEM((chunk_slots, half), BF),
            pltpu.VMEM((2, 4, chunk_slots, half), BF),
            pltpu.VMEM((chunk_slots, hidden_units), BF),
            pltpu.VMEM((4, chunk_slots, half), BF),
            pltpu.VMEM((4, chunk_slots, half), BF),
            pltpu.VMEM((4, chunk_slots, half), BF),
            pltpu.VMEM((chunk_slots // 2, half), BF),
            pltpu.VMEM((chunk_slots // 2, half), BF),
            pltpu.VMEM((chunk_slots, half), BF),
            pltpu.VMEM((chunk_slots, half), BF),
            pltpu.VMEM((chunk_slots, half), F32),
            pltpu.VMEM((chunk_slots, half), BF),
            pltpu.VMEM((tokens, half), F32),
            pltpu.VMEM((tokens, half), F32),
            dma((4,)), dma((3,)), dma((3,)), dma((n_ex,)), dma((n_ex,)), dma((2, 4)), dma((2, 4)),
            dma((4,)), dma((4,)), dma((4, 4)), dma((4, 4)), dma((4,)), dma((4,)),
            dma((4,)), dma((4,)), dma((2, 4)), dma((2, 4)), dma((n_ex,)), dma((n_ex,)),
        ]
    def kernel(*refs):
        layer_kernel(
            n_dp, n_ex, cap, refs[13:17],
            (rows, cache, src, rows // sentences, chunks, refs[0:13], refs[18]), refs[19], refs[17],
        )

    return pl.pallas_call(
        kernel,
        out_shape=jax.ShapeDtypeStruct((steps, rows, width), BF),
        in_specs=[pl.BlockSpec(memory_space=pl.ANY)] * 17,
        out_specs=pl.BlockSpec(memory_space=pltpu.VMEM),
        scratch_shapes=(tuple(attention_scratch), tuple(expert_scratch)),
        compiler_params=pltpu.CompilerParams(
            collective_id=0, has_side_effects=True, vmem_limit_bytes=60 * 2**20
        ),
    )(
        hidden, q_self, k_new, v_new, q_cross, parents, key_scale, value_scale, norm_gain.reshape(1, width),
        cache_keys.reshape(n_self, width), cache_values.reshape(n_self, width),
        cross_keys.reshape(n_cross, width), cross_values.reshape(n_cross, width),
        jnp.swapaxes(expert_ids, 1, 2), router.T,
        w_in.reshape(width, hidden_units), w_out.reshape(hidden_units, width),
    )


def solution(mesh):
    in_specs = (
        P(None, ("dp", "expert"), None),
        P(None, ("dp", "expert"), None),
        P(None, ("dp", "expert"), None),
        P(None, ("dp", "expert"), None),
        P(None, ("dp", "expert"), None),
        P(("dp", "expert"), None, None),
        P(("dp", "expert"), None, None),
        P(("dp", "expert"), None, None),
        P(("dp", "expert"), None, None),
        P(("dp", "expert"), None),
        P(("dp", "expert"), None),
        P(None, ("dp", "expert")),
        P(None, ("dp", "expert"), None),
        P(),
        P(),
        P("expert", None, "dp"),
        P("expert", "dp", None),
    )
    out_specs = P(None, ("dp", "expert"), None)
    return jax.shard_map(layer, mesh=mesh, in_specs=in_specs, out_specs=out_specs, check_vma=False)
```

```python
import functools
import math

import jax
import jax.numpy as jnp
from jax import lax
from jax.experimental import pallas as pl
from jax.experimental.pallas import tpu as pltpu
from jax.sharding import PartitionSpec as P

epsilon = 1e-05
MESH = pl.DeviceIdType.MESH
BF = jnp.bfloat16
F32 = jnp.float32
LOW = -1e30
FLOOR = -1e20


def iota(shape, dim):
    return lax.broadcasted_iota(jnp.int32, shape, dim)


def as_column(row, n):
    return jnp.sum(jnp.where(iota((n, n), 0) == iota((n, n), 1), row, 0.0), axis=1, keepdims=True)


def pick(row, index_col, n):
    lanes = iota((n, n), 1).astype(F32)
    return jnp.sum(jnp.where(lanes == index_col, row, 0.0), axis=1, keepdims=True)


def inside(value, start, n):
    return (value >= start) & (value < start + n)


def remote_rank(row, start, n):
    far = jnp.where(inside(row, start, n), 0.0, 1.0)
    far_col = as_column(far, n)
    rank = jnp.sum(jnp.where(iota((n, n), 0) < iota((n, n), 1), far_col, 0.0), axis=0, keepdims=True)
    return far, rank


def bdot(a, b):
    return lax.dot_general(a, b, (((1,), (0,)), ((), ())), preferred_element_type=F32)


def tdot(a, b):
    return lax.dot_general(a, b, (((1,), (1,)), ((), ())), preferred_element_type=F32)


def attention_part(n_dp, n_ex, rows, cache, src, beams, chunks, inputs, scratch, residual, normed, first_row, enter):
    (
        hidden_hbm, q_self_hbm, k_new_hbm, v_new_hbm, q_cross_hbm, parents_hbm, ks_hbm, vs_hbm, gain_hbm,
        ck_hbm, cv_hbm, xk_hbm, xv_hbm,
    ) = inputs
    (
    hidden, q_self, k_new, v_new, q_cross, parents, key_scale, value_scale, gain,
    kbuf, vbuf, xkbuf, xvbuf, q_all, o_all, o_send, x_out, bias, bias_e, bias_x, scales,
    stat, par_own, par_in, q_d, q_e, in_c, in_d, in_e, o_d, o_e, back_c, back_d, back_e, stat_in, stat_in2,
    s_self, w_self, s_cross, w_cross, load_sem, small_sem, send_sem, recv_sem,
    ) = scratch
    width = hidden.shape[2]
    heads = key_scale.shape[1]
    size = width // heads
    per_chunk = heads // chunks
    quarter = width // 4
    n_dev = n_dp * n_ex
    me = lax.axis_index("dp") * n_ex + lax.axis_index("expert")

    def at(offset):
        other = lax.rem(me + offset + n_dev, n_dev)
        return (other // n_ex, lax.rem(other, n_ex))

    def load(k, c, source, buffer):
        part = width // chunks
        return pltpu.make_async_copy(
            source.at[:, pl.ds(pl.multiple_of(c * part, part), part)], buffer.at[c], load_sem.at[k, c]
        )

    small = [
        pltpu.make_async_copy(source, target, small_sem.at[i])
        for i, (source, target) in enumerate((
            (parents_hbm, parents), (q_self_hbm, q_self), (k_new_hbm, k_new), (v_new_hbm, v_new),
            (ks_hbm, key_scale), (vs_hbm, value_scale), (q_cross_hbm, q_cross), (hidden_hbm, hidden),
            (gain_hbm, gain),
        ))
    ]
    for copy in small:
        copy.start()
    early = chunks // 2
    for c in range(early):
        load(2, c, xk_hbm, xkbuf).start()
        load(3, c, xv_hbm, xvbuf).start()
    for c in range(chunks):
        load(0, c, ck_hbm, kbuf).start()
        load(1, c, cv_hbm, vbuf).start()
    for c in range(early, chunks):
        load(2, c, xk_hbm, xkbuf).start()
        load(3, c, xv_hbm, xvbuf).start()

    par_own[...] = jnp.zeros_like(par_own)
    small[0].wait()
    small[1].wait()
    par_own[0:2, 0:rows] = parents[...]
    own = (me * rows).astype(F32)
    after = (lax.rem(me + 1, n_dev) * rows).astype(F32)
    after2 = (lax.rem(me + 2, n_dev) * rows).astype(F32)
    p0 = parents[0:1, :].astype(F32)
    p1 = parents[1:2, :].astype(F32)
    far0, rank0 = remote_rank(p0, own, rows)
    far1, rank1 = remote_rank(p1, own, rows)
    far0_col, rank0_col = as_column(far0, rows), as_column(rank0, rows)
    far1_col, rank1_col = as_column(far1, rows), as_column(rank1, rows)
    sub = iota((16, rows), 0)
    lane = iota((rows, 16), 1)

    def compact(value, far, rank):
        total = jnp.zeros((16, quarter), F32)
        for k in range(4):
            hot = ((sub >> 2) == k) & ((sub & 3).astype(F32) == rank) & (far > 0.5)
            total += bdot(jnp.where(hot, 1.0, 0.0).astype(BF), value[:, k * quarter:(k + 1) * quarter])
        return total.astype(BF)

    q_d[...] = compact(q_self[0], far0, rank0)
    q_e[...] = compact(q_self[1], far1, rank1)

    def remote(source, target, number, offset):
        return pltpu.make_async_remote_copy(
            src_ref=source, dst_ref=target, send_sem=send_sem.at[number], recv_sem=recv_sem.at[number],
            device_id=at(offset), device_id_type=MESH,
        )

    out_copies = [
        remote(par_own, par_in.at[0], 0, -1),
        remote(par_own, par_in.at[1], 1, -2),
        remote(q_d, in_d, 2, -1),
        remote(q_e, in_e, 3, -2),
        remote(q_self.at[1], in_c, 4, -1),
    ]
    enter()
    for copy in out_copies:
        copy.start()

    small[4].wait()
    small[5].wait()
    sentence = (iota((2 * rows, 1), 0) & (rows - 1)) // beams
    ks = jnp.zeros((2 * rows, heads), F32)
    vs = jnp.zeros((2 * rows, heads), F32)
    for s in range(rows // beams):
        ks = jnp.where(sentence == s, key_scale[s:s + 1, :], ks)
        vs = jnp.where(sentence == s, value_scale[s:s + 1, :], vs)
    root = 1.0 / math.sqrt(size)
    scales[0, :, 0:heads] = ks * root
    scales[1, :, 0:heads] = vs
    n_cross = (rows // beams) * src
    bias_x[...] = jnp.where(
        iota((2 * rows, n_cross), 1) // src == (iota((2 * rows, n_cross), 0) & (rows - 1)) // beams, 0.0, LOW
    )
    def cross_chunk(c, carry):
        load(2, c, xk_hbm, xkbuf).wait()
        load(3, c, xv_hbm, xvbuf).wait()
        lanes_x = iota((2 * rows, 128), 1)
        heads_at = [pl.ds(pl.multiple_of((c * per_chunk + j) * size, size), size) for j in range(per_chunk)]
        for j in range(per_chunk):
            ks_h = jnp.sum(jnp.where(lanes_x == c * per_chunk + j, scales[0], 0.0), axis=1, keepdims=True)
            q = jnp.concatenate([q_cross[0, :, heads_at[j]], q_cross[1, :, heads_at[j]]], axis=0)
            s_cross[j] = tdot(q, xkbuf[c, :, j * size:(j + 1) * size]) * ks_h + bias_x[...]
        totals = []
        for j in range(per_chunk):
            s = s_cross[j]
            w = jnp.exp(s - jnp.max(s, axis=1, keepdims=True))
            totals.append(jnp.sum(w, axis=1, keepdims=True))
            w_cross[j] = w.astype(BF)
        for j in range(per_chunk):
            vs_h = jnp.sum(jnp.where(lanes_x == c * per_chunk + j, scales[1], 0.0), axis=1, keepdims=True)
            o = bdot(w_cross[j], xvbuf[c, :, j * size:(j + 1) * size])
            x_out[:, heads_at[j]] = o * (vs_h / totals[j])
        return carry

    small[6].wait()
    lax.fori_loop(0, early, cross_chunk, 0)
    q_all[0:rows, :] = q_self[0]
    q_all[rows:2 * rows, :] = q_self[1]

    for i in (2, 3, 7, 8):
        small[i].wait()
    for copy in out_copies:
        copy.wait()
    q_all[2 * rows:3 * rows, :] = in_c[...]
    a16, b16 = iota((16, 16), 0), iota((16, 16), 1)
    for k in range(4):
        take_d = jnp.where((b16 == a16 + 4 * k) & (a16 < 4), 1.0, 0.0).astype(BF)
        take_e = jnp.where((b16 == a16 - 4 + 4 * k) & (a16 >= 4) & (a16 < 8), 1.0, 0.0).astype(BF)
        q_all[3 * rows:4 * rows, k * quarter:(k + 1) * quarter] = (
            bdot(take_d, in_d[...]) + bdot(take_e, in_e[...])
        ).astype(BF)

    n0 = par_in[0, 0:1, 0:rows].astype(F32)
    n1 = par_in[0, 1:2, 0:rows].astype(F32)
    m1 = par_in[1, 1:2, 0:rows].astype(F32)
    p0_col, p1_col = as_column(p0, rows), as_column(p1, rows)
    n1_col = as_column(n1, rows)
    index = iota((rows, 1), 0).astype(F32)
    none = jnp.full((rows, 1), -1000.0, F32)

    def local(value):
        return jnp.where(inside(value, own, rows), value - own, -1.0)

    own_b = p1_col - own
    in_own = inside(p1_col, own, rows)
    row_b = jnp.where(in_own, local(pick(p0, own_b, rows)), -1.0)
    first_b = jnp.where(in_own, own_b, -1.0)
    in_next = inside(n1_col, after, rows)
    in_here = inside(n1_col, own, rows)
    row_c = jnp.where(
        in_next,
        local(pick(n0, n1_col - after, rows)),
        jnp.where(in_here, local(pick(p0, n1_col - own, rows)), -1.0),
    )
    first_c = jnp.where(in_here & jnp.logical_not(in_next), n1_col - own, -1.0)
    far_n, rank_n = remote_rank(n0, after, rows)
    far_m, rank_m = remote_rank(m1, after2, rows)
    i_col = iota((rows, rows), 0).astype(F32)
    val_d = jnp.sum(jnp.where((rank_n == i_col) & (far_n > 0.5), n0, 0.0), axis=1, keepdims=True)
    val_e = jnp.sum(jnp.where((rank_m == i_col - 4.0) & (far_m > 0.5), m1, 0.0), axis=1, keepdims=True)
    row_de = jnp.where(
        index < 4.0,
        local(val_d),
        jnp.where(
            (index < 8.0) & inside(val_e, after, rows), local(pick(n0, val_e - after, rows)), -1.0
        ),
    )
    row_sel = jnp.concatenate([local(p0_col), row_b, row_c, row_de], axis=0)
    first_sel = jnp.concatenate([index, first_b, first_c, none], axis=0)
    second_sel = jnp.concatenate([none, index, none, none], axis=0)
    slots = 4 * rows
    bias[...] = jnp.where((iota((slots, rows * cache), 1) // cache).astype(F32) == row_sel, 0.0, LOW)
    lane_e = iota((slots, 2 * rows), 1).astype(F32)
    bias_e[...] = jnp.where((lane_e == first_sel) | (lane_e - rows == second_sel), 0.0, LOW)

    stat[...] = jnp.zeros_like(stat)
    lanes = iota((slots, 128), 1)

    def self_chunk(c, carry):
        load(0, c, ck_hbm, kbuf).wait()
        load(1, c, cv_hbm, vbuf).wait()
        heads_at = [pl.ds(pl.multiple_of((c * per_chunk + j) * size, size), size) for j in range(per_chunk)]
        extras = []
        for j in range(per_chunk):
            q = q_all[:, heads_at[j]]
            k_extra = jnp.concatenate([k_new[0, :, heads_at[j]], k_new[1, :, heads_at[j]]], axis=0)
            s_self[j] = tdot(q, kbuf[c, :, j * size:(j + 1) * size]) * root + bias[...]
            extras.append(tdot(q, k_extra) * root + bias_e[...])
        for j in range(per_chunk):
            s, s_e = s_self[j], extras[j]
            top = jnp.maximum(
                jnp.maximum(jnp.max(s, axis=1, keepdims=True), jnp.max(s_e, axis=1, keepdims=True)), FLOOR
            )
            w = jnp.exp(s - top)
            w_e = jnp.exp(s_e - top)
            total = jnp.sum(w, axis=1, keepdims=True) + jnp.sum(w_e, axis=1, keepdims=True)
            w_self[j] = w.astype(BF)
            extras[j] = w_e.astype(BF)
            here = lanes == c * per_chunk + j
            stat[0] = jnp.where(here, top, stat[0])
            stat[1] = jnp.where(here, total, stat[1])
        for j in range(per_chunk):
            v_extra = jnp.concatenate([v_new[0, :, heads_at[j]], v_new[1, :, heads_at[j]]], axis=0)
            o_all[:, heads_at[j]] = bdot(w_self[j], vbuf[c, :, j * size:(j + 1) * size]) + bdot(
                extras[j], v_extra
            )
        return carry

    lax.fori_loop(0, chunks, self_chunk, 0)

    o_send[...] = o_all[2 * rows:4 * rows, :].astype(BF)
    total_d = jnp.zeros((16, quarter), F32)
    total_e = jnp.zeros((16, quarter), F32)
    for k in range(4):
        piece = o_send[rows:2 * rows, k * quarter:(k + 1) * quarter]
        put_d = jnp.where(((a16 >> 2) == k) & (b16 == (a16 & 3)), 1.0, 0.0).astype(BF)
        put_e = jnp.where(((a16 >> 2) == k) & (b16 == (a16 & 3) + 4), 1.0, 0.0).astype(BF)
        total_d += bdot(put_d, piece)
        total_e += bdot(put_e, piece)
    o_d[...] = total_d.astype(BF)
    o_e[...] = total_e.astype(BF)
    back_copies = [
        remote(o_send.at[pl.ds(0, rows)], back_c, 5, 1),
        remote(o_d, back_d, 6, 1),
        remote(o_e, back_e, 7, 2),
        remote(stat.at[:, pl.ds(2 * rows, rows + 8)], stat_in, 8, 1),
        remote(stat.at[:, pl.ds(3 * rows, 8)], stat_in2, 9, 2),
    ]
    for copy in back_copies:
        copy.start()

    lax.fori_loop(early, chunks, cross_chunk, 0)

    for copy in back_copies:
        copy.wait()

    def spread(compact_ref, far_col, rank_col):
        pieces = []
        for k in range(4):
            hot = ((lane >> 2) == k) & ((lane & 3).astype(F32) == rank_col) & (far_col > 0.5)
            pieces.append(bdot(jnp.where(hot, 1.0, 0.0).astype(BF), compact_ref[...]))
        return pieces

    def spread_stat(ref, start, far_col, rank_col):
        top = jnp.where(far_col > 0.5, 0.0, FLOOR) + jnp.zeros((rows, 128), F32)
        total = jnp.zeros((rows, 128), F32)
        for j in range(4):
            hot = (rank_col == float(j)) & (far_col > 0.5)
            top += jnp.where(hot, ref[0, start + j:start + j + 1, :], 0.0)
            total += jnp.where(hot, ref[1, start + j:start + j + 1, :], 0.0)
        return top, total

    o_far0 = spread(back_d, far0_col, rank0_col)
    o_far1 = spread(back_e, far1_col, rank1_col)
    stats0 = [
        (stat[0, 0:rows, :], stat[1, 0:rows, :]),
        spread_stat(stat_in, rows, far0_col, rank0_col),
    ]
    stats1 = [
        (stat[0, rows:2 * rows, :], stat[1, rows:2 * rows, :]),
        (stat_in[0, 0:rows, :], stat_in[1, 0:rows, :]),
        spread_stat(stat_in2, 4, far1_col, rank1_col),
    ]

    def weights(stats):
        top = stats[0][0]
        for t, _ in stats[1:]:
            top = jnp.maximum(top, t)
        parts = [jnp.exp(t - top) for t, _ in stats]
        total = sum(w * l for w, (_, l) in zip(parts, stats))
        return [w / total for w in parts]

    w0 = weights(stats0)
    w1 = weights(stats1)
    per_quarter = heads // 4
    for t in range(2):
        for h in range(heads):
            at_h = slice(h * size, (h + 1) * size)
            k, j = h // per_quarter, h % per_quarter
            inner = slice(j * size, (j + 1) * size)
            if t == 0:
                mixed = o_all[0:rows, at_h] * w0[0][:, h:h + 1] + o_far0[k][:, inner] * w0[1][:, h:h + 1]
            else:
                mixed = (
                    o_all[rows:2 * rows, at_h] * w1[0][:, h:h + 1]
                    + back_c[:, at_h].astype(F32) * w1[1][:, h:h + 1]
                    + o_far1[k][:, inner] * w1[2][:, h:h + 1]
                )
            residual[t * rows:(t + 1) * rows, at_h] = (
                hidden[t, :, at_h].astype(F32) + mixed + x_out[t * rows:(t + 1) * rows, at_h]
            )
    value = residual[...]
    average = jnp.mean(value, axis=1, keepdims=True)
    centered = value - average
    variance = jnp.mean(centered * centered, axis=1, keepdims=True)
    normed[first_row, :] = (centered * lax.rsqrt(variance + epsilon) * gain[...]).astype(BF)


def layer_kernel(
    n_dp, n_ex, cap,
    inputs, attention_args, scratch, out_ref,
):
    ids_hbm, router_hbm, w_in_hbm, w_out_hbm = inputs
    (
        residual, normed, ids, info, info_far, router, w_in, w_out, normed_far, outgoing, outgoing_far,
        xbuf, units, p_mine, p_send, p_back, fin_a, fin_b, home, returned, returned_far,
        far_out, far_in, y_send, y_back,
        load_sem, pair_s, pair_r, far_s, far_r, a2a_s, a2a_r, far_a2a_s, far_a2a_r, near_s, near_r, sib_s, sib_r,
        part_s, part_r, fin_s, fin_r, ret_s, ret_r, far_ret_s, far_ret_r,
    ) = scratch
    steps, rows = ids.shape[0], ids.shape[2]
    tokens = steps * rows
    width = residual.shape[1]
    half = width // 2
    hidden_units = w_in.shape[1]
    slots = 2 * steps * cap
    chunk = n_ex * slots
    group = chunk // 4
    dp = lax.axis_index("dp")
    me = lax.axis_index("expert")
    core = lax.rem(dp, 2)
    n_y = n_dp // 2
    place = dp // 2
    sibling = (dp + 1 - 2 * core, me)
    up_y = (lax.rem(place + 1, n_y) * 2 + core, me)
    down_y = (lax.rem(place + n_y - 1, n_y) * 2 + core, me)
    far_place = lax.rem(place + 2, n_y) * 2
    far_same = (far_place + core, me)

    def peer(o):
        return (dp, lax.rem(me + o, n_ex))

    def peer_back(o):
        return (dp, lax.rem(me - o + n_ex, n_ex))

    barrier = pltpu.get_barrier_semaphore()
    position = dp * n_ex + me

    def along(offset):
        other = lax.rem(position + offset + n_dp * n_ex, n_dp * n_ex)
        return (other // n_ex, lax.rem(other, n_ex))

    others = (
        [sibling, up_y, down_y, (far_place, me), (far_place + 1, me)]
        + [peer(o) for o in range(1, n_ex)]
        + [along(o) for o in (-1, -2, 1, 2)]
    )
    for other in others:
        pl.semaphore_signal(barrier, inc=1, device_id=other, device_id_type=MESH)

    mine = pl.ds(pl.multiple_of(core * tokens, tokens), tokens)
    loads = [
        pltpu.make_async_copy(ids_hbm, ids, load_sem.at[0]),
        pltpu.make_async_copy(router_hbm, router, load_sem.at[1]),
        pltpu.make_async_copy(w_in_hbm, w_in, load_sem.at[2]),
        pltpu.make_async_copy(w_out_hbm, w_out, load_sem.at[3]),
    ]

    def enter():
        for copy in loads:
            copy.start()
        pl.semaphore_wait(barrier, len(others))

    attention_part(n_dp, n_ex, *attention_args, residual, normed, mine, enter)

    started = []

    def send(source, target, s_sem, r_sem, device):
        copy = pltpu.make_async_remote_copy(
            src_ref=source, dst_ref=target, send_sem=s_sem, recv_sem=r_sem,
            device_id=device, device_id_type=MESH,
        )
        copy.start()
        started.append(copy)
        return copy

    pair = [send(normed.at[mine], normed.at[mine], pair_s.at[0], pair_r.at[0], sibling)]
    far = [
        send(
            normed.at[mine, pl.ds(c * half, half)], normed_far.at[mine], far_s.at[c], far_r.at[core], (far_place + c, me)
        )
        for c in range(2)
    ]

    loads[0].wait()
    loads[1].wait()
    logits = tdot(normed[mine, :], router[...])
    lane_e = iota((tokens, n_ex), 1).astype(F32)
    lane_i = iota((tokens, 128), 1)
    named = [
        jnp.concatenate([as_column(ids[t, k:k + 1, :].astype(F32), rows) for t in range(steps)], axis=0)
        for k in range(2)
    ]
    picked = [jnp.sum(jnp.where(lane_e == n, logits, 0.0), axis=1, keepdims=True) for n in named]
    first_gate = 1.0 / (1.0 + jnp.exp(picked[1] - picked[0]))
    info[core] = jnp.where(lane_i == 0, named[0], jnp.where(lane_i == 1, named[1], first_gate))
    pair.append(send(info.at[core], info.at[core], pair_s.at[1], pair_r.at[1], sibling))
    for c in range(2):
        far.append(send(info.at[core], info_far.at[core], far_s.at[2 + c], far_r.at[2 + core], (far_place + c, me)))

    lane_x = iota((tokens, 128), 1).astype(F32)
    lower = (iota((tokens, tokens), 1) < iota((tokens, tokens), 0)) & (
        iota((tokens, tokens), 0) // rows == iota((tokens, tokens), 1) // rows
    )
    lower = jnp.where(lower, 1.0, 0.0).astype(BF)
    step_of = (iota((tokens, 1), 0) // rows).astype(F32)
    lane_c = iota((tokens, chunk), 1).astype(F32)
    my_expert = me.astype(F32)

    def routes(table):
        hot_rows, gate_rows = [], []
        for c in range(2):
            named = [table[c, :, k:k + 1] for k in range(2)]
            gate = table[c, :, 2:3]
            one_hot = [lane_x == n for n in named]
            before = bdot(lower, jnp.where(one_hot[0] | one_hot[1], 1.0, 0.0).astype(BF))
            hots = []
            for k in range(2):
                spot = jnp.sum(jnp.where(one_hot[k], before, 0.0), axis=1, keepdims=True)
                distance = named[k] - my_expert
                distance = jnp.where(distance < 0.0, distance + n_ex, distance)
                column = distance * slots + spot + step_of * cap + c * steps * cap
                hots.append(lane_c == column)
            hot_rows.append(jnp.where(hots[0] | hots[1], 1.0, 0.0).astype(BF))
            gate_rows.append(jnp.where(hots[0], gate, 0.0) + jnp.where(hots[1], 1.0 - gate, 0.0))
        gates = jnp.concatenate(gate_rows, axis=0)
        high = gates.astype(BF)
        return jnp.concatenate(hot_rows, axis=0), (high, (gates - high.astype(F32)).astype(BF))

    def spread(hot, value):
        return lax.dot_general(hot, value, (((0,), (0,)), ((), ())), preferred_element_type=F32).astype(BF)

    def block(o):
        return pl.ds(o * slots, slots)

    def piece(g):
        return pl.ds(g * group, group)

    at_half = pl.ds(pl.multiple_of(core * half, half), half)
    for copy in pair:
        copy.wait_recv()
    dispatch, mix = routes(info)
    outgoing[...] = spread(dispatch, normed[:, at_half])
    arrivals = [None] + [
        send(outgoing.at[block(o)], xbuf.at[core, 0, block(o)], a2a_s.at[o], a2a_r.at[o], peer(o))
        for o in range(1, n_ex)
    ]
    xbuf[core, 0, block(0), :] = outgoing[block(0), :]
    recv_far = [
        pltpu.make_async_remote_copy(
            src_ref=normed.at[mine, pl.ds(0, half)], dst_ref=normed_far.at[pl.ds(c * tokens, tokens)],
            send_sem=far_s.at[c], recv_sem=far_r.at[c], device_id=far_same, device_id_type=MESH,
        )
        for c in range(2)
    ] + [
        pltpu.make_async_remote_copy(
            src_ref=info.at[core], dst_ref=info_far.at[c],
            send_sem=far_s.at[2 + c], recv_sem=far_r.at[2 + c], device_id=far_same, device_id_type=MESH,
        )
        for c in range(2)
    ]
    for copy in recv_far:
        copy.wait_recv()
    dispatch_far, mix_far = routes(info_far)
    outgoing_far[...] = spread(dispatch_far, normed_far[...])
    far_arrivals = [None] + [
        send(outgoing_far.at[block(o)], xbuf.at[core, 3, block(o)], far_a2a_s.at[o], far_a2a_r.at[o], peer(o))
        for o in range(1, n_ex)
    ]
    xbuf[core, 3, block(0), :] = outgoing_far[block(0), :]

    per_group = n_ex // 4

    def to_sibling(k, g):
        return send(
            xbuf.at[core, k, piece(g)], xbuf.at[core, k, piece(g)], sib_s.at[k, g], sib_r.at[k, g], sibling
        )

    def from_near(k, g):
        return 1 + g // 2, 2 * (k - 1) + g % 2

    tile = min(256, half, hidden_units)

    def first_product(k, slot):
        def first(j, carry):
            cols = pl.ds(pl.multiple_of(j * tile, tile), tile)
            a = bdot(xbuf[0, k], w_in[0:half, cols]) + bdot(xbuf[1, k], w_in[half:width, cols])
            units[slot, :, cols] = jnp.maximum(a, 0.0).astype(BF)
            return carry

        lax.fori_loop(0, hidden_units // tile, first, 0)

    def second_product(k, slot):
        def second(base, target):
            def step(j, carry):
                cols = pl.ds(pl.multiple_of(base + j * tile, tile), tile)
                target[k, :, pl.ds(pl.multiple_of(j * tile, tile), tile)] = bdot(
                    units[slot], w_out[:, cols]
                ).astype(BF)
                return carry

            lax.fori_loop(0, half // tile, step, 0)

        second((1 - core) * half, p_send)
        copy = send(p_send.at[k], p_back.at[k], part_s.at[k], part_r.at[k], sibling)
        second(core * half, p_mine)
        return copy

    def reduce_part(k):
        return p_mine[k].astype(F32) + p_back[k].astype(F32)

    sib, near, final = {}, {}, {}
    for g in range(4):
        for o in range(g * per_group, (g + 1) * per_group):
            if o:
                arrivals[o].wait_recv()
        for k in (1, 2):
            to_chunk, spot = from_near(k, g)
            near[k, g] = send(
                xbuf.at[core, 0, piece(g)], xbuf.at[core, to_chunk, piece(spot)],
                near_s.at[k - 1, g], near_r.at[k - 1, g], up_y if k == 1 else down_y,
            )
        sib[0, g] = to_sibling(0, g)
    loads[2].wait()
    loads[3].wait()
    for g in range(4):
        sib[0, g].wait_recv()
    first_product(0, 0)
    parts = {0: second_product(0, 0)}

    def near_arrived(h):
        for g in (2 * h, 2 * h + 1):
            for k in (1, 2):
                near[k, g].wait_recv()
                to_chunk, spot = from_near(k, g)
                sib[to_chunk, spot] = to_sibling(to_chunk, spot)

    def finish_near(h):
        parts[1 + h].wait()
        p_send[1 + h] = reduce_part(1 + h).astype(BF)
        for g in (2 * h, 2 * h + 1):
            for k in (1, 2):
                from_chunk, spot = from_near(k, g)
                final[k, g] = send(
                    p_send.at[from_chunk, piece(spot)], (fin_b if k == 1 else fin_a).at[piece(g)],
                    fin_s.at[k - 1, g], fin_r.at[k - 1, g], down_y if k == 1 else up_y,
                )

    near_arrived(0)
    for g in range(4):
        for o in range(g * per_group, (g + 1) * per_group):
            if o:
                far_arrivals[o].wait_recv()
        sib[3, g] = to_sibling(3, g)
    for spot in range(4):
        sib[1, spot].wait_recv()
    first_product(1, 1)
    parts[1] = second_product(1, 1)
    near_arrived(1)
    for g in range(4):
        sib[3, g].wait_recv()
    first_product(3, 0)
    finish_near(0)
    for spot in range(4):
        sib[2, spot].wait_recv()
    first_product(2, 1)
    parts[2] = second_product(2, 1)
    parts[3] = second_product(3, 0)
    finish_near(1)
    parts[0].wait()
    home[...] = reduce_part(0)
    parts[3].wait()
    p_mine[3] = reduce_part(3).astype(BF)
    far_replies = [None] + [
        send(
            p_mine.at[3, block(o)], returned_far.at[block(o)], far_ret_s.at[o], far_ret_r.at[o], peer_back(o)
        )
        for o in range(1, n_ex)
    ]
    returned_far[block(0), :] = p_mine[3, block(0), :]
    replies = [None] * n_ex

    def reply(groups):
        for g in groups:
            final[1, g].wait_recv()
            final[2, g].wait_recv()
            total = home[piece(g), :] + fin_a[piece(g), :].astype(F32) + fin_b[piece(g), :].astype(F32)
            p_mine[0, piece(g), :] = total.astype(BF)
            for o in range(g * per_group, (g + 1) * per_group):
                if o:
                    replies[o] = send(
                        p_mine.at[0, block(o)], returned.at[block(o)], ret_s.at[o], ret_r.at[o], peer_back(o)
                    )

    reply((0, 1))
    for o in range(1, n_ex):
        far_replies[o].wait_recv()
    back_far = returned_far[...]
    far_out[...] = (bdot(mix_far[0], back_far) + bdot(mix_far[1], back_far)).astype(BF)
    far_home = send(far_out, far_in, far_s.at[4], far_r.at[4], far_same)

    reply((2, 3))
    returned[block(0), :] = p_mine[0, block(0), :]
    far_home.wait_recv()
    for o in range(1, n_ex):
        replies[o].wait_recv()
    back = returned[...]
    y = bdot(mix[0], back) + bdot(mix[1], back) + far_in[...].astype(F32)
    is_first = core == 0
    y_send[...] = jnp.where(is_first, y[tokens:], y[:tokens])
    swap = send(y_send, y_back, pair_s.at[2], pair_r.at[2], sibling)
    residual[:, at_half] = residual[:, at_half] + jnp.where(is_first, y[:tokens], y[tokens:])
    swap.wait_recv()
    at_other = pl.ds(pl.multiple_of((1 - core) * half, half), half)
    residual[:, at_other] = residual[:, at_other] + y_back[...]
    for t in range(steps):
        out_ref[t] = residual[t * rows:(t + 1) * rows, :].astype(BF)
    waited = {id(p) for p in parts.values()}
    for copy in started:
        if id(copy) not in waited:
            copy.wait_send()


def layer(hidden, q_self, k_new, v_new, q_cross, cache_keys, cache_values, cross_keys, cross_values,
          key_scale, value_scale, parents, expert_ids, norm_gain, router, w_in, w_out):
    steps, rows, width = hidden.shape
    heads = key_scale.shape[1]
    cache = cache_keys.shape[1]
    sentences, src = cross_keys.shape[:2]
    chunks = 4
    n_dp, n_ex = lax.axis_size("dp"), lax.axis_size("expert")
    part = width // chunks
    n_self, n_cross, slots = rows * cache, sentences * src, 4 * rows
    quarter = width // 4
    tokens = steps * rows
    hidden_units = w_in.shape[2]
    half = width // 2
    cap = 4 * rows // n_ex
    chunk_slots = n_ex * 2 * steps * cap
    dma = pltpu.SemaphoreType.DMA
    attention_scratch = [pltpu.VMEM((steps, rows, width), BF)] * 5 + [
            pltpu.VMEM((steps, rows), jnp.int32),
            pltpu.VMEM((sentences, heads), F32),
            pltpu.VMEM((sentences, heads), F32),
            pltpu.VMEM((1, width), F32),
            pltpu.VMEM((chunks, n_self, part), BF),
            pltpu.VMEM((chunks, n_self, part), BF),
            pltpu.VMEM((chunks, n_cross, part), BF),
            pltpu.VMEM((chunks, n_cross, part), BF),
            pltpu.VMEM((slots, width), BF),
            pltpu.VMEM((slots, width), F32),
            pltpu.VMEM((2 * rows, width), BF),
            pltpu.VMEM((2 * rows, width), F32),
            pltpu.VMEM((slots, n_self), F32),
            pltpu.VMEM((slots, 2 * rows), F32),
            pltpu.VMEM((2 * rows, n_cross), F32),
            pltpu.VMEM((2, 2 * rows, 128), F32),
            pltpu.VMEM((2, slots, 128), F32),
            pltpu.VMEM((8, 128), jnp.int32),
            pltpu.VMEM((2, 8, 128), jnp.int32),
            pltpu.VMEM((16, quarter), BF),
            pltpu.VMEM((16, quarter), BF),
            pltpu.VMEM((rows, width), BF),
            pltpu.VMEM((16, quarter), BF),
            pltpu.VMEM((16, quarter), BF),
            pltpu.VMEM((16, quarter), BF),
            pltpu.VMEM((16, quarter), BF),
            pltpu.VMEM((rows, width), BF),
            pltpu.VMEM((16, quarter), BF),
            pltpu.VMEM((16, quarter), BF),
            pltpu.VMEM((2, rows + 8, 128), F32),
            pltpu.VMEM((2, 8, 128), F32),
            pltpu.VMEM((heads // chunks, slots, n_self), F32),
            pltpu.VMEM((heads // chunks, slots, n_self), BF),
            pltpu.VMEM((heads // chunks, 2 * rows, n_cross), F32),
            pltpu.VMEM((heads // chunks, 2 * rows, n_cross), BF),
            pltpu.SemaphoreType.DMA((4, chunks)),
            pltpu.SemaphoreType.DMA((9,)),
            pltpu.SemaphoreType.DMA((10,)),
            pltpu.SemaphoreType.DMA((10,)),
        ]
    expert_scratch = [
            pltpu.VMEM((tokens, width), F32),
            pltpu.VMEM((2 * tokens, width), BF),
            pltpu.VMEM((steps, 2, rows), jnp.int32),
            pltpu.VMEM((2, tokens, 128), F32),
            pltpu.VMEM((2, tokens, 128), F32),
            pltpu.VMEM((n_ex, width), BF),
            pltpu.VMEM((width, hidden_units), BF),
            pltpu.VMEM((hidden_units, width), BF),
            pltpu.VMEM((2 * tokens, half), BF),
            pltpu.VMEM((chunk_slots, half), BF),
            pltpu.VMEM((chunk_slots, half), BF),
            pltpu.VMEM((2, 4, chunk_slots, half), BF),
            pltpu.VMEM((2, chunk_slots, hidden_units), BF),
            pltpu.VMEM((4, chunk_slots, half), BF),
            pltpu.VMEM((4, chunk_slots, half), BF),
            pltpu.VMEM((4, chunk_slots, half), BF),
            pltpu.VMEM((chunk_slots, half), BF),
            pltpu.VMEM((chunk_slots, half), BF),
            pltpu.VMEM((chunk_slots, half), F32),
            pltpu.VMEM((chunk_slots, half), BF),
            pltpu.VMEM((chunk_slots, half), BF),
            pltpu.VMEM((2 * tokens, half), BF),
            pltpu.VMEM((2 * tokens, half), BF),
            pltpu.VMEM((tokens, half), F32),
            pltpu.VMEM((tokens, half), F32),
            dma((4,)), dma((3,)), dma((3,)), dma((5,)), dma((5,)), dma((n_ex,)), dma((n_ex,)),
            dma((n_ex,)), dma((n_ex,)), dma((2, 4)), dma((2, 4)), dma((4, 4)), dma((4, 4)), dma((4,)), dma((4,)),
            dma((2, 4)), dma((2, 4)), dma((n_ex,)), dma((n_ex,)), dma((n_ex,)), dma((n_ex,)),
    ]

    def kernel(*refs):
        layer_kernel(
            n_dp, n_ex, cap, refs[13:17],
            (rows, cache, src, rows // sentences, chunks, refs[0:13], refs[18]), refs[19], refs[17],
        )

    return pl.pallas_call(
        kernel,
        out_shape=jax.ShapeDtypeStruct((steps, rows, width), BF),
        in_specs=[pl.BlockSpec(memory_space=pl.ANY)] * 17,
        out_specs=pl.BlockSpec(memory_space=pltpu.VMEM),
        scratch_shapes=(tuple(attention_scratch), tuple(expert_scratch)),
        compiler_params=pltpu.CompilerParams(
            collective_id=0, has_side_effects=True, vmem_limit_bytes=60 * 2**20
        ),
    )(
        hidden, q_self, k_new, v_new, q_cross, parents, key_scale, value_scale, norm_gain.reshape(1, width),
        cache_keys.reshape(n_self, width), cache_values.reshape(n_self, width),
        cross_keys.reshape(n_cross, width), cross_values.reshape(n_cross, width),
        jnp.swapaxes(expert_ids, 1, 2), router.T,
        w_in.reshape(width, hidden_units), w_out.reshape(hidden_units, width),
    )


def solution(mesh):
    in_specs = (
        P(None, ("dp", "expert"), None),
        P(None, ("dp", "expert"), None),
        P(None, ("dp", "expert"), None),
        P(None, ("dp", "expert"), None),
        P(None, ("dp", "expert"), None),
        P(("dp", "expert"), None, None),
        P(("dp", "expert"), None, None),
        P(("dp", "expert"), None, None),
        P(("dp", "expert"), None, None),
        P(("dp", "expert"), None),
        P(("dp", "expert"), None),
        P(None, ("dp", "expert")),
        P(None, ("dp", "expert"), None),
        P(),
        P(),
        P("expert", None, "dp"),
        P("expert", "dp", None),
    )
    out_specs = P(None, ("dp", "expert"), None)
    return jax.shard_map(layer, mesh=mesh, in_specs=in_specs, out_specs=out_specs, check_vma=False)
```

```python
import functools
import math

import jax
import jax.numpy as jnp
from jax import lax
from jax.experimental import pallas as pl
from jax.experimental.pallas import tpu as pltpu
from jax.sharding import PartitionSpec as P

epsilon = 1e-05
MESH = pl.DeviceIdType.MESH
BF = jnp.bfloat16
F32 = jnp.float32
LOW = -1e30
FLOOR = -1e20


def iota(shape, dim):
    return lax.broadcasted_iota(jnp.int32, shape, dim)


def as_column(row, n):
    return jnp.sum(jnp.where(iota((n, n), 0) == iota((n, n), 1), row, 0.0), axis=1, keepdims=True)


def pick(row, index_col, n):
    lanes = iota((n, n), 1).astype(F32)
    return jnp.sum(jnp.where(lanes == index_col, row, 0.0), axis=1, keepdims=True)


def inside(value, start, n):
    return (value >= start) & (value < start + n)


def remote_rank(row, start, n):
    far = jnp.where(inside(row, start, n), 0.0, 1.0)
    far_col = as_column(far, n)
    rank = jnp.sum(jnp.where(iota((n, n), 0) < iota((n, n), 1), far_col, 0.0), axis=0, keepdims=True)
    return far, rank


def bdot(a, b):
    return lax.dot_general(a, b, (((1,), (0,)), ((), ())), preferred_element_type=F32)


def tdot(a, b):
    return lax.dot_general(a, b, (((1,), (1,)), ((), ())), preferred_element_type=F32)


def attention_part(n_dp, n_ex, rows, cache, src, beams, chunks, inputs, scratch, residual, normed, first_row, enter, tell, prepare):
    (
        hidden_hbm, q_self_hbm, k_new_hbm, v_new_hbm, q_cross_hbm, parents_hbm, ks_hbm, vs_hbm, gain_hbm,
        ck_hbm, cv_hbm, xk_hbm, xv_hbm,
    ) = inputs
    (
    hidden, q_self, k_new, v_new, q_cross, parents, key_scale, value_scale, gain,
    kbuf, vbuf, xkbuf, xvbuf, q_all, o_all, o_send, x_out, bias, bias_e, bias_x, scales,
    stat, par_own, par_in, q_d, q_e, in_c, in_d, in_e, o_d, o_e, back_c, back_d, back_e, stat_in, stat_in2,
    s_self, w_self, s_cross, w_cross, load_sem, small_sem, send_sem, recv_sem,
    ) = scratch
    width = hidden.shape[2]
    heads = key_scale.shape[1]
    size = width // heads
    per_chunk = heads // chunks
    quarter = width // 4
    n_dev = n_dp * n_ex
    me = lax.axis_index("dp") * n_ex + lax.axis_index("expert")

    def at(offset):
        other = lax.rem(me + offset + n_dev, n_dev)
        return (other // n_ex, lax.rem(other, n_ex))

    def load(k, c, source, buffer):
        part = width // chunks
        return pltpu.make_async_copy(
            source.at[:, pl.ds(pl.multiple_of(c * part, part), part)], buffer.at[c], load_sem.at[k, c]
        )

    small = [
        pltpu.make_async_copy(source, target, small_sem.at[i])
        for i, (source, target) in enumerate((
            (parents_hbm, parents), (q_self_hbm, q_self), (k_new_hbm, k_new), (v_new_hbm, v_new),
            (ks_hbm, key_scale), (vs_hbm, value_scale), (q_cross_hbm, q_cross), (hidden_hbm, hidden),
            (gain_hbm, gain),
        ))
    ]
    for copy in small:
        copy.start()
    early = chunks // 2
    for c in range(early):
        load(2, c, xk_hbm, xkbuf).start()
        load(3, c, xv_hbm, xvbuf).start()
    for c in range(chunks):
        load(0, c, ck_hbm, kbuf).start()
        load(1, c, cv_hbm, vbuf).start()
    for c in range(early, chunks):
        load(2, c, xk_hbm, xkbuf).start()
        load(3, c, xv_hbm, xvbuf).start()

    par_own[...] = jnp.zeros_like(par_own)
    small[0].wait()
    small[1].wait()
    par_own[0:2, 0:rows] = parents[...]
    own = (me * rows).astype(F32)
    after = (lax.rem(me + 1, n_dev) * rows).astype(F32)
    after2 = (lax.rem(me + 2, n_dev) * rows).astype(F32)
    p0 = parents[0:1, :].astype(F32)
    p1 = parents[1:2, :].astype(F32)
    far0, rank0 = remote_rank(p0, own, rows)
    far1, rank1 = remote_rank(p1, own, rows)
    far0_col, rank0_col = as_column(far0, rows), as_column(rank0, rows)
    far1_col, rank1_col = as_column(far1, rows), as_column(rank1, rows)
    sub = iota((16, rows), 0)
    lane = iota((rows, 16), 1)

    def compact(value, far, rank):
        total = jnp.zeros((16, quarter), F32)
        for k in range(4):
            hot = ((sub >> 2) == k) & ((sub & 3).astype(F32) == rank) & (far > 0.5)
            total += bdot(jnp.where(hot, 1.0, 0.0).astype(BF), value[:, k * quarter:(k + 1) * quarter])
        return total.astype(BF)

    q_d[...] = compact(q_self[0], far0, rank0)
    q_e[...] = compact(q_self[1], far1, rank1)

    def remote(source, target, number, offset):
        return pltpu.make_async_remote_copy(
            src_ref=source, dst_ref=target, send_sem=send_sem.at[number], recv_sem=recv_sem.at[number],
            device_id=at(offset), device_id_type=MESH,
        )

    out_copies = [
        remote(par_own, par_in.at[0], 0, -1),
        remote(par_own, par_in.at[1], 1, -2),
        remote(q_d, in_d, 2, -1),
        remote(q_e, in_e, 3, -2),
        remote(q_self.at[1], in_c, 4, -1),
    ]
    enter()
    for copy in out_copies:
        copy.start()
    sent = tell()

    small[4].wait()
    small[5].wait()
    sentence = (iota((2 * rows, 1), 0) & (rows - 1)) // beams
    ks = jnp.zeros((2 * rows, heads), F32)
    vs = jnp.zeros((2 * rows, heads), F32)
    for s in range(rows // beams):
        ks = jnp.where(sentence == s, key_scale[s:s + 1, :], ks)
        vs = jnp.where(sentence == s, value_scale[s:s + 1, :], vs)
    root = 1.0 / math.sqrt(size)
    scales[0, :, 0:heads] = ks * root
    scales[1, :, 0:heads] = vs
    n_cross = (rows // beams) * src
    bias_x[...] = jnp.where(
        iota((2 * rows, n_cross), 1) // src == (iota((2 * rows, n_cross), 0) & (rows - 1)) // beams, 0.0, LOW
    )
    def cross_chunk(c, carry):
        load(2, c, xk_hbm, xkbuf).wait()
        load(3, c, xv_hbm, xvbuf).wait()
        lanes_x = iota((2 * rows, 128), 1)
        heads_at = [pl.ds(pl.multiple_of((c * per_chunk + j) * size, size), size) for j in range(per_chunk)]
        for j in range(per_chunk):
            ks_h = jnp.sum(jnp.where(lanes_x == c * per_chunk + j, scales[0], 0.0), axis=1, keepdims=True)
            q = jnp.concatenate([q_cross[0, :, heads_at[j]], q_cross[1, :, heads_at[j]]], axis=0)
            s_cross[j] = tdot(q, xkbuf[c, :, j * size:(j + 1) * size]) * ks_h + bias_x[...]
        totals = []
        for j in range(per_chunk):
            s = s_cross[j]
            w = jnp.exp(s - jnp.max(s, axis=1, keepdims=True))
            totals.append(jnp.sum(w, axis=1, keepdims=True))
            w_cross[j] = w.astype(BF)
        for j in range(per_chunk):
            vs_h = jnp.sum(jnp.where(lanes_x == c * per_chunk + j, scales[1], 0.0), axis=1, keepdims=True)
            o = bdot(w_cross[j], xvbuf[c, :, j * size:(j + 1) * size])
            x_out[:, heads_at[j]] = o * (vs_h / totals[j])
        return carry

    small[6].wait()
    lax.fori_loop(0, early, cross_chunk, 0)
    q_all[0:rows, :] = q_self[0]
    q_all[rows:2 * rows, :] = q_self[1]

    for i in (2, 3, 7, 8):
        small[i].wait()
    for copy in out_copies:
        copy.wait()
    q_all[2 * rows:3 * rows, :] = in_c[...]
    a16, b16 = iota((16, 16), 0), iota((16, 16), 1)
    for k in range(4):
        take_d = jnp.where((b16 == a16 + 4 * k) & (a16 < 4), 1.0, 0.0).astype(BF)
        take_e = jnp.where((b16 == a16 - 4 + 4 * k) & (a16 >= 4) & (a16 < 8), 1.0, 0.0).astype(BF)
        q_all[3 * rows:4 * rows, k * quarter:(k + 1) * quarter] = (
            bdot(take_d, in_d[...]) + bdot(take_e, in_e[...])
        ).astype(BF)

    n0 = par_in[0, 0:1, 0:rows].astype(F32)
    n1 = par_in[0, 1:2, 0:rows].astype(F32)
    m1 = par_in[1, 1:2, 0:rows].astype(F32)
    p0_col, p1_col = as_column(p0, rows), as_column(p1, rows)
    n1_col = as_column(n1, rows)
    index = iota((rows, 1), 0).astype(F32)
    none = jnp.full((rows, 1), -1000.0, F32)

    def local(value):
        return jnp.where(inside(value, own, rows), value - own, -1.0)

    own_b = p1_col - own
    in_own = inside(p1_col, own, rows)
    row_b = jnp.where(in_own, local(pick(p0, own_b, rows)), -1.0)
    first_b = jnp.where(in_own, own_b, -1.0)
    in_next = inside(n1_col, after, rows)
    in_here = inside(n1_col, own, rows)
    row_c = jnp.where(
        in_next,
        local(pick(n0, n1_col - after, rows)),
        jnp.where(in_here, local(pick(p0, n1_col - own, rows)), -1.0),
    )
    first_c = jnp.where(in_here & jnp.logical_not(in_next), n1_col - own, -1.0)
    far_n, rank_n = remote_rank(n0, after, rows)
    far_m, rank_m = remote_rank(m1, after2, rows)
    i_col = iota((rows, rows), 0).astype(F32)
    val_d = jnp.sum(jnp.where((rank_n == i_col) & (far_n > 0.5), n0, 0.0), axis=1, keepdims=True)
    val_e = jnp.sum(jnp.where((rank_m == i_col - 4.0) & (far_m > 0.5), m1, 0.0), axis=1, keepdims=True)
    row_de = jnp.where(
        index < 4.0,
        local(val_d),
        jnp.where(
            (index < 8.0) & inside(val_e, after, rows), local(pick(n0, val_e - after, rows)), -1.0
        ),
    )
    row_sel = jnp.concatenate([local(p0_col), row_b, row_c, row_de], axis=0)
    first_sel = jnp.concatenate([index, first_b, first_c, none], axis=0)
    second_sel = jnp.concatenate([none, index, none, none], axis=0)
    slots = 4 * rows
    bias[...] = jnp.where((iota((slots, rows * cache), 1) // cache).astype(F32) == row_sel, 0.0, LOW)
    lane_e = iota((slots, 2 * rows), 1).astype(F32)
    bias_e[...] = jnp.where((lane_e == first_sel) | (lane_e - rows == second_sel), 0.0, LOW)

    stat[...] = jnp.zeros_like(stat)
    lanes = iota((slots, 128), 1)

    def self_chunk(c, carry):
        load(0, c, ck_hbm, kbuf).wait()
        load(1, c, cv_hbm, vbuf).wait()
        heads_at = [pl.ds(pl.multiple_of((c * per_chunk + j) * size, size), size) for j in range(per_chunk)]
        extras = []
        for j in range(per_chunk):
            q = q_all[:, heads_at[j]]
            k_extra = jnp.concatenate([k_new[0, :, heads_at[j]], k_new[1, :, heads_at[j]]], axis=0)
            s_self[j] = tdot(q, kbuf[c, :, j * size:(j + 1) * size]) * root + bias[...]
            extras.append(tdot(q, k_extra) * root + bias_e[...])
        for j in range(per_chunk):
            s, s_e = s_self[j], extras[j]
            top = jnp.maximum(
                jnp.maximum(jnp.max(s, axis=1, keepdims=True), jnp.max(s_e, axis=1, keepdims=True)), FLOOR
            )
            w = jnp.exp(s - top)
            w_e = jnp.exp(s_e - top)
            total = jnp.sum(w, axis=1, keepdims=True) + jnp.sum(w_e, axis=1, keepdims=True)
            w_self[j] = w.astype(BF)
            extras[j] = w_e.astype(BF)
            here = lanes == c * per_chunk + j
            stat[0] = jnp.where(here, top, stat[0])
            stat[1] = jnp.where(here, total, stat[1])
        for j in range(per_chunk):
            v_extra = jnp.concatenate([v_new[0, :, heads_at[j]], v_new[1, :, heads_at[j]]], axis=0)
            o_all[:, heads_at[j]] = bdot(w_self[j], vbuf[c, :, j * size:(j + 1) * size]) + bdot(
                extras[j], v_extra
            )
        return carry

    lax.fori_loop(0, chunks, self_chunk, 0)

    o_send[...] = o_all[2 * rows:4 * rows, :].astype(BF)
    total_d = jnp.zeros((16, quarter), F32)
    total_e = jnp.zeros((16, quarter), F32)
    for k in range(4):
        piece = o_send[rows:2 * rows, k * quarter:(k + 1) * quarter]
        put_d = jnp.where(((a16 >> 2) == k) & (b16 == (a16 & 3)), 1.0, 0.0).astype(BF)
        put_e = jnp.where(((a16 >> 2) == k) & (b16 == (a16 & 3) + 4), 1.0, 0.0).astype(BF)
        total_d += bdot(put_d, piece)
        total_e += bdot(put_e, piece)
    o_d[...] = total_d.astype(BF)
    o_e[...] = total_e.astype(BF)
    back_copies = [
        remote(o_send.at[pl.ds(0, rows)], back_c, 5, 1),
        remote(o_d, back_d, 6, 1),
        remote(o_e, back_e, 7, 2),
        remote(stat.at[:, pl.ds(2 * rows, rows + 8)], stat_in, 8, 1),
        remote(stat.at[:, pl.ds(3 * rows, 8)], stat_in2, 9, 2),
    ]
    for copy in back_copies:
        copy.start()

    prepare(sent)
    lax.fori_loop(early, chunks, cross_chunk, 0)

    for copy in back_copies:
        copy.wait()

    def spread(compact_ref, far_col, rank_col):
        pieces = []
        for k in range(4):
            hot = ((lane >> 2) == k) & ((lane & 3).astype(F32) == rank_col) & (far_col > 0.5)
            pieces.append(bdot(jnp.where(hot, 1.0, 0.0).astype(BF), compact_ref[...]))
        return pieces

    def spread_stat(ref, start, far_col, rank_col):
        top = jnp.where(far_col > 0.5, 0.0, FLOOR) + jnp.zeros((rows, 128), F32)
        total = jnp.zeros((rows, 128), F32)
        for j in range(4):
            hot = (rank_col == float(j)) & (far_col > 0.5)
            top += jnp.where(hot, ref[0, start + j:start + j + 1, :], 0.0)
            total += jnp.where(hot, ref[1, start + j:start + j + 1, :], 0.0)
        return top, total

    o_far0 = spread(back_d, far0_col, rank0_col)
    o_far1 = spread(back_e, far1_col, rank1_col)
    stats0 = [
        (stat[0, 0:rows, :], stat[1, 0:rows, :]),
        spread_stat(stat_in, rows, far0_col, rank0_col),
    ]
    stats1 = [
        (stat[0, rows:2 * rows, :], stat[1, rows:2 * rows, :]),
        (stat_in[0, 0:rows, :], stat_in[1, 0:rows, :]),
        spread_stat(stat_in2, 4, far1_col, rank1_col),
    ]

    def weights(stats):
        top = stats[0][0]
        for t, _ in stats[1:]:
            top = jnp.maximum(top, t)
        parts = [jnp.exp(t - top) for t, _ in stats]
        total = sum(w * l for w, (_, l) in zip(parts, stats))
        return [w / total for w in parts]

    w0 = weights(stats0)
    w1 = weights(stats1)
    per_quarter = heads // 4
    for t in range(2):
        for h in range(heads):
            at_h = slice(h * size, (h + 1) * size)
            k, j = h // per_quarter, h % per_quarter
            inner = slice(j * size, (j + 1) * size)
            if t == 0:
                mixed = o_all[0:rows, at_h] * w0[0][:, h:h + 1] + o_far0[k][:, inner] * w0[1][:, h:h + 1]
            else:
                mixed = (
                    o_all[rows:2 * rows, at_h] * w1[0][:, h:h + 1]
                    + back_c[:, at_h].astype(F32) * w1[1][:, h:h + 1]
                    + o_far1[k][:, inner] * w1[2][:, h:h + 1]
                )
            residual[t * rows:(t + 1) * rows, at_h] = (
                hidden[t, :, at_h].astype(F32) + mixed + x_out[t * rows:(t + 1) * rows, at_h]
            )
    value = residual[...]
    average = jnp.mean(value, axis=1, keepdims=True)
    centered = value - average
    variance = jnp.mean(centered * centered, axis=1, keepdims=True)
    normed[first_row, :] = (centered * lax.rsqrt(variance + epsilon) * gain[...]).astype(BF)


def layer_kernel(
    n_dp, n_ex, cap,
    inputs, attention_args, scratch, out_ref,
):
    ids_hbm, router_hbm, w_in_hbm, w_out_hbm = inputs
    (
        residual, normed, ids, told, told_far, hot, dispatch, info, info_far, router, w_in, w_out, normed_far, outgoing, outgoing_far,
        xbuf, units, p_mine, p_send, p_back, fin_a, fin_b, home, returned, returned_far,
        far_out, far_in, y_send, y_back,
        load_sem, ids_s, ids_r, pair_s, pair_r, far_s, far_r, a2a_s, a2a_r, far_a2a_s, far_a2a_r, near_s, near_r, sib_s, sib_r,
        part_s, part_r, fin_s, fin_r, ret_s, ret_r, far_ret_s, far_ret_r,
    ) = scratch
    steps, rows = ids.shape[0], ids.shape[2]
    tokens = steps * rows
    width = residual.shape[1]
    half = width // 2
    hidden_units = w_in.shape[1]
    slots = 2 * steps * cap
    chunk = n_ex * slots
    group = chunk // 4
    dp = lax.axis_index("dp")
    me = lax.axis_index("expert")
    core = lax.rem(dp, 2)
    n_y = n_dp // 2
    place = dp // 2
    sibling = (dp + 1 - 2 * core, me)
    up_y = (lax.rem(place + 1, n_y) * 2 + core, me)
    down_y = (lax.rem(place + n_y - 1, n_y) * 2 + core, me)
    far_place = lax.rem(place + 2, n_y) * 2
    far_same = (far_place + core, me)

    def peer(o):
        return (dp, lax.rem(me + o, n_ex))

    def peer_back(o):
        return (dp, lax.rem(me - o + n_ex, n_ex))

    barrier = pltpu.get_barrier_semaphore()
    position = dp * n_ex + me

    def along(offset):
        other = lax.rem(position + offset + n_dp * n_ex, n_dp * n_ex)
        return (other // n_ex, lax.rem(other, n_ex))

    others = (
        [sibling, up_y, down_y, (far_place, me), (far_place + 1, me)]
        + [peer(o) for o in range(1, n_ex)]
        + [along(o) for o in (-1, -2, 1, 2)]
    )
    for other in others:
        pl.semaphore_signal(barrier, inc=1, device_id=other, device_id_type=MESH)

    mine = pl.ds(pl.multiple_of(core * tokens, tokens), tokens)
    loads = [
        pltpu.make_async_copy(ids_hbm, ids, load_sem.at[0]),
        pltpu.make_async_copy(router_hbm, router, load_sem.at[1]),
        pltpu.make_async_copy(w_in_hbm, w_in, load_sem.at[2]),
        pltpu.make_async_copy(w_out_hbm, w_out, load_sem.at[3]),
    ]

    for copy in loads[:2]:
        copy.start()

    def enter():
        for copy in loads[2:]:
            copy.start()
        pl.semaphore_wait(barrier, len(others))

    started = []

    def send(source, target, s_sem, r_sem, device):
        copy = pltpu.make_async_remote_copy(
            src_ref=source, dst_ref=target, send_sem=s_sem, recv_sem=r_sem,
            device_id=device, device_id_type=MESH,
        )
        copy.start()
        started.append(copy)
        return copy

    def from_far(source, target, s_sem, r_sem):
        return pltpu.make_async_remote_copy(
            src_ref=source, dst_ref=target, send_sem=s_sem, recv_sem=r_sem,
            device_id=far_same, device_id_type=MESH,
        )

    lane_i = iota((tokens, 128), 1)

    def tell():
        loads[0].wait()
        named = [
            jnp.concatenate([as_column(ids[t, k:k + 1, :].astype(F32), rows) for t in range(steps)], axis=0)
            for k in range(2)
        ]
        told[core] = jnp.where(lane_i == 0, named[0], named[1])
        sent = [send(told.at[core], told.at[core], ids_s.at[0], ids_r.at[0], sibling)]
        for c in range(2):
            sent.append(send(told.at[core], told_far.at[core], ids_s.at[1 + c], ids_r.at[1 + core], (far_place + c, me)))
        return sent

    def prepare(sent):
        sent[0].wait_recv()
        for c in range(2):
            from_far(told.at[core], told_far.at[c], ids_s.at[1 + c], ids_r.at[1 + c]).wait_recv()
        lane_x = lane_i.astype(F32)
        lower = (iota((tokens, tokens), 1) < iota((tokens, tokens), 0)) & (
            iota((tokens, tokens), 0) // rows == iota((tokens, tokens), 1) // rows
        )
        lower = jnp.where(lower, 1.0, 0.0).astype(BF)
        step_of = (iota((tokens, 1), 0) // rows).astype(F32)
        lane_c = iota((tokens, chunk), 1).astype(F32)
        my_expert = me.astype(F32)
        for which, table in enumerate((told, told_far)):
            either = []
            for c in range(2):
                named = [table[c, :, k:k + 1] for k in range(2)]
                one_hot = [lane_x == n for n in named]
                before = bdot(lower, jnp.where(one_hot[0] | one_hot[1], 1.0, 0.0).astype(BF))
                hots = []
                for k in range(2):
                    spot = jnp.sum(jnp.where(one_hot[k], before, 0.0), axis=1, keepdims=True)
                    distance = named[k] - my_expert
                    distance = jnp.where(distance < 0.0, distance + n_ex, distance)
                    column = distance * slots + spot + step_of * cap + c * steps * cap
                    hots.append(jnp.where(lane_c == column, 1.0, 0.0))
                    hot[which, k, c * tokens:(c + 1) * tokens, :] = hots[k]
                either.append(hots[0] + hots[1])
            dispatch[which] = jnp.concatenate(either, axis=0).T.astype(BF)

    attention_part(n_dp, n_ex, *attention_args, residual, normed, mine, enter, tell, prepare)

    pair = [send(normed.at[mine], normed.at[mine], pair_s.at[0], pair_r.at[0], sibling)]
    far = [
        send(
            normed.at[mine, pl.ds(c * half, half)], normed_far.at[mine], far_s.at[c], far_r.at[core], (far_place + c, me)
        )
        for c in range(2)
    ]

    loads[1].wait()
    logits = tdot(normed[mine, :], router[...])
    lane_e = iota((tokens, n_ex), 1).astype(F32)
    picked = [
        jnp.sum(jnp.where(lane_e == told[core, :, k:k + 1], logits, 0.0), axis=1, keepdims=True) for k in range(2)
    ]
    info[core] = 1.0 / (1.0 + jnp.exp(picked[1] - picked[0])) + jnp.zeros((tokens, 128), F32)
    pair.append(send(info.at[core], info.at[core], pair_s.at[1], pair_r.at[1], sibling))
    for c in range(2):
        far.append(send(info.at[core], info_far.at[core], far_s.at[2 + c], far_r.at[2 + core], (far_place + c, me)))

    def mixed(which, table, back):
        gate = jnp.concatenate([table[c, :, 0:1] for c in range(2)], axis=0)
        gates = hot[which, 0] * gate + hot[which, 1] * (1.0 - gate)
        high = gates.astype(BF)
        return bdot(high, back) + bdot((gates - high.astype(F32)).astype(BF), back)

    def block(o):
        return pl.ds(o * slots, slots)

    def piece(g):
        return pl.ds(g * group, group)

    at_half = pl.ds(pl.multiple_of(core * half, half), half)
    pair[0].wait_recv()
    outgoing[...] = bdot(dispatch[0], normed[:, at_half]).astype(BF)
    arrivals = [None] + [
        send(outgoing.at[block(o)], xbuf.at[core, 0, block(o)], a2a_s.at[o], a2a_r.at[o], peer(o))
        for o in range(1, n_ex)
    ]
    xbuf[core, 0, block(0), :] = outgoing[block(0), :]
    for c in range(2):
        from_far(
            normed.at[mine, pl.ds(0, half)], normed_far.at[pl.ds(c * tokens, tokens)], far_s.at[c], far_r.at[c]
        ).wait_recv()
    outgoing_far[...] = bdot(dispatch[1], normed_far[...]).astype(BF)
    far_arrivals = [None] + [
        send(outgoing_far.at[block(o)], xbuf.at[core, 3, block(o)], far_a2a_s.at[o], far_a2a_r.at[o], peer(o))
        for o in range(1, n_ex)
    ]
    xbuf[core, 3, block(0), :] = outgoing_far[block(0), :]

    per_group = n_ex // 4

    def to_sibling(k, g):
        return send(
            xbuf.at[core, k, piece(g)], xbuf.at[core, k, piece(g)], sib_s.at[k, g], sib_r.at[k, g], sibling
        )

    def from_near(k, g):
        return 1 + g // 2, 2 * (k - 1) + g % 2

    tile = min(256, half, hidden_units)

    def first_product(k, slot):
        def first(j, carry):
            cols = pl.ds(pl.multiple_of(j * tile, tile), tile)
            a = bdot(xbuf[0, k], w_in[0:half, cols]) + bdot(xbuf[1, k], w_in[half:width, cols])
            units[slot, :, cols] = jnp.maximum(a, 0.0).astype(BF)
            return carry

        lax.fori_loop(0, hidden_units // tile, first, 0)

    def second_product(k, slot):
        def second(base, target):
            def step(j, carry):
                cols = pl.ds(pl.multiple_of(base + j * tile, tile), tile)
                target[k, :, pl.ds(pl.multiple_of(j * tile, tile), tile)] = bdot(
                    units[slot], w_out[:, cols]
                ).astype(BF)
                return carry

            lax.fori_loop(0, half // tile, step, 0)

        second((1 - core) * half, p_send)
        copy = send(p_send.at[k], p_back.at[k], part_s.at[k], part_r.at[k], sibling)
        second(core * half, p_mine)
        return copy

    def reduce_part(k):
        return p_mine[k].astype(F32) + p_back[k].astype(F32)

    sib, near, final = {}, {}, {}
    for g in range(4):
        for o in range(g * per_group, (g + 1) * per_group):
            if o:
                arrivals[o].wait_recv()
        for k in (1, 2):
            to_chunk, spot = from_near(k, g)
            near[k, g] = send(
                xbuf.at[core, 0, piece(g)], xbuf.at[core, to_chunk, piece(spot)],
                near_s.at[k - 1, g], near_r.at[k - 1, g], up_y if k == 1 else down_y,
            )
        sib[0, g] = to_sibling(0, g)
    loads[2].wait()
    loads[3].wait()
    for g in range(4):
        sib[0, g].wait_recv()
    first_product(0, 0)
    parts = {0: second_product(0, 0)}

    def near_arrived(h):
        for g in (2 * h, 2 * h + 1):
            for k in (1, 2):
                near[k, g].wait_recv()
                to_chunk, spot = from_near(k, g)
                sib[to_chunk, spot] = to_sibling(to_chunk, spot)

    def finish_near(h):
        parts[1 + h].wait()
        p_send[1 + h] = reduce_part(1 + h).astype(BF)
        for g in (2 * h, 2 * h + 1):
            for k in (1, 2):
                from_chunk, spot = from_near(k, g)
                final[k, g] = send(
                    p_send.at[from_chunk, piece(spot)], (fin_b if k == 1 else fin_a).at[piece(g)],
                    fin_s.at[k - 1, g], fin_r.at[k - 1, g], down_y if k == 1 else up_y,
                )

    near_arrived(0)
    for g in range(4):
        for o in range(g * per_group, (g + 1) * per_group):
            if o:
                far_arrivals[o].wait_recv()
        sib[3, g] = to_sibling(3, g)
    for spot in range(4):
        sib[1, spot].wait_recv()
    first_product(1, 1)
    parts[1] = second_product(1, 1)
    near_arrived(1)
    for g in range(4):
        sib[3, g].wait_recv()
    first_product(3, 0)
    parts[3] = second_product(3, 0)
    finish_near(0)
    for spot in range(4):
        sib[2, spot].wait_recv()
    parts[3].wait()
    p_mine[3] = reduce_part(3).astype(BF)
    far_replies = [None] + [
        send(
            p_mine.at[3, block(o)], returned_far.at[block(o)], far_ret_s.at[o], far_ret_r.at[o], peer_back(o)
        )
        for o in range(1, n_ex)
    ]
    returned_far[block(0), :] = p_mine[3, block(0), :]
    first_product(2, 1)
    parts[2] = second_product(2, 1)
    finish_near(1)
    parts[0].wait()
    home[...] = reduce_part(0)
    replies = [None] * n_ex

    def reply(groups):
        for g in groups:
            final[1, g].wait_recv()
            final[2, g].wait_recv()
            total = home[piece(g), :] + fin_a[piece(g), :].astype(F32) + fin_b[piece(g), :].astype(F32)
            p_mine[0, piece(g), :] = total.astype(BF)
            for o in range(g * per_group, (g + 1) * per_group):
                if o:
                    replies[o] = send(
                        p_mine.at[0, block(o)], returned.at[block(o)], ret_s.at[o], ret_r.at[o], peer_back(o)
                    )

    reply((0, 1, 2, 3))
    for o in range(1, n_ex):
        far_replies[o].wait_recv()
    back_far = returned_far[...]
    for c in range(2):
        from_far(info.at[core], info_far.at[c], far_s.at[2 + c], far_r.at[2 + c]).wait_recv()
    far_out[...] = mixed(1, info_far, back_far).astype(BF)
    far_home = send(far_out, far_in, far_s.at[4], far_r.at[4], far_same)

    returned[block(0), :] = p_mine[0, block(0), :]
    far_home.wait_recv()
    for o in range(1, n_ex):
        replies[o].wait_recv()
    back = returned[...]
    pair[1].wait_recv()
    y = mixed(0, info, back) + far_in[...].astype(F32)
    is_first = core == 0
    y_send[...] = jnp.where(is_first, y[tokens:], y[:tokens])
    swap = send(y_send, y_back, pair_s.at[2], pair_r.at[2], sibling)
    residual[:, at_half] = residual[:, at_half] + jnp.where(is_first, y[:tokens], y[tokens:])
    swap.wait_recv()
    at_other = pl.ds(pl.multiple_of((1 - core) * half, half), half)
    residual[:, at_other] = residual[:, at_other] + y_back[...]
    for t in range(steps):
        out_ref[t] = residual[t * rows:(t + 1) * rows, :].astype(BF)
    waited = {id(p) for p in parts.values()}
    for copy in started:
        if id(copy) not in waited:
            copy.wait_send()


def layer(hidden, q_self, k_new, v_new, q_cross, cache_keys, cache_values, cross_keys, cross_values,
          key_scale, value_scale, parents, expert_ids, norm_gain, router, w_in, w_out):
    steps, rows, width = hidden.shape
    heads = key_scale.shape[1]
    cache = cache_keys.shape[1]
    sentences, src = cross_keys.shape[:2]
    chunks = 4
    n_dp, n_ex = lax.axis_size("dp"), lax.axis_size("expert")
    part = width // chunks
    n_self, n_cross, slots = rows * cache, sentences * src, 4 * rows
    quarter = width // 4
    tokens = steps * rows
    hidden_units = w_in.shape[2]
    half = width // 2
    cap = 4 * rows // n_ex
    chunk_slots = n_ex * 2 * steps * cap
    dma = pltpu.SemaphoreType.DMA
    attention_scratch = [pltpu.VMEM((steps, rows, width), BF)] * 5 + [
            pltpu.VMEM((steps, rows), jnp.int32),
            pltpu.VMEM((sentences, heads), F32),
            pltpu.VMEM((sentences, heads), F32),
            pltpu.VMEM((1, width), F32),
            pltpu.VMEM((chunks, n_self, part), BF),
            pltpu.VMEM((chunks, n_self, part), BF),
            pltpu.VMEM((chunks, n_cross, part), BF),
            pltpu.VMEM((chunks, n_cross, part), BF),
            pltpu.VMEM((slots, width), BF),
            pltpu.VMEM((slots, width), F32),
            pltpu.VMEM((2 * rows, width), BF),
            pltpu.VMEM((2 * rows, width), F32),
            pltpu.VMEM((slots, n_self), F32),
            pltpu.VMEM((slots, 2 * rows), F32),
            pltpu.VMEM((2 * rows, n_cross), F32),
            pltpu.VMEM((2, 2 * rows, 128), F32),
            pltpu.VMEM((2, slots, 128), F32),
            pltpu.VMEM((8, 128), jnp.int32),
            pltpu.VMEM((2, 8, 128), jnp.int32),
            pltpu.VMEM((16, quarter), BF),
            pltpu.VMEM((16, quarter), BF),
            pltpu.VMEM((rows, width), BF),
            pltpu.VMEM((16, quarter), BF),
            pltpu.VMEM((16, quarter), BF),
            pltpu.VMEM((16, quarter), BF),
            pltpu.VMEM((16, quarter), BF),
            pltpu.VMEM((rows, width), BF),
            pltpu.VMEM((16, quarter), BF),
            pltpu.VMEM((16, quarter), BF),
            pltpu.VMEM((2, rows + 8, 128), F32),
            pltpu.VMEM((2, 8, 128), F32),
            pltpu.VMEM((heads // chunks, slots, n_self), F32),
            pltpu.VMEM((heads // chunks, slots, n_self), BF),
            pltpu.VMEM((heads // chunks, 2 * rows, n_cross), F32),
            pltpu.VMEM((heads // chunks, 2 * rows, n_cross), BF),
            pltpu.SemaphoreType.DMA((4, chunks)),
            pltpu.SemaphoreType.DMA((9,)),
            pltpu.SemaphoreType.DMA((10,)),
            pltpu.SemaphoreType.DMA((10,)),
        ]
    expert_scratch = [
            pltpu.VMEM((tokens, width), F32),
            pltpu.VMEM((2 * tokens, width), BF),
            pltpu.VMEM((steps, 2, rows), jnp.int32),
            pltpu.VMEM((2, tokens, 128), F32),
            pltpu.VMEM((2, tokens, 128), F32),
            pltpu.VMEM((2, 2, 2 * tokens, chunk_slots), F32),
            pltpu.VMEM((2, chunk_slots, 2 * tokens), BF),
            pltpu.VMEM((2, tokens, 128), F32),
            pltpu.VMEM((2, tokens, 128), F32),
            pltpu.VMEM((n_ex, width), BF),
            pltpu.VMEM((width, hidden_units), BF),
            pltpu.VMEM((hidden_units, width), BF),
            pltpu.VMEM((2 * tokens, half), BF),
            pltpu.VMEM((chunk_slots, half), BF),
            pltpu.VMEM((chunk_slots, half), BF),
            pltpu.VMEM((2, 4, chunk_slots, half), BF),
            pltpu.VMEM((2, chunk_slots, hidden_units), BF),
            pltpu.VMEM((4, chunk_slots, half), BF),
            pltpu.VMEM((4, chunk_slots, half), BF),
            pltpu.VMEM((4, chunk_slots, half), BF),
            pltpu.VMEM((chunk_slots, half), BF),
            pltpu.VMEM((chunk_slots, half), BF),
            pltpu.VMEM((chunk_slots, half), F32),
            pltpu.VMEM((chunk_slots, half), BF),
            pltpu.VMEM((chunk_slots, half), BF),
            pltpu.VMEM((2 * tokens, half), BF),
            pltpu.VMEM((2 * tokens, half), BF),
            pltpu.VMEM((tokens, half), F32),
            pltpu.VMEM((tokens, half), F32),
            dma((4,)), dma((3,)), dma((3,)), dma((3,)), dma((3,)), dma((5,)), dma((5,)), dma((n_ex,)), dma((n_ex,)),
            dma((n_ex,)), dma((n_ex,)), dma((2, 4)), dma((2, 4)), dma((4, 4)), dma((4, 4)), dma((4,)), dma((4,)),
            dma((2, 4)), dma((2, 4)), dma((n_ex,)), dma((n_ex,)), dma((n_ex,)), dma((n_ex,)),
    ]

    def kernel(*refs):
        layer_kernel(
            n_dp, n_ex, cap, refs[13:17],
            (rows, cache, src, rows // sentences, chunks, refs[0:13], refs[18]), refs[19], refs[17],
        )

    return pl.pallas_call(
        kernel,
        out_shape=jax.ShapeDtypeStruct((steps, rows, width), BF),
        in_specs=[pl.BlockSpec(memory_space=pl.ANY)] * 17,
        out_specs=pl.BlockSpec(memory_space=pltpu.VMEM),
        scratch_shapes=(tuple(attention_scratch), tuple(expert_scratch)),
        compiler_params=pltpu.CompilerParams(
            collective_id=0, has_side_effects=True, vmem_limit_bytes=60 * 2**20
        ),
    )(
        hidden, q_self, k_new, v_new, q_cross, parents, key_scale, value_scale, norm_gain.reshape(1, width),
        cache_keys.reshape(n_self, width), cache_values.reshape(n_self, width),
        cross_keys.reshape(n_cross, width), cross_values.reshape(n_cross, width),
        jnp.swapaxes(expert_ids, 1, 2), router.T,
        w_in.reshape(width, hidden_units), w_out.reshape(hidden_units, width),
    )


def solution(mesh):
    in_specs = (
        P(None, ("dp", "expert"), None),
        P(None, ("dp", "expert"), None),
        P(None, ("dp", "expert"), None),
        P(None, ("dp", "expert"), None),
        P(None, ("dp", "expert"), None),
        P(("dp", "expert"), None, None),
        P(("dp", "expert"), None, None),
        P(("dp", "expert"), None, None),
        P(("dp", "expert"), None, None),
        P(("dp", "expert"), None),
        P(("dp", "expert"), None),
        P(None, ("dp", "expert")),
        P(None, ("dp", "expert"), None),
        P(),
        P(),
        P("expert", None, "dp"),
        P("expert", "dp", None),
    )
    out_specs = P(None, ("dp", "expert"), None)
    return jax.shard_map(layer, mesh=mesh, in_specs=in_specs, out_specs=out_specs, check_vma=False)
```

```python
import functools
import math

import jax
import jax.numpy as jnp
from jax import lax
from jax.experimental import pallas as pl
from jax.experimental.pallas import tpu as pltpu
from jax.sharding import PartitionSpec as P

epsilon = 1e-05
MESH = pl.DeviceIdType.MESH
BF = jnp.bfloat16
F32 = jnp.float32
LOW = -1e30
FLOOR = -1e20


def iota(shape, dim):
    return lax.broadcasted_iota(jnp.int32, shape, dim)


def as_column(row, n):
    return jnp.sum(jnp.where(iota((n, n), 0) == iota((n, n), 1), row, 0.0), axis=1, keepdims=True)


def pick(row, index_col, n):
    lanes = iota((n, n), 1).astype(F32)
    return jnp.sum(jnp.where(lanes == index_col, row, 0.0), axis=1, keepdims=True)


def inside(value, start, n):
    return (value >= start) & (value < start + n)


def remote_rank(row, start, n):
    far = jnp.where(inside(row, start, n), 0.0, 1.0)
    far_col = as_column(far, n)
    rank = jnp.sum(jnp.where(iota((n, n), 0) < iota((n, n), 1), far_col, 0.0), axis=0, keepdims=True)
    return far, rank


def bdot(a, b):
    return lax.dot_general(a, b, (((1,), (0,)), ((), ())), preferred_element_type=F32)


def tdot(a, b):
    return lax.dot_general(a, b, (((1,), (1,)), ((), ())), preferred_element_type=F32)


def attention_part(n_dp, n_ex, rows, cache, src, beams, chunks, inputs, scratch, residual, normed, first_row, enter, tell, prepare):
    (
        hidden_hbm, q_self_hbm, k_new_hbm, v_new_hbm, q_cross_hbm, parents_hbm, ks_hbm, vs_hbm, gain_hbm,
        ck_hbm, cv_hbm, xk_hbm, xv_hbm,
    ) = inputs
    (
    hidden, q_self, k_new, v_new, q_cross, parents, key_scale, value_scale, gain,
    kbuf, vbuf, xkbuf, xvbuf, q_all, o_all, o_send, x_out, bias, bias_e, bias_x, scales,
    stat, par_own, par_in, q_d, q_e, in_c, in_d, in_e, o_d, o_e, back_c, back_d, back_e, stat_in, stat_in2,
    s_self, w_self, s_cross, w_cross, load_sem, small_sem, send_sem, recv_sem,
    ) = scratch
    width = hidden.shape[2]
    heads = key_scale.shape[1]
    size = width // heads
    per_chunk = heads // chunks
    quarter = width // 4
    n_dev = n_dp * n_ex
    me = lax.axis_index("dp") * n_ex + lax.axis_index("expert")

    def at(offset):
        other = lax.rem(me + offset + n_dev, n_dev)
        return (other // n_ex, lax.rem(other, n_ex))

    def load(k, c, source, buffer):
        part = width // chunks
        return pltpu.make_async_copy(
            source.at[:, pl.ds(pl.multiple_of(c * part, part), part)], buffer.at[c], load_sem.at[k, c]
        )

    small = [
        pltpu.make_async_copy(source, target, small_sem.at[i])
        for i, (source, target) in enumerate((
            (parents_hbm, parents), (q_self_hbm, q_self), (k_new_hbm, k_new), (v_new_hbm, v_new),
            (ks_hbm, key_scale), (vs_hbm, value_scale), (q_cross_hbm, q_cross), (hidden_hbm, hidden),
            (gain_hbm, gain),
        ))
    ]
    for copy in small:
        copy.start()
    early = chunks // 2
    for c in range(early):
        load(2, c, xk_hbm, xkbuf).start()
        load(3, c, xv_hbm, xvbuf).start()
    for c in range(chunks):
        load(0, c, ck_hbm, kbuf).start()
        load(1, c, cv_hbm, vbuf).start()
    for c in range(early, chunks):
        load(2, c, xk_hbm, xkbuf).start()
        load(3, c, xv_hbm, xvbuf).start()

    par_own[...] = jnp.zeros_like(par_own)
    small[0].wait()
    small[1].wait()
    par_own[0:2, 0:rows] = parents[...]
    own = (me * rows).astype(F32)
    after = (lax.rem(me + 1, n_dev) * rows).astype(F32)
    after2 = (lax.rem(me + 2, n_dev) * rows).astype(F32)
    p0 = parents[0:1, :].astype(F32)
    p1 = parents[1:2, :].astype(F32)
    far0, rank0 = remote_rank(p0, own, rows)
    far1, rank1 = remote_rank(p1, own, rows)
    far0_col, rank0_col = as_column(far0, rows), as_column(rank0, rows)
    far1_col, rank1_col = as_column(far1, rows), as_column(rank1, rows)
    sub = iota((16, rows), 0)
    lane = iota((rows, 16), 1)

    def compact(value, far, rank):
        total = jnp.zeros((16, quarter), F32)
        for k in range(4):
            hot = ((sub >> 2) == k) & ((sub & 3).astype(F32) == rank) & (far > 0.5)
            total += bdot(jnp.where(hot, 1.0, 0.0).astype(BF), value[:, k * quarter:(k + 1) * quarter])
        return total.astype(BF)

    q_d[...] = compact(q_self[0], far0, rank0)
    q_e[...] = compact(q_self[1], far1, rank1)

    def remote(source, target, number, offset):
        return pltpu.make_async_remote_copy(
            src_ref=source, dst_ref=target, send_sem=send_sem.at[number], recv_sem=recv_sem.at[number],
            device_id=at(offset), device_id_type=MESH,
        )

    out_copies = [
        remote(par_own, par_in.at[0], 0, -1),
        remote(par_own, par_in.at[1], 1, -2),
        remote(q_d, in_d, 2, -1),
        remote(q_e, in_e, 3, -2),
        remote(q_self.at[1], in_c, 4, -1),
    ]
    enter()
    for copy in out_copies:
        copy.start()
    sent = tell()

    small[4].wait()
    small[5].wait()
    sentence = (iota((2 * rows, 1), 0) & (rows - 1)) // beams
    ks = jnp.zeros((2 * rows, heads), F32)
    vs = jnp.zeros((2 * rows, heads), F32)
    for s in range(rows // beams):
        ks = jnp.where(sentence == s, key_scale[s:s + 1, :], ks)
        vs = jnp.where(sentence == s, value_scale[s:s + 1, :], vs)
    root = 1.0 / math.sqrt(size)
    scales[0, :, 0:heads] = ks * root
    scales[1, :, 0:heads] = vs
    n_cross = (rows // beams) * src
    bias_x[...] = jnp.where(
        iota((2 * rows, n_cross), 1) // src == (iota((2 * rows, n_cross), 0) & (rows - 1)) // beams, 0.0, LOW
    )
    def cross_chunk(c, carry):
        load(2, c, xk_hbm, xkbuf).wait()
        load(3, c, xv_hbm, xvbuf).wait()
        lanes_x = iota((2 * rows, 128), 1)
        heads_at = [pl.ds(pl.multiple_of((c * per_chunk + j) * size, size), size) for j in range(per_chunk)]
        for j in range(per_chunk):
            ks_h = jnp.sum(jnp.where(lanes_x == c * per_chunk + j, scales[0], 0.0), axis=1, keepdims=True)
            q = jnp.concatenate([q_cross[0, :, heads_at[j]], q_cross[1, :, heads_at[j]]], axis=0)
            s_cross[j] = tdot(q, xkbuf[c, :, j * size:(j + 1) * size]) * ks_h + bias_x[...]
        totals = []
        for j in range(per_chunk):
            s = s_cross[j]
            w = jnp.exp(s - jnp.max(s, axis=1, keepdims=True))
            totals.append(jnp.sum(w, axis=1, keepdims=True))
            w_cross[j] = w.astype(BF)
        for j in range(per_chunk):
            vs_h = jnp.sum(jnp.where(lanes_x == c * per_chunk + j, scales[1], 0.0), axis=1, keepdims=True)
            o = bdot(w_cross[j], xvbuf[c, :, j * size:(j + 1) * size])
            x_out[:, heads_at[j]] = o * (vs_h / totals[j])
        return carry

    small[6].wait()
    lax.fori_loop(0, early, cross_chunk, 0)
    q_all[0:rows, :] = q_self[0]
    q_all[rows:2 * rows, :] = q_self[1]

    for i in (2, 3, 7, 8):
        small[i].wait()
    for copy in out_copies:
        copy.wait()
    q_all[2 * rows:3 * rows, :] = in_c[...]
    a16, b16 = iota((16, 16), 0), iota((16, 16), 1)
    for k in range(4):
        take_d = jnp.where((b16 == a16 + 4 * k) & (a16 < 4), 1.0, 0.0).astype(BF)
        take_e = jnp.where((b16 == a16 - 4 + 4 * k) & (a16 >= 4) & (a16 < 8), 1.0, 0.0).astype(BF)
        q_all[3 * rows:4 * rows, k * quarter:(k + 1) * quarter] = (
            bdot(take_d, in_d[...]) + bdot(take_e, in_e[...])
        ).astype(BF)

    n0 = par_in[0, 0:1, 0:rows].astype(F32)
    n1 = par_in[0, 1:2, 0:rows].astype(F32)
    m1 = par_in[1, 1:2, 0:rows].astype(F32)
    p0_col, p1_col = as_column(p0, rows), as_column(p1, rows)
    n1_col = as_column(n1, rows)
    index = iota((rows, 1), 0).astype(F32)
    none = jnp.full((rows, 1), -1000.0, F32)

    def local(value):
        return jnp.where(inside(value, own, rows), value - own, -1.0)

    own_b = p1_col - own
    in_own = inside(p1_col, own, rows)
    row_b = jnp.where(in_own, local(pick(p0, own_b, rows)), -1.0)
    first_b = jnp.where(in_own, own_b, -1.0)
    in_next = inside(n1_col, after, rows)
    in_here = inside(n1_col, own, rows)
    row_c = jnp.where(
        in_next,
        local(pick(n0, n1_col - after, rows)),
        jnp.where(in_here, local(pick(p0, n1_col - own, rows)), -1.0),
    )
    first_c = jnp.where(in_here & jnp.logical_not(in_next), n1_col - own, -1.0)
    far_n, rank_n = remote_rank(n0, after, rows)
    far_m, rank_m = remote_rank(m1, after2, rows)
    i_col = iota((rows, rows), 0).astype(F32)
    val_d = jnp.sum(jnp.where((rank_n == i_col) & (far_n > 0.5), n0, 0.0), axis=1, keepdims=True)
    val_e = jnp.sum(jnp.where((rank_m == i_col - 4.0) & (far_m > 0.5), m1, 0.0), axis=1, keepdims=True)
    row_de = jnp.where(
        index < 4.0,
        local(val_d),
        jnp.where(
            (index < 8.0) & inside(val_e, after, rows), local(pick(n0, val_e - after, rows)), -1.0
        ),
    )
    row_sel = jnp.concatenate([local(p0_col), row_b, row_c, row_de], axis=0)
    first_sel = jnp.concatenate([index, first_b, first_c, none], axis=0)
    second_sel = jnp.concatenate([none, index, none, none], axis=0)
    slots = 4 * rows
    bias[...] = jnp.where((iota((slots, rows * cache), 1) // cache).astype(F32) == row_sel, 0.0, LOW)
    lane_e = iota((slots, 2 * rows), 1).astype(F32)
    bias_e[...] = jnp.where((lane_e == first_sel) | (lane_e - rows == second_sel), 0.0, LOW)

    stat[...] = jnp.zeros_like(stat)
    lanes = iota((slots, 128), 1)

    def self_chunk(c, carry):
        load(0, c, ck_hbm, kbuf).wait()
        load(1, c, cv_hbm, vbuf).wait()
        heads_at = [pl.ds(pl.multiple_of((c * per_chunk + j) * size, size), size) for j in range(per_chunk)]
        extras = []
        for j in range(per_chunk):
            q = q_all[:, heads_at[j]]
            k_extra = jnp.concatenate([k_new[0, :, heads_at[j]], k_new[1, :, heads_at[j]]], axis=0)
            s_self[j] = tdot(q, kbuf[c, :, j * size:(j + 1) * size]) * root + bias[...]
            extras.append(tdot(q, k_extra) * root + bias_e[...])
        for j in range(per_chunk):
            s, s_e = s_self[j], extras[j]
            top = jnp.maximum(
                jnp.maximum(jnp.max(s, axis=1, keepdims=True), jnp.max(s_e, axis=1, keepdims=True)), FLOOR
            )
            w = jnp.exp(s - top)
            w_e = jnp.exp(s_e - top)
            total = jnp.sum(w, axis=1, keepdims=True) + jnp.sum(w_e, axis=1, keepdims=True)
            w_self[j] = w.astype(BF)
            extras[j] = w_e.astype(BF)
            here = lanes == c * per_chunk + j
            stat[0] = jnp.where(here, top, stat[0])
            stat[1] = jnp.where(here, total, stat[1])
        for j in range(per_chunk):
            v_extra = jnp.concatenate([v_new[0, :, heads_at[j]], v_new[1, :, heads_at[j]]], axis=0)
            o_all[:, heads_at[j]] = bdot(w_self[j], vbuf[c, :, j * size:(j + 1) * size]) + bdot(
                extras[j], v_extra
            )
        return carry

    lax.fori_loop(0, chunks, self_chunk, 0)

    o_send[...] = o_all[2 * rows:4 * rows, :].astype(BF)
    total_d = jnp.zeros((16, quarter), F32)
    total_e = jnp.zeros((16, quarter), F32)
    for k in range(4):
        piece = o_send[rows:2 * rows, k * quarter:(k + 1) * quarter]
        put_d = jnp.where(((a16 >> 2) == k) & (b16 == (a16 & 3)), 1.0, 0.0).astype(BF)
        put_e = jnp.where(((a16 >> 2) == k) & (b16 == (a16 & 3) + 4), 1.0, 0.0).astype(BF)
        total_d += bdot(put_d, piece)
        total_e += bdot(put_e, piece)
    o_d[...] = total_d.astype(BF)
    o_e[...] = total_e.astype(BF)
    back_copies = [
        remote(o_send.at[pl.ds(0, rows)], back_c, 5, 1),
        remote(o_d, back_d, 6, 1),
        remote(o_e, back_e, 7, 2),
        remote(stat.at[:, pl.ds(2 * rows, rows + 8)], stat_in, 8, 1),
        remote(stat.at[:, pl.ds(3 * rows, 8)], stat_in2, 9, 2),
    ]
    for copy in back_copies:
        copy.start()

    prepare(sent)
    lax.fori_loop(early, chunks, cross_chunk, 0)

    for copy in back_copies:
        copy.wait()

    def spread(compact_ref, far_col, rank_col):
        pieces = []
        for k in range(4):
            hot = ((lane >> 2) == k) & ((lane & 3).astype(F32) == rank_col) & (far_col > 0.5)
            pieces.append(bdot(jnp.where(hot, 1.0, 0.0).astype(BF), compact_ref[...]))
        return pieces

    def spread_stat(ref, start, far_col, rank_col):
        top = jnp.where(far_col > 0.5, 0.0, FLOOR) + jnp.zeros((rows, 128), F32)
        total = jnp.zeros((rows, 128), F32)
        for j in range(4):
            hot = (rank_col == float(j)) & (far_col > 0.5)
            top += jnp.where(hot, ref[0, start + j:start + j + 1, :], 0.0)
            total += jnp.where(hot, ref[1, start + j:start + j + 1, :], 0.0)
        return top, total

    o_far0 = spread(back_d, far0_col, rank0_col)
    o_far1 = spread(back_e, far1_col, rank1_col)
    stats0 = [
        (stat[0, 0:rows, :], stat[1, 0:rows, :]),
        spread_stat(stat_in, rows, far0_col, rank0_col),
    ]
    stats1 = [
        (stat[0, rows:2 * rows, :], stat[1, rows:2 * rows, :]),
        (stat_in[0, 0:rows, :], stat_in[1, 0:rows, :]),
        spread_stat(stat_in2, 4, far1_col, rank1_col),
    ]

    def weights(stats):
        top = stats[0][0]
        for t, _ in stats[1:]:
            top = jnp.maximum(top, t)
        parts = [jnp.exp(t - top) for t, _ in stats]
        total = sum(w * l for w, (_, l) in zip(parts, stats))
        return [w / total for w in parts]

    w0 = weights(stats0)
    w1 = weights(stats1)
    per_quarter = heads // 4
    for t in range(2):
        for h in range(heads):
            at_h = slice(h * size, (h + 1) * size)
            k, j = h // per_quarter, h % per_quarter
            inner = slice(j * size, (j + 1) * size)
            if t == 0:
                mixed = o_all[0:rows, at_h] * w0[0][:, h:h + 1] + o_far0[k][:, inner] * w0[1][:, h:h + 1]
            else:
                mixed = (
                    o_all[rows:2 * rows, at_h] * w1[0][:, h:h + 1]
                    + back_c[:, at_h].astype(F32) * w1[1][:, h:h + 1]
                    + o_far1[k][:, inner] * w1[2][:, h:h + 1]
                )
            residual[t * rows:(t + 1) * rows, at_h] = (
                hidden[t, :, at_h].astype(F32) + mixed + x_out[t * rows:(t + 1) * rows, at_h]
            )
    value = residual[...]
    average = jnp.mean(value, axis=1, keepdims=True)
    centered = value - average
    variance = jnp.mean(centered * centered, axis=1, keepdims=True)
    normed[first_row, :] = (centered * lax.rsqrt(variance + epsilon) * gain[...]).astype(BF)


def layer_kernel(
    n_dp, n_ex, cap,
    inputs, attention_args, scratch, out_ref,
):
    ids_hbm, router_hbm, w_in_hbm, w_out_hbm = inputs
    (
        residual, normed, ids, told, told_far, hot, dispatch, info, info_far, router, w_in, w_out, normed_far, outgoing, outgoing_far,
        xbuf, units, p_mine, p_send, p_back, fin_a, fin_b, home, returned, returned_far,
        far_out, far_in, y_send, y_back,
        load_sem, ids_s, ids_r, pair_s, pair_r, far_s, far_r, a2a_s, a2a_r, far_a2a_s, far_a2a_r, near_s, near_r, sib_s, sib_r,
        part_s, part_r, fin_s, fin_r, ret_s, ret_r, far_ret_s, far_ret_r,
    ) = scratch
    steps, rows = ids.shape[0], ids.shape[2]
    tokens = steps * rows
    width = residual.shape[1]
    half = width // 2
    hidden_units = w_in.shape[1]
    slots = 2 * steps * cap
    chunk = n_ex * slots
    group = chunk // 4
    dp = lax.axis_index("dp")
    me = lax.axis_index("expert")
    core = lax.rem(dp, 2)
    n_y = n_dp // 2
    place = dp // 2
    sibling = (dp + 1 - 2 * core, me)
    up_y = (lax.rem(place + 1, n_y) * 2 + core, me)
    down_y = (lax.rem(place + n_y - 1, n_y) * 2 + core, me)
    far_place = lax.rem(place + 2, n_y) * 2
    far_same = (far_place + core, me)

    def peer(o):
        return (dp, lax.rem(me + o, n_ex))

    def peer_back(o):
        return (dp, lax.rem(me - o + n_ex, n_ex))

    barrier = pltpu.get_barrier_semaphore()
    position = dp * n_ex + me

    def along(offset):
        other = lax.rem(position + offset + n_dp * n_ex, n_dp * n_ex)
        return (other // n_ex, lax.rem(other, n_ex))

    others = (
        [sibling, up_y, down_y, (far_place, me), (far_place + 1, me)]
        + [peer(o) for o in range(1, n_ex)]
        + [along(o) for o in (-1, -2, 1, 2)]
    )
    for other in others:
        pl.semaphore_signal(barrier, inc=1, device_id=other, device_id_type=MESH)

    mine = pl.ds(pl.multiple_of(core * tokens, tokens), tokens)
    loads = [
        pltpu.make_async_copy(ids_hbm, ids, load_sem.at[0]),
        pltpu.make_async_copy(router_hbm, router, load_sem.at[1]),
        pltpu.make_async_copy(w_in_hbm, w_in, load_sem.at[2]),
        pltpu.make_async_copy(w_out_hbm, w_out, load_sem.at[3]),
    ]

    for copy in loads[:2]:
        copy.start()

    def enter():
        for copy in loads[2:]:
            copy.start()
        pl.semaphore_wait(barrier, len(others))

    started = []

    def send(source, target, s_sem, r_sem, device):
        copy = pltpu.make_async_remote_copy(
            src_ref=source, dst_ref=target, send_sem=s_sem, recv_sem=r_sem,
            device_id=device, device_id_type=MESH,
        )
        copy.start()
        started.append(copy)
        return copy

    def from_far(source, target, s_sem, r_sem):
        return pltpu.make_async_remote_copy(
            src_ref=source, dst_ref=target, send_sem=s_sem, recv_sem=r_sem,
            device_id=far_same, device_id_type=MESH,
        )

    lane_i = iota((tokens, 128), 1)

    def tell():
        loads[0].wait()
        named = [
            jnp.concatenate([as_column(ids[t, k:k + 1, :].astype(F32), rows) for t in range(steps)], axis=0)
            for k in range(2)
        ]
        told[core] = jnp.where(lane_i == 0, named[0], named[1])
        sent = [send(told.at[core], told.at[core], ids_s.at[0], ids_r.at[0], sibling)]
        for c in range(2):
            sent.append(send(told.at[core], told_far.at[core], ids_s.at[1 + c], ids_r.at[1 + core], (far_place + c, me)))
        return sent

    def prepare(sent):
        sent[0].wait_recv()
        for c in range(2):
            from_far(told.at[core], told_far.at[c], ids_s.at[1 + c], ids_r.at[1 + c]).wait_recv()
        lane_x = lane_i.astype(F32)
        lower = (iota((tokens, tokens), 1) < iota((tokens, tokens), 0)) & (
            iota((tokens, tokens), 0) // rows == iota((tokens, tokens), 1) // rows
        )
        lower = jnp.where(lower, 1.0, 0.0).astype(BF)
        step_of = (iota((tokens, 1), 0) // rows).astype(F32)
        lane_c = iota((tokens, chunk), 1).astype(F32)
        my_expert = me.astype(F32)
        for which, table in enumerate((told, told_far)):
            either = []
            for c in range(2):
                named = [table[c, :, k:k + 1] for k in range(2)]
                one_hot = [lane_x == n for n in named]
                before = bdot(lower, jnp.where(one_hot[0] | one_hot[1], 1.0, 0.0).astype(BF))
                hots = []
                for k in range(2):
                    spot = jnp.sum(jnp.where(one_hot[k], before, 0.0), axis=1, keepdims=True)
                    distance = named[k] - my_expert
                    distance = jnp.where(distance < 0.0, distance + n_ex, distance)
                    column = distance * slots + spot + step_of * cap + c * steps * cap
                    hots.append(jnp.where(lane_c == column, 1.0, 0.0))
                    hot[which, k, c * tokens:(c + 1) * tokens, :] = hots[k]
                either.append(hots[0] + hots[1])
            dispatch[which] = jnp.concatenate(either, axis=0).T.astype(BF)

    attention_part(n_dp, n_ex, *attention_args, residual, normed, mine, enter, tell, prepare)

    pair = [send(normed.at[mine], normed.at[mine], pair_s.at[0], pair_r.at[0], sibling)]
    far = [
        send(
            normed.at[mine, pl.ds(c * half, half)], normed_far.at[mine], far_s.at[c], far_r.at[core], (far_place + c, me)
        )
        for c in range(2)
    ]

    loads[1].wait()
    logits = tdot(normed[mine, :], router[...])
    lane_e = iota((tokens, n_ex), 1).astype(F32)
    picked = [
        jnp.sum(jnp.where(lane_e == told[core, :, k:k + 1], logits, 0.0), axis=1, keepdims=True) for k in range(2)
    ]
    info[core] = 1.0 / (1.0 + jnp.exp(picked[1] - picked[0])) + jnp.zeros((tokens, 128), F32)
    pair.append(send(info.at[core], info.at[core], pair_s.at[1], pair_r.at[1], sibling))
    for c in range(2):
        far.append(send(info.at[core], info_far.at[core], far_s.at[2 + c], far_r.at[2 + core], (far_place + c, me)))

    def mixed(which, table, back):
        gate = jnp.concatenate([table[c, :, 0:1] for c in range(2)], axis=0)
        gates = hot[which, 0] * gate + hot[which, 1] * (1.0 - gate)
        high = gates.astype(BF)
        return bdot(high, back) + bdot((gates - high.astype(F32)).astype(BF), back)

    def block(o):
        return pl.ds(o * slots, slots)

    def piece(g):
        return pl.ds(g * group, group)

    at_half = pl.ds(pl.multiple_of(core * half, half), half)
    pair[0].wait_recv()
    outgoing[...] = bdot(dispatch[0], normed[:, at_half]).astype(BF)
    arrivals = [None] + [
        send(outgoing.at[block(o)], xbuf.at[core, 0, block(o)], a2a_s.at[o], a2a_r.at[o], peer(o))
        for o in range(1, n_ex)
    ]
    xbuf[core, 0, block(0), :] = outgoing[block(0), :]
    for c in range(2):
        from_far(
            normed.at[mine, pl.ds(0, half)], normed_far.at[pl.ds(c * tokens, tokens)], far_s.at[c], far_r.at[c]
        ).wait_recv()
    outgoing_far[...] = bdot(dispatch[1], normed_far[...]).astype(BF)
    far_arrivals = [None] + [
        send(outgoing_far.at[block(o)], xbuf.at[core, 3, block(o)], far_a2a_s.at[o], far_a2a_r.at[o], peer(o))
        for o in range(1, n_ex)
    ]
    xbuf[core, 3, block(0), :] = outgoing_far[block(0), :]

    per_group = n_ex // 4

    def to_sibling(k, g):
        return send(
            xbuf.at[core, k, piece(g)], xbuf.at[core, k, piece(g)], sib_s.at[k, g], sib_r.at[k, g], sibling
        )

    def from_near(k, g):
        return 1 + g // 2, 2 * (k - 1) + g % 2

    tile = min(1024, half, hidden_units)

    def first_product(k, slot):
        def first(j, carry):
            cols = pl.ds(pl.multiple_of(j * tile, tile), tile)
            a = bdot(xbuf[0, k], w_in[0:half, cols]) + bdot(xbuf[1, k], w_in[half:width, cols])
            units[slot, :, cols] = jnp.maximum(a, 0.0).astype(BF)
            return carry

        lax.fori_loop(0, hidden_units // tile, first, 0)

    def second_product(k, slot):
        def second(base, target):
            def step(j, carry):
                cols = pl.ds(pl.multiple_of(base + j * tile, tile), tile)
                target[k, :, pl.ds(pl.multiple_of(j * tile, tile), tile)] = bdot(
                    units[slot], w_out[:, cols]
                ).astype(BF)
                return carry

            lax.fori_loop(0, half // tile, step, 0)

        second((1 - core) * half, p_send)
        copy = send(p_send.at[k], p_back.at[k], part_s.at[k], part_r.at[k], sibling)
        second(core * half, p_mine)
        return copy

    def reduce_part(k):
        return p_mine[k].astype(F32) + p_back[k].astype(F32)

    sib, near, final = {}, {}, {}
    for g in range(4):
        for o in range(g * per_group, (g + 1) * per_group):
            if o:
                arrivals[o].wait_recv()
        for k in (1, 2):
            to_chunk, spot = from_near(k, g)
            near[k, g] = send(
                xbuf.at[core, 0, piece(g)], xbuf.at[core, to_chunk, piece(spot)],
                near_s.at[k - 1, g], near_r.at[k - 1, g], up_y if k == 1 else down_y,
            )
        sib[0, g] = to_sibling(0, g)
    loads[2].wait()
    loads[3].wait()
    for g in range(4):
        sib[0, g].wait_recv()
    first_product(0, 0)
    parts = {0: second_product(0, 0)}

    def near_arrived(h):
        for g in (2 * h, 2 * h + 1):
            for k in (1, 2):
                near[k, g].wait_recv()
                to_chunk, spot = from_near(k, g)
                sib[to_chunk, spot] = to_sibling(to_chunk, spot)

    def finish_near(h):
        parts[1 + h].wait()
        p_send[1 + h] = reduce_part(1 + h).astype(BF)
        for g in (2 * h, 2 * h + 1):
            for k in (1, 2):
                from_chunk, spot = from_near(k, g)
                final[k, g] = send(
                    p_send.at[from_chunk, piece(spot)], (fin_b if k == 1 else fin_a).at[piece(g)],
                    fin_s.at[k - 1, g], fin_r.at[k - 1, g], down_y if k == 1 else up_y,
                )

    near_arrived(0)
    for g in range(4):
        for o in range(g * per_group, (g + 1) * per_group):
            if o:
                far_arrivals[o].wait_recv()
        sib[3, g] = to_sibling(3, g)
    for spot in range(4):
        sib[1, spot].wait_recv()
    first_product(1, 1)
    parts[1] = second_product(1, 1)
    near_arrived(1)
    for g in range(4):
        sib[3, g].wait_recv()
    first_product(3, 0)
    parts[3] = second_product(3, 0)
    finish_near(0)
    for spot in range(4):
        sib[2, spot].wait_recv()
    parts[3].wait()
    p_mine[3] = reduce_part(3).astype(BF)
    far_replies = [None] + [
        send(
            p_mine.at[3, block(o)], returned_far.at[block(o)], far_ret_s.at[o], far_ret_r.at[o], peer_back(o)
        )
        for o in range(1, n_ex)
    ]
    returned_far[block(0), :] = p_mine[3, block(0), :]
    first_product(2, 1)
    parts[2] = second_product(2, 1)
    finish_near(1)
    parts[0].wait()
    home[...] = reduce_part(0)
    replies = [None] * n_ex

    def reply(groups):
        for g in groups:
            final[1, g].wait_recv()
            final[2, g].wait_recv()
            total = home[piece(g), :] + fin_a[piece(g), :].astype(F32) + fin_b[piece(g), :].astype(F32)
            p_mine[0, piece(g), :] = total.astype(BF)
            for o in range(g * per_group, (g + 1) * per_group):
                if o:
                    replies[o] = send(
                        p_mine.at[0, block(o)], returned.at[block(o)], ret_s.at[o], ret_r.at[o], peer_back(o)
                    )

    reply((0, 1, 2, 3))
    for o in range(1, n_ex):
        far_replies[o].wait_recv()
    back_far = returned_far[...]
    for c in range(2):
        from_far(info.at[core], info_far.at[c], far_s.at[2 + c], far_r.at[2 + c]).wait_recv()
    far_out[...] = mixed(1, info_far, back_far).astype(BF)
    far_home = send(far_out, far_in, far_s.at[4], far_r.at[4], far_same)

    returned[block(0), :] = p_mine[0, block(0), :]
    far_home.wait_recv()
    for o in range(1, n_ex):
        replies[o].wait_recv()
    back = returned[...]
    pair[1].wait_recv()
    y = mixed(0, info, back) + far_in[...].astype(F32)
    is_first = core == 0
    y_send[...] = jnp.where(is_first, y[tokens:], y[:tokens])
    swap = send(y_send, y_back, pair_s.at[2], pair_r.at[2], sibling)
    residual[:, at_half] = residual[:, at_half] + jnp.where(is_first, y[:tokens], y[tokens:])
    swap.wait_recv()
    at_other = pl.ds(pl.multiple_of((1 - core) * half, half), half)
    residual[:, at_other] = residual[:, at_other] + y_back[...]
    for t in range(steps):
        out_ref[t] = residual[t * rows:(t + 1) * rows, :].astype(BF)
    waited = {id(p) for p in parts.values()}
    for copy in started:
        if id(copy) not in waited:
            copy.wait_send()


def layer(hidden, q_self, k_new, v_new, q_cross, cache_keys, cache_values, cross_keys, cross_values,
          key_scale, value_scale, parents, expert_ids, norm_gain, router, w_in, w_out):
    steps, rows, width = hidden.shape
    heads = key_scale.shape[1]
    cache = cache_keys.shape[1]
    sentences, src = cross_keys.shape[:2]
    chunks = 4
    n_dp, n_ex = lax.axis_size("dp"), lax.axis_size("expert")
    part = width // chunks
    n_self, n_cross, slots = rows * cache, sentences * src, 4 * rows
    quarter = width // 4
    tokens = steps * rows
    hidden_units = w_in.shape[2]
    half = width // 2
    cap = 4 * rows // n_ex
    chunk_slots = n_ex * 2 * steps * cap
    dma = pltpu.SemaphoreType.DMA
    attention_scratch = [pltpu.VMEM((steps, rows, width), BF)] * 5 + [
            pltpu.VMEM((steps, rows), jnp.int32),
            pltpu.VMEM((sentences, heads), F32),
            pltpu.VMEM((sentences, heads), F32),
            pltpu.VMEM((1, width), F32),
            pltpu.VMEM((chunks, n_self, part), BF),
            pltpu.VMEM((chunks, n_self, part), BF),
            pltpu.VMEM((chunks, n_cross, part), BF),
            pltpu.VMEM((chunks, n_cross, part), BF),
            pltpu.VMEM((slots, width), BF),
            pltpu.VMEM((slots, width), F32),
            pltpu.VMEM((2 * rows, width), BF),
            pltpu.VMEM((2 * rows, width), F32),
            pltpu.VMEM((slots, n_self), F32),
            pltpu.VMEM((slots, 2 * rows), F32),
            pltpu.VMEM((2 * rows, n_cross), F32),
            pltpu.VMEM((2, 2 * rows, 128), F32),
            pltpu.VMEM((2, slots, 128), F32),
            pltpu.VMEM((8, 128), jnp.int32),
            pltpu.VMEM((2, 8, 128), jnp.int32),
            pltpu.VMEM((16, quarter), BF),
            pltpu.VMEM((16, quarter), BF),
            pltpu.VMEM((rows, width), BF),
            pltpu.VMEM((16, quarter), BF),
            pltpu.VMEM((16, quarter), BF),
            pltpu.VMEM((16, quarter), BF),
            pltpu.VMEM((16, quarter), BF),
            pltpu.VMEM((rows, width), BF),
            pltpu.VMEM((16, quarter), BF),
            pltpu.VMEM((16, quarter), BF),
            pltpu.VMEM((2, rows + 8, 128), F32),
            pltpu.VMEM((2, 8, 128), F32),
            pltpu.VMEM((heads // chunks, slots, n_self), F32),
            pltpu.VMEM((heads // chunks, slots, n_self), BF),
            pltpu.VMEM((heads // chunks, 2 * rows, n_cross), F32),
            pltpu.VMEM((heads // chunks, 2 * rows, n_cross), BF),
            pltpu.SemaphoreType.DMA((4, chunks)),
            pltpu.SemaphoreType.DMA((9,)),
            pltpu.SemaphoreType.DMA((10,)),
            pltpu.SemaphoreType.DMA((10,)),
        ]
    expert_scratch = [
            pltpu.VMEM((tokens, width), F32),
            pltpu.VMEM((2 * tokens, width), BF),
            pltpu.VMEM((steps, 2, rows), jnp.int32),
            pltpu.VMEM((2, tokens, 128), F32),
            pltpu.VMEM((2, tokens, 128), F32),
            pltpu.VMEM((2, 2, 2 * tokens, chunk_slots), F32),
            pltpu.VMEM((2, chunk_slots, 2 * tokens), BF),
            pltpu.VMEM((2, tokens, 128), F32),
            pltpu.VMEM((2, tokens, 128), F32),
            pltpu.VMEM((n_ex, width), BF),
            pltpu.VMEM((width, hidden_units), BF),
            pltpu.VMEM((hidden_units, width), BF),
            pltpu.VMEM((2 * tokens, half), BF),
            pltpu.VMEM((chunk_slots, half), BF),
            pltpu.VMEM((chunk_slots, half), BF),
            pltpu.VMEM((2, 4, chunk_slots, half), BF),
            pltpu.VMEM((2, chunk_slots, hidden_units), BF),
            pltpu.VMEM((4, chunk_slots, half), BF),
            pltpu.VMEM((4, chunk_slots, half), BF),
            pltpu.VMEM((4, chunk_slots, half), BF),
            pltpu.VMEM((chunk_slots, half), BF),
            pltpu.VMEM((chunk_slots, half), BF),
            pltpu.VMEM((chunk_slots, half), F32),
            pltpu.VMEM((chunk_slots, half), BF),
            pltpu.VMEM((chunk_slots, half), BF),
            pltpu.VMEM((2 * tokens, half), BF),
            pltpu.VMEM((2 * tokens, half), BF),
            pltpu.VMEM((tokens, half), F32),
            pltpu.VMEM((tokens, half), F32),
            dma((4,)), dma((3,)), dma((3,)), dma((3,)), dma((3,)), dma((5,)), dma((5,)), dma((n_ex,)), dma((n_ex,)),
            dma((n_ex,)), dma((n_ex,)), dma((2, 4)), dma((2, 4)), dma((4, 4)), dma((4, 4)), dma((4,)), dma((4,)),
            dma((2, 4)), dma((2, 4)), dma((n_ex,)), dma((n_ex,)), dma((n_ex,)), dma((n_ex,)),
    ]

    def kernel(*refs):
        layer_kernel(
            n_dp, n_ex, cap, refs[13:17],
            (rows, cache, src, rows // sentences, chunks, refs[0:13], refs[18]), refs[19], refs[17],
        )

    return pl.pallas_call(
        kernel,
        out_shape=jax.ShapeDtypeStruct((steps, rows, width), BF),
        in_specs=[pl.BlockSpec(memory_space=pl.ANY)] * 17,
        out_specs=pl.BlockSpec(memory_space=pltpu.VMEM),
        scratch_shapes=(tuple(attention_scratch), tuple(expert_scratch)),
        compiler_params=pltpu.CompilerParams(
            collective_id=0, has_side_effects=True, vmem_limit_bytes=60 * 2**20
        ),
    )(
        hidden, q_self, k_new, v_new, q_cross, parents, key_scale, value_scale, norm_gain.reshape(1, width),
        cache_keys.reshape(n_self, width), cache_values.reshape(n_self, width),
        cross_keys.reshape(n_cross, width), cross_values.reshape(n_cross, width),
        jnp.swapaxes(expert_ids, 1, 2), router.T,
        w_in.reshape(width, hidden_units), w_out.reshape(hidden_units, width),
    )


def solution(mesh):
    in_specs = (
        P(None, ("dp", "expert"), None),
        P(None, ("dp", "expert"), None),
        P(None, ("dp", "expert"), None),
        P(None, ("dp", "expert"), None),
        P(None, ("dp", "expert"), None),
        P(("dp", "expert"), None, None),
        P(("dp", "expert"), None, None),
        P(("dp", "expert"), None, None),
        P(("dp", "expert"), None, None),
        P(("dp", "expert"), None),
        P(("dp", "expert"), None),
        P(None, ("dp", "expert")),
        P(None, ("dp", "expert"), None),
        P(),
        P(),
        P("expert", None, "dp"),
        P("expert", "dp", None),
    )
    out_specs = P(None, ("dp", "expert"), None)
    return jax.shard_map(layer, mesh=mesh, in_specs=in_specs, out_specs=out_specs, check_vma=False)
```
